32 devices in a mesh: dp: 4 (over y, x), fsdp: 8 (over z, core).
Axes of the slice: x: 2, y: 2, z: 4, core: 2. Of those that a mesh axis runs over, the one named last changes fastest.
Arguments:
- states: float32 [32768, 256], P(('dp', 'fsdp')), may hold values from -6 to 6
- inject: float32 [32768, 256], P(('dp', 'fsdp')), may hold values from -4 to 4
- ln1_gain: bfloat16 [256], P('fsdp'), may hold values from 0.099609375 to 1.8984375
- w_qkv: bfloat16 [256, 768], P('fsdp'), may hold values from -0.375 to 0.375
- w_out: bfloat16 [256, 256], P('fsdp'), may hold values from -1.5 to 1.5
- ln2_gain: bfloat16 [256], P('fsdp'), may hold values from 0.099609375 to 1.8984375
- w_up: bfloat16 [256, 1024], P('fsdp'), may hold values from -0.375 to 0.375
- w_down: bfloat16 [1024, 256], P('fsdp'), may hold values from -0.1875 to 0.1875
- prompt_lengths: int32 [32, 16], P(('dp', 'fsdp')), may hold values from 1 to 101, 1024 in all within a row
- loop_counts: int32 [32, 16], P(('dp', 'fsdp')), may hold values from 12 to 30
- cotangent: float32 [32768, 256], P(('dp', 'fsdp')), may hold values from -6 to 6
Outputs:
- final_states: float32 [32768, 256], P(('dp', 'fsdp'))
- states_grad: float32 [32768, 256], P(('dp', 'fsdp'))
- inject_grad: float32 [32768, 256], P(('dp', 'fsdp'))
- ln1_gain_grad: float32 [256], P('fsdp')
- w_qkv_grad: float32 [256, 768], P('fsdp')
- w_out_grad: float32 [256, 256], P('fsdp')
- ln2_gain_grad: float32 [256], P('fsdp')
- w_up_grad: float32 [256, 1024], P('fsdp')
- w_down_grad: float32 [1024, 256], P('fsdp')
The draws below stay inside these ranges and needn't reach their ends.
Inputs may be any that keep to these rules, and one draw needn't show every extreme that they name: `prompt_lengths`: each row sums to 1024; its longest prompt has exactly 101 tokens.
All inputs are finite; a program needn't handle non-finite values.
Results may differ from the reference program's by a relative error of at most 0.02.
Values may be sent and summed in bfloat16 or wider, within the bound.
No kernel may reach another device: no remote copies, remote signals or barrier semaphores. Data moves between devices by JAX's collectives and lax.ppermute only.
A program may use at most 128 MiB of HBM per device.

```python
import math
import jax
import jax.numpy as jnp
import numpy as np
from jax import lax

D = 256
HEADS = 8
FF = 1024
TOK_DEV = 1024
PROMPTS_DEV = 16
ITERS = 2
TOKENS = 32768
N_DP = 4
N_FSDP = 8
DEVICES = 32


def touch_ends(values, key, low, largest):
    longest = values.shape.index(max(values.shape))
    spots = []
    for shift in (0, 1):
        where = [jax.random.randint(jax.random.fold_in(key, axis), (), 0, length) for axis, length in enumerate(values.shape)]
        where[longest] = (where[longest] + shift) % values.shape[longest]
        spots.append(tuple(where))
    return values.at[spots[0]].set(low).at[spots[1]].set(largest)


def level_of(key, shape, cuts, least, largest):
    factor_of, own = 1.0, jax.random.fold_in(key, 6)
    for dim, parts in cuts:
        heights = jnp.exp(jax.random.uniform(jax.random.fold_in(own, dim), (parts,), jnp.float32, least / len(cuts), largest / len(cuts)))
        factor_of = factor_of * jnp.repeat(heights, shape[dim] // parts).reshape([-1 if axis == dim else 1 for axis in range(len(shape))])
    return factor_of


def profile(number_of, total, reach, skew):
    loads = [(1 << 20) // math.isqrt(rank ** skew) + 1 for rank in range(2, number_of + 1)]
    surplus, given = total - reach - (number_of - 1), [1] * (number_of - 1)
    while surplus > 0:
        free = [i for i in range(number_of - 1) if given[i] < reach]
        pool, left = sum([loads[i] for i in free]), surplus
        for i in free:
            extra = min(reach - given[i], max(1, left * loads[i] // pool), surplus)
            given[i] = given[i] + extra
            surplus = surplus - extra
    return np.array([reach] + given)


def uneven(stream_key, count, total, limit, lean):
    if count == 2:
        one = jax.random.randint(stream_key, (), max(1, total - limit), min(limit, total - 1) + 1)
        return jnp.stack([one, total - one])
    sizes = jnp.asarray(profile(count, total, limit, lean), jnp.int32)
    twos = (count - 1) // 2
    giver, receiver = sizes[1:1 + 2 * twos:2], sizes[2:2 + 2 * twos:2]
    room = jnp.minimum(giver - 1, limit - receiver)
    moved = jax.random.randint(jax.random.fold_in(stream_key, 1), (twos,), 0, 1 << 20) % (room + 1)
    sizes = sizes.at[1:1 + 2 * twos:2].set(giver - moved).at[2:2 + 2 * twos:2].set(receiver + moved)
    return sizes[jax.random.permutation(jax.random.fold_in(stream_key, 2), count)]


def scatter_about(rng, extent, scale, most, split=(), held_as=jnp.bfloat16):
    factor_of = level_of(rng, extent, split, -0.22, 0.18) if split else 1.0
    drawn = jax.random.normal(rng, extent, jnp.float32) * scale * factor_of
    return jnp.minimum(jnp.maximum(drawn, -most), most).astype(held_as)


def setup_inputs(seed: int = 0) -> dict:
    key_of = jax.random.split(jax.random.key(seed), 12)
    states = scatter_about(key_of[0], (TOKENS, D), 1.0, 6.0, ((0, 32),), jnp.float32)
    inject = scatter_about(key_of[1], (TOKENS, D), 0.5, 4.0, ((0, 32),), jnp.float32)
    ln1_gain = jnp.clip(1.0 + 0.18 * jax.random.normal(key_of[2], (D,), jnp.float32), 0.099609375, 1.8984375).astype(jnp.bfloat16)
    w_qkv = scatter_about(key_of[3], (D, 3 * D), D ** -0.5, 0.375, ((0, 8),))
    w_out = scatter_about(key_of[4], (D, D), (D // 16) ** -0.5, 1.5, ((0, 8),))
    ln2_gain = jnp.clip(1.0 + 0.18 * jax.random.normal(key_of[5], (D,), jnp.float32), 0.099609375, 1.8984375).astype(jnp.bfloat16)
    w_up = scatter_about(key_of[6], (D, FF), D ** -0.5, 0.375, ((0, 8),))
    w_down = scatter_about(key_of[7], (FF, D), FF ** -0.5, 0.1875, ((0, 8),))
    prompt_lengths = jax.vmap(lambda own: uneven(own, PROMPTS_DEV, TOK_DEV, min(101, TOK_DEV), 1))(jax.random.split(key_of[8], DEVICES)).reshape((DEVICES, PROMPTS_DEV)).astype(jnp.int32)
    loop_counts = touch_ends(jax.random.randint(key_of[9], (DEVICES, PROMPTS_DEV), 12, 31), jax.random.fold_in(key_of[9], 1), 12, 30).astype(jnp.int32)
    cotangent = scatter_about(key_of[10], (TOKENS, D), 1.0, 6.0, ((0, 32),), jnp.float32)
    return dict(states=states, inject=inject, ln1_gain=ln1_gain, w_qkv=w_qkv, w_out=w_out, ln2_gain=ln2_gain, w_up=w_up, w_down=w_down, prompt_lengths=prompt_lengths, loop_counts=loop_counts, cotangent=cotangent)


@jax.custom_vjp
def low(v):
    return lax.optimization_barrier(v.astype(jnp.bfloat16)).astype(jnp.float32)

@jax.custom_vjp
def low_back(v):
    return v

def low_keep(v):
    return (low(v), None)

def low_pass(kept, grad):
    return (grad,)

def back_keep(v):
    return (v, None)

def back_low(kept, grad):
    return (low(grad),)
low.defvjp(low_keep, low_pass)
low_back.defvjp(back_keep, back_low)

def norm_rows(values, gain_row):
    center = values - lax.optimization_barrier(jnp.mean(values, axis=-1, keepdims=True))
    spread = lax.optimization_barrier(jnp.mean(center * center, axis=-1, keepdims=True))
    return center * lax.rsqrt(spread + 1e-05) * gain_row

def gelu_tanh(values):
    return 0.5 * values * (1.0 + jnp.tanh(0.7978845608028654 * (values + 0.044715 * values * values * values)))

def matmul_high(left, right):
    return jnp.dot(left, right, precision=lax.Precision.HIGHEST, preferred_element_type=jnp.float32)

def attend(packed, segment):
    head_dim = D // HEADS
    query_all = packed[:, :D].reshape(TOK_DEV, HEADS, head_dim)
    key_all = packed[:, D:2 * D].reshape(TOK_DEV, HEADS, head_dim)
    value_all = packed[:, 2 * D:].reshape(TOK_DEV, HEADS, head_dim)
    raw_scores = jnp.einsum('rhd,thd->hrt', query_all, key_all, precision=lax.Precision.HIGHEST) * head_dim ** (-0.5)
    scores = low_back(raw_scores)
    position = jnp.arange(TOK_DEV, dtype=jnp.int32)
    allowed = (segment[:, None] == segment[None, :]) & (position[None, :] <= position[:, None])
    scores = jnp.where(allowed[None], scores, -1e+30)
    row_max = lax.optimization_barrier(jnp.max(scores, axis=-1, keepdims=True))
    shifted = jnp.exp(scores - row_max)
    attn_probs = low(shifted / lax.optimization_barrier(jnp.sum(shifted, axis=-1, keepdims=True)))
    output = jnp.einsum('hrt,thd->rhd', attn_probs, value_all, precision=lax.Precision.HIGHEST)
    return output.reshape(TOK_DEV, D)

def two_loops(state, injected, segment, gain_first, weight_qkv, weight_out, gain_second, weight_up, weight_down):
    for repeat in range(ITERS):
        entered = state + injected
        normed_one = low(norm_rows(entered, gain_first))
        packed = low_back(low(matmul_high(normed_one, weight_qkv)))
        heads_low = low_back(low(jax.checkpoint(attend)(packed, segment)))
        middle = entered + low_back(matmul_high(heads_low, weight_out))
        normed_two = low(norm_rows(middle, gain_second))
        hidden = low_back(matmul_high(normed_two, weight_up))
        active = low(gelu_tanh(hidden))
        state = middle + low_back(matmul_high(active, weight_down))
    return state

def reference(states, inject, ln1_gain, w_qkv, w_out, ln2_gain, w_up, w_down, prompt_lengths, loop_counts, cotangent):
    blocks_count = N_DP * N_FSDP
    prompt_ends = jnp.cumsum(prompt_lengths, axis=1).astype(jnp.int32)
    position = jnp.arange(TOK_DEV, dtype=jnp.int32)
    segment = lax.optimization_barrier(jnp.sum((position[None, :, None] >= prompt_ends[:, None, :]).astype(jnp.int32), axis=2)).astype(jnp.int32)
    rates = 12.0 / loop_counts.astype(jnp.float32)
    row_weight = jnp.take_along_axis(rates, segment, axis=1).reshape(TOKENS, 1)
    params = (ln1_gain.astype(jnp.float32), w_qkv.astype(jnp.float32), w_out.astype(jnp.float32), ln2_gain.astype(jnp.float32), w_up.astype(jnp.float32), w_down.astype(jnp.float32))

    def forward(state_all, inject_all, gain_first, weight_qkv, weight_out, gain_second, weight_up, weight_down):

        def per_block(items):
            return two_loops(items[0], items[1], items[2], gain_first, weight_qkv, weight_out, gain_second, weight_up, weight_down)
        result = lax.map(per_block, (state_all.reshape(blocks_count, TOK_DEV, D), inject_all.reshape(blocks_count, TOK_DEV, D), segment))
        return result.reshape(TOKENS, D)
    final_states, pullback = jax.vjp(forward, states, inject, *params)
    grads = pullback(cotangent * row_weight)
    return (final_states, grads[0], grads[1], grads[2], grads[3], grads[4], grads[5], grads[6], grads[7])
```

```python
import functools
import types

import jax
import jax.numpy as jnp
from jax import lax
from jax.experimental import pallas as pl
from jax.experimental.pallas import tpu as pltpu
from jax.sharding import PartitionSpec as P

BF = jnp.bfloat16
F32 = jnp.float32
HEADS = 8
ITERS = 2
BLK = 128
CHUNK = 256
NEG = -1e30
LOG2E = 1.4426950408889634
LN2 = 0.6931471805599453
GELU_A = 0.7978845608028654
GELU_B = GELU_A * 0.044715


def dot(a, b):
    return jnp.dot(a, b, preferred_element_type=F32)

def dot_tn(a, b):
    return lax.dot_general(a, b, (((0,), (0,)), ((), ())), preferred_element_type=F32)

def dot_nt(a, b):
    return lax.dot_general(a, b, (((1,), (1,)), ((), ())), preferred_element_type=F32)

def rows(start, size):
    return pl.ds(pl.multiple_of(start, size), size)

def ln_fwd(x):
    c = x - jnp.mean(x, axis=1, keepdims=True)
    r = lax.rsqrt(jnp.mean(c * c, axis=1, keepdims=True) + 1e-5)
    return c * r, r

def ln_bwd(y, n, r):
    return r * (y - jnp.mean(y, axis=1, keepdims=True) - n * jnp.mean(y * n, axis=1, keepdims=True))

def make_masks(len_ref, mask_ref, nb):
    pos = lax.broadcasted_iota(jnp.int32, (1, BLK), 1)
    ends = []
    total = jnp.int32(0)
    for p in range(len_ref.shape[1]):
        total = total + len_ref[0, p]
        ends.append(total)

    def block(i, _):
        q = pos + i * BLK
        start = jnp.zeros((1, BLK), jnp.int32)
        for e in ends:
            start = jnp.where(q >= e, e, start)
        k = lax.broadcasted_iota(jnp.int32, (2 * BLK, BLK), 0) + (i - 1) * BLK
        mask_ref[i] = jnp.where((k >= start) & (k <= q), 0.0, NEG).astype(F32)
        return 0

    lax.fori_loop(0, nb, block, 0)

def pad_zero(s):
    s.kp[0:BLK, :] = jnp.zeros((BLK, s.kp.shape[1]), BF)
    s.vp[0:BLK, :] = jnp.zeros((BLK, s.vp.shape[1]), BF)
    s.kt[0] = jnp.zeros(s.kt.shape[1:], BF)
    s.vt[0] = jnp.zeros(s.vt.shape[1:], BF)

def project(s, j, ent, wqkv):
    d = ent.shape[1]
    n, r = ln_fwd(ent)
    nb16 = n.astype(BF)
    s.n1[rows(j * CHUNK, CHUNK), :] = nb16
    s.r1[rows(j * CHUNK, CHUNK), :] = jnp.broadcast_to(r, (CHUNK, 128))
    scale = LOG2E * (d // HEADS) ** -0.5
    q = (dot(nb16, wqkv[:, 0:d]) * scale).astype(BF)
    k = dot(nb16, wqkv[:, d:2 * d]).astype(BF)
    v = dot(nb16, wqkv[:, 2 * d:3 * d]).astype(BF)
    s.qs[rows(j * CHUNK, CHUNK), :] = q
    s.kp[pl.ds(pl.multiple_of(j * CHUNK + BLK, BLK), CHUNK), :] = k
    s.vp[pl.ds(pl.multiple_of(j * CHUNK + BLK, BLK), CHUNK), :] = v
    qt, kt, vt = q.T, k.T, v.T
    for b in range(CHUNK // BLK):
        i = j * (CHUNK // BLK) + b
        s.qst[i] = qt[:, b * BLK:(b + 1) * BLK]
        s.kt[i + 1] = kt[:, b * BLK:(b + 1) * BLK]
        s.vt[i + 1] = vt[:, b * BLK:(b + 1) * BLK]

def split_heads(tile, a, hd):
    z = jnp.zeros_like(tile)
    row = lax.broadcasted_iota(jnp.int32, tile.shape, 0)
    left = jnp.where((row >= a) & (row < a + hd), tile, z)
    right = jnp.where((row >= a + hd) & (row < a + 2 * hd), tile, z)
    return jnp.concatenate([left, right], axis=1)

def stack_heads(tile, a, hd):
    z = jnp.zeros_like(tile)
    lane = lax.broadcasted_iota(jnp.int32, tile.shape, 1)
    top = jnp.where((lane >= a) & (lane < a + hd), tile, z)
    low = jnp.where((lane >= a + hd) & (lane < a + 2 * hd), tile, z)
    return jnp.concatenate([top, low], axis=0)

def attend(s, i, mask_ref):
    d = s.qs.shape[1]
    hd = d // HEADS
    mask = mask_ref[i]
    mask2 = jnp.concatenate([mask, mask], axis=1)
    ones = jnp.ones((16, 2 * BLK), BF)
    for t in range(d // 128):
        kw = s.kp[pl.ds(pl.multiple_of(i * BLK, BLK), 2 * BLK), t * 128:(t + 1) * 128]
        qt = s.qst[i, t * 128:(t + 1) * 128, :]
        for pp in range(128 // (2 * hd)):
            pair = t * (128 // (2 * hd)) + pp
            lo = pair * 2 * hd
            sc = dot(kw, split_heads(qt, pp * 2 * hd, hd)) + mask2
            m = jnp.max(sc, axis=0, keepdims=True)
            e = jnp.exp2(sc - m).astype(BF)
            s.e[i, pair] = e
            vt = jnp.concatenate([s.vt[i, lo:lo + 2 * hd, :], s.vt[i + 1, lo:lo + 2 * hd, :]], axis=1)
            o = dot(jnp.concatenate([vt, ones], axis=0), e)
            inv = 1.0 / o[2 * hd:2 * hd + 1, :]
            s.linv[i, 2 * pair:2 * pair + 1, :] = inv[:, :BLK]
            s.linv[i, 2 * pair + 1:2 * pair + 2, :] = inv[:, BLK:]
            s.ht[i, lo:lo + hd, :] = (o[0:hd, :BLK] * inv[:, :BLK]).astype(BF)
            s.ht[i, lo + hd:lo + 2 * hd, :] = (o[hd:2 * hd, BLK:] * inv[:, BLK:]).astype(BF)

def heads_chunk(s, j):
    return jnp.concatenate([s.ht[j * (CHUNK // BLK) + b] for b in range(CHUNK // BLK)], axis=1)

def mlp(s, j, ent, wout, wup, wdown):
    mid = ent + dot_tn(heads_chunk(s, j), wout[...])
    n, r = ln_fwd(mid)
    nb16 = n.astype(BF)
    at = rows(j * CHUNK, CHUNK)
    s.n2[at, :] = nb16
    s.r2[at, :] = jnp.broadcast_to(r, (CHUNK, 128))
    acc = mid
    for f in range(wup.shape[1] // 256):
        c = slice(f * 256, (f + 1) * 256)
        h = dot(nb16, wup[:, c])
        h2 = h * h
        th = jnp.tanh(h * (GELU_B * h2 + GELU_A))
        sg = 0.5 * th + 0.5
        a = h * sg
        act = a.astype(BF)
        s.act[at, c] = act
        s.gp[at, c] = (sg + a * (1.0 - th) * (3 * GELU_B * h2 + GELU_A)).astype(BF)
        acc = acc + dot(act, wdown[c, :])
    return acc

def mlp_back(s, j, g, wdown_t, wup_t):
    at = rows(j * CHUNK, CHUNK)
    gb = g.astype(BF)
    s.g2[at, :] = gb
    acc = None
    for f in range(wdown_t.shape[1] // 256):
        c = slice(f * 256, (f + 1) * 256)
        dh = (dot(gb, wdown_t[:, c]) * s.gp[at, c].astype(F32)).astype(BF)
        s.dh[at, c] = dh
        part = dot(dh, wup_t[c, :])
        acc = part if acc is None else acc + part
    g = g + ln_bwd(acc, s.n2[at, :].astype(F32), s.r2[at, 0:1])
    s.gm[at, :] = g.astype(BF)
    return g

def attend_back(s, i, wout, dk_ref, dv_ref):
    d = s.qs.shape[1]
    hd = d // HEADS
    at = rows(i * BLK, BLK)
    win = pl.ds(pl.multiple_of(i * BLK, BLK), 2 * BLK)
    dot_ = dot_nt(wout[...], s.gm[at, :])
    li = jnp.concatenate([jnp.broadcast_to(s.linv[i, h:h + 1, :], (hd, BLK)) for h in range(HEADS)], axis=0)
    dost = (dot_ * li).astype(BF)
    doh = (dost.astype(F32) * s.ht[i].astype(F32)).astype(BF)
    dos = dost.T
    minus = jnp.full((2 * BLK, 128), -1.0, BF)
    dqs = []
    for t in range(d // 128):
        tl = slice(t * 128, (t + 1) * 128)
        av = jnp.concatenate([s.vp[win, tl], minus], axis=1)
        qtok = s.qs[at, tl]
        dk = dv = None
        for pp in range(128 // (2 * hd)):
            pair = t * (128 // (2 * hd)) + pp
            lo = pair * 2 * hd
            a = pp * 2 * hd
            bd = jnp.concatenate([split_heads(dost[tl, :], a, hd), split_heads(doh[tl, :], a, hd)], axis=0)
            dp = dot(av, bd)
            e = s.e[i, pair]
            ds = (e.astype(F32) * dp).astype(BF)
            pv = dot(e, stack_heads(dos[:, tl], a, hd))
            pk = dot(ds, stack_heads(qtok, a, hd))
            dv = pv if dv is None else dv + pv
            dk = pk if dk is None else dk + pk
            kt = jnp.concatenate([s.kt[i, lo:lo + 2 * hd, :], s.kt[i + 1, lo:lo + 2 * hd, :]], axis=1)
            dq = dot(kt, ds)
            dqs.append(dq[0:hd, :BLK])
            dqs.append(dq[hd:2 * hd, BLK:])
        top, low = pl.ds(pl.multiple_of(i * BLK, BLK), BLK), pl.ds(pl.multiple_of(i * BLK + BLK, BLK), BLK)
        dk_ref[top, tl] += dk[:BLK]
        dv_ref[top, tl] += dv[:BLK]
        dk_ref[low, tl] = dk[BLK:]
        dv_ref[low, tl] = dv[BLK:]
    dq = jnp.concatenate(dqs, axis=0) * hd ** -0.5
    s.dpk[at, 0:d] = dq.astype(BF).T

def project_back(s, j, g, wqkv_t, dk_ref, dv_ref):
    d = g.shape[1]
    at = rows(j * CHUNK, CHUNK)
    pat = pl.ds(pl.multiple_of(j * CHUNK + BLK, BLK), CHUNK)
    dk = (dk_ref[pat, :] * LN2).astype(BF)
    dv = dv_ref[pat, :].astype(BF)
    s.dpk[at, d:2 * d] = dk
    s.dpk[at, 2 * d:3 * d] = dv
    y = dot(s.dpk[at, 0:d], wqkv_t[0:d, :]) + dot(dk, wqkv_t[d:2 * d, :]) + dot(dv, wqkv_t[2 * d:, :])
    return g + ln_bwd(y, s.n1[at, :].astype(F32), s.r1[at, 0:1])

def saved_shapes(t, d, ff):
    nb = t // BLK
    return dict(n1=((t, d), BF), r1=((t, 128), F32), qs=((t, d), BF), kp=((t + BLK, d), BF), vp=((t + BLK, d), BF),
                qst=((nb, d, BLK), BF), kt=((nb + 1, d, BLK), BF), vt=((nb + 1, d, BLK), BF), e=((nb, HEADS // 2, 2 * BLK, 2 * BLK), BF),
                ht=((nb, d, BLK), BF), linv=((nb, HEADS, BLK), F32))
def more_shapes(t, d, ff):
    return dict(n2=((t, d), BF), r2=((t, 128), F32), act=((t, ff), BF), gp=((t, ff), BF),
                g2=((t, d), BF), gm=((t, d), BF), dh=((t, ff), BF), dpk=((t, 3 * d), BF))

def loop(n, body):
    lax.fori_loop(0, n, lambda i, _: (body(i), 0)[1], 0)

def all_kernel(names, parts, me_ref, len_ref, cnt_ref, *refs):
    states, inject, cot = refs[:3]
    qkv_parts, rest_parts = refs[3:3 + parts], refs[3 + parts:3 + 2 * parts]
    refs = refs[3 + 2 * parts:]
    out, gout, ginj, keep, send = refs[:5]
    sc = dict(zip(names, refs[5:]))
    wqkv, wout, wup, wdown, mqkv, mout, mup, mdown_t, mdown = [sc[k] for k in ("wqkv", "wout", "wup", "wdown", "mqkv", "mout", "mup", "mdown_t", "mdown")]
    me = me_ref[0]
    place_qkv(me, qkv_parts, wqkv)
    place_rest(me, rest_parts, wout, wup, wdown)
    its = [types.SimpleNamespace(**{k[:-1]: v for k, v in sc.items() if k[-1] == str(i)}) for i in range(2)]
    mask, state, dkr, dvr, wqkv_t, wup_t, wdown_t, wout_t = [sc[k] for k in ("mask", "state", "dk", "dv", "wqkv_t", "wup_t", "wdown_t", "tr")]
    t, d = states.shape
    nb, nc = t // BLK, t // CHUNK
    make_masks(len_ref, mask, nb)
    wqkv_t[...] = wqkv[...].T
    wup_t[...] = wup[...].T
    wdown_t[...] = wdown[...].T
    for it, s in enumerate(its):
        src, dst = (states, state) if it == 0 else (state, out)
        pad_zero(s)
        loop(nc, lambda j: project(s, j, src[rows(j * CHUNK, CHUNK), :] + inject[rows(j * CHUNK, CHUNK), :], wqkv))
        loop(nb, lambda i: attend(s, i, mask))
        def m(j):
            at = rows(j * CHUNK, CHUNK)
            dst[at, :] = mlp(s, j, src[at, :] + inject[at, :], wout, wup, wdown)
        loop(nc, m)
    ends = []
    total = jnp.int32(0)
    for p in range(len_ref.shape[1]):
        ends.append(total)
        total = total + len_ref[0, p]
    def wgt(j):
        at = rows(j * CHUNK, CHUNK)
        pos = lax.broadcasted_iota(jnp.int32, (CHUNK, 128), 0) + j * CHUNK
        w = jnp.zeros((CHUNK, 128), F32)
        for p, e in enumerate(ends):
            w = jnp.where(pos >= e, 12.0 / cnt_ref[0, p].astype(F32), w)
        gout[at, :] = cot[at, :] * jnp.concatenate([w] * (d // 128), axis=1)
    loop(nc, wgt)
    for it in (1, 0):
        s = its[it]
        def mb(j):
            at = rows(j * CHUNK, CHUNK)
            gout[at, :] = mlp_back(s, j, gout[at, :], wdown_t, wup_t)
        loop(nc, mb)
        dkr[0:BLK, :] = jnp.zeros((BLK, d), F32)
        dvr[0:BLK, :] = jnp.zeros((BLK, d), F32)
        loop(nb, lambda i: attend_back(s, i, wout, dkr, dvr))
        def pb(j):
            at = rows(j * CHUNK, CHUNK)
            g = project_back(s, j, gout[at, :], wqkv_t, dkr, dvr)
            gout[at, :] = g
            ginj[at, :] = g if it == 1 else ginj[at, :] + g
        loop(nc, pb)
    def wg(lhs, rhs, dst, transpose):
        for it in range(2):
            if transpose: wout_t[it] = lhs[it][...].T
        def tile(c):
            cc = pl.ds(pl.multiple_of(c * 256, 256), 256)
            dst[:, cc] = (dot(wout_t[0], rhs[0][:, cc]) + dot(wout_t[1], rhs[1][:, cc])).astype(BF)
        loop(dst.shape[1] // 256, tile)
    wg([s.g2 for s in its], [s.act for s in its], mdown_t, True)
    wg([s.n2 for s in its], [s.dh for s in its], mup, True)
    wg([s.n1 for s in its], [s.dpk for s in its], mqkv, True)
    for it in range(2):
        for b in range(nb):
            wout_t[it, :, b * BLK:(b + 1) * BLK] = its[it].ht[b]
    wg(None, [s.gm for s in its], mout, False)
    mdown[...] = mdown_t[...].T
    for x in range(parts):
        dst = send if x % 2 else keep
        owner = me ^ x
        r, k = d // parts, x // 2
        lo = 0
        for m in (mqkv, mout, mup):
            for c in range(m.shape[1] // 256):
                dst[k, lo:lo + r, :] = m[rows(owner * r, r), c * 256:(c + 1) * 256]
                lo += r
        r = mdown.shape[0] // parts
        dst[k, lo:lo + r, :] = mdown[rows(owner * r, r), :]

def place_qkv(me, parts, wqkv):
    r = wqkv.shape[0] // len(parts)
    for x, p in enumerate(parts):
        wqkv[rows((me ^ x) * r, r), :] = p[...]

def place_rest(me, parts, wout, wup, wdown):
    r, rd = wout.shape[0] // len(parts), wdown.shape[0] // len(parts)
    for x, p in enumerate(parts):
        at = rows((me ^ x) * r, r)
        wout[at, :] = p[0:r, :]
        for c in range(wup.shape[1] // 256):
            wup[at, c * 256:(c + 1) * 256] = p[(c + 1) * r:(c + 2) * r, :]
        lo = r * (1 + wup.shape[1] // 256)
        wdown[rows((me ^ x) * rd, rd), :] = p[lo:lo + rd, :]

def compute_all(me, states, inject, qkv_parts, rest_parts, lengths, counts, cot, ff):
    t, d = states.shape
    nb = t // BLK
    parts = len(qkv_parts)
    sh = {}
    for i in range(2):
        for k, v in {**saved_shapes(t, d, ff), **more_shapes(t, d, ff)}.items(): sh[k + str(i)] = v
    sh.update(mask=((nb, 2 * BLK, BLK), F32), state=((t, d), F32), dk=((t + BLK, d), F32), dv=((t + BLK, d), F32),
              wqkv_t=((3 * d, d), BF), wup_t=((ff, d), BF), wdown_t=((d, ff), BF), tr=((2, d, t), BF),
              wqkv=((d, 3 * d), BF), wout=((d, d), BF), wup=((d, ff), BF), wdown=((ff, d), BF),
              mqkv=((d, 3 * d), BF), mout=((d, d), BF), mup=((d, ff), BF), mdown_t=((d, ff), BF), mdown=((ff, d), BF))
    S = jax.ShapeDtypeStruct
    vm = pl.BlockSpec(memory_space=pltpu.VMEM)
    sm = pl.BlockSpec(memory_space=pltpu.SMEM)
    piece = (4 * d + 2 * ff) // parts
    half = S((max(parts // 2, 1), piece, d), BF)
    outs = (S((t, d), F32),) * 3 + (half, half)
    return pl.pallas_call(
        functools.partial(all_kernel, list(sh), parts), out_shape=outs, in_specs=[sm, sm, sm] + [vm] * (3 + 2 * parts), out_specs=(vm,) * 5,
        scratch_shapes=[pltpu.VMEM(*v) for v in sh.values()],
        compiler_params=pltpu.CompilerParams(vmem_limit_bytes=63 << 20), name="compute")(
        me, lengths, counts, states, inject, cot, *qkv_parts, *rest_parts)


def exchange(x, axis, size, step):
    return lax.ppermute(x, axis, [(i, i ^ step) for i in range(size)])

def gather_parts(x, size):
    far = [x] + [exchange(x, "fsdp", size, 2 * k) for k in range(1, size // 2)]
    near = [exchange(v, "fsdp", size, 1) for v in far]
    return [v for pair in zip(far, near) for v in pair]

def add_parts(first, others):
    total = first.astype(F32)
    for v in others:
        total = total + v.astype(F32)
    return total

def reduce_parts(keep, send, n_fsdp, n_dp):
    near = exchange(send, "fsdp", n_fsdp, 1)
    summed = [add_parts(keep[k], [near[k]]) for k in range(n_fsdp // 2)]
    far = [exchange(summed[k].astype(BF), "fsdp", n_fsdp, 2 * k) for k in range(1, n_fsdp // 2)]
    share = add_parts(summed[0], far).astype(BF)
    return add_parts(share, [exchange(share, "dp", n_dp, k) for k in range(1, n_dp)])

def on_device(n_dp, n_fsdp, states, inject, ln1_gain, w_qkv, w_out, ln2_gain, w_up, w_down, prompt_lengths, loop_counts, cotangent):
    d = states.shape[1]
    r, ff = w_up.shape
    wide = lambda v: [v[:, c:c + d] for c in range(0, v.shape[1], d)]
    gain_one, gain_two = ln1_gain.astype(F32)[:, None], ln2_gain.astype(F32)[:, None]
    qkv = (w_qkv.astype(F32) * gain_one).astype(BF)
    up = (w_up.astype(F32) * gain_two).astype(BF)
    rest = jnp.concatenate([w_out] + wide(up) + [w_down], axis=0)
    direct = r % 16 == 0
    if direct:
        me = lax.axis_index("fsdp").astype(jnp.int32).reshape(1)
        qkv_parts, rest_parts = gather_parts(qkv, n_fsdp), gather_parts(rest, n_fsdp)
    else:
        me = jnp.zeros((1,), jnp.int32)
        full = lambda v: lax.all_gather(v, "fsdp", axis=0, tiled=True)
        qkv_parts = [full(qkv)]
        rest_parts = [jnp.concatenate([full(w_out)] + wide(full(up)) + [full(w_down)], axis=0)]
    final, grad_states, grad_inject, keep, send = compute_all(
        me, states, inject, qkv_parts, rest_parts, prompt_lengths, loop_counts, cotangent, ff)
    if direct:
        total = reduce_parts(keep, send, n_fsdp, n_dp)
    else:
        whole = keep[0].astype(F32)
        share = lambda v: lax.psum(lax.psum_scatter(v.astype(BF), "fsdp", scatter_dimension=0, tiled=True), "dp").astype(F32)
        pieces = [share(whole[c * d:(c + 1) * d]) for c in range(4 + ff // d)] + [share(whole[4 * d + ff:])]
        total = jnp.concatenate(pieces, axis=0)
    join = lambda lo, n: jnp.concatenate([total[lo + c * r:lo + (c + 1) * r] for c in range(n)], axis=1)
    m_qkv, m_out, m_up = join(0, 3), join(3 * r, 1), join(4 * r, ff // d)
    m_down = total[(4 + ff // d) * r:]
    return (final, grad_states, grad_inject,
            jnp.sum(m_qkv * w_qkv.astype(F32), axis=1), m_qkv * gain_one, m_out,
            jnp.sum(m_up * w_up.astype(F32), axis=1), m_up * gain_two, m_down)

def solution(mesh):
    tok, vec, mat = P(("dp", "fsdp"), None), P("fsdp"), P("fsdp", None)
    return jax.shard_map(
        functools.partial(on_device, mesh.shape["dp"], mesh.shape["fsdp"]), mesh=mesh,
        in_specs=(tok, tok, vec, mat, mat, vec, mat, mat, tok, tok, tok),
        out_specs=(tok, tok, tok, vec, mat, mat, vec, mat, mat), check_vma=False)
```

```python
import functools
import types

import jax
import jax.numpy as jnp
from jax import lax
from jax.experimental import pallas as pl
from jax.experimental.pallas import tpu as pltpu
from jax.sharding import PartitionSpec as P

BF = jnp.bfloat16
F32 = jnp.float32
HEADS = 8
ITERS = 2
BLK = 128
CHUNK = 512
NEG = -1e30
LOG2E = 1.4426950408889634
LN2 = 0.6931471805599453
GELU_A = 0.7978845608028654
GELU_B = GELU_A * 0.044715
FLOPS_FIRST = 10 ** 9
FLOPS_LAST = 10 ** 10


def dot(a, b):
    return jnp.dot(a, b, preferred_element_type=F32)

def dot_tn(a, b):
    return lax.dot_general(a, b, (((0,), (0,)), ((), ())), preferred_element_type=F32)

def dot_nt(a, b):
    return lax.dot_general(a, b, (((1,), (1,)), ((), ())), preferred_element_type=F32)

def rows(start, size):
    return pl.ds(pl.multiple_of(start, size), size)

def ln_fwd(x):
    c = x - jnp.mean(x, axis=1, keepdims=True)
    r = lax.rsqrt(jnp.mean(c * c, axis=1, keepdims=True) + 1e-5)
    return c * r, r

def ln_bwd(y, n, r):
    return r * (y - jnp.mean(y, axis=1, keepdims=True) - n * jnp.mean(y * n, axis=1, keepdims=True))

def loop(n, body):
    lax.fori_loop(0, n, lambda i, _: (body(i), 0)[1], 0)

def make_masks(len_ref, mask_ref, nb):
    pos = lax.broadcasted_iota(jnp.int32, (1, BLK), 1)
    ends = []
    total = jnp.int32(0)
    for p in range(len_ref.shape[1]):
        total = total + len_ref[0, p]
        ends.append(total)

    def block(i, _):
        q = pos + i * BLK
        start = jnp.zeros((1, BLK), jnp.int32)
        for e in ends:
            start = jnp.where(q >= e, e, start)
        k = lax.broadcasted_iota(jnp.int32, (2 * BLK, BLK), 0) + (i - 1) * BLK
        mask_ref[i] = jnp.where((k >= start) & (k <= q), 0.0, NEG).astype(F32)
        return 0

    lax.fori_loop(0, nb, block, 0)

def pad_zero(s):
    s.kp[0:BLK, :] = jnp.zeros((BLK, s.kp.shape[1]), BF)
    s.vp[0:BLK, :] = jnp.zeros((BLK, s.vp.shape[1]), BF)
    s.kt[0] = jnp.zeros(s.kt.shape[1:], BF)
    s.vt[0] = jnp.zeros(s.vt.shape[1:], BF)

def project(s, j, ent, wqkv):
    d = ent.shape[1]
    n, r = ln_fwd(ent)
    nb16 = n.astype(BF)
    s.n1[rows(j * CHUNK, CHUNK), :] = nb16
    s.r1[rows(j * CHUNK, CHUNK), :] = jnp.broadcast_to(r, (CHUNK, 128))
    scale = LOG2E * (d // HEADS) ** -0.5
    q = (dot(nb16, wqkv[:, 0:d]) * scale).astype(BF)
    k = dot(nb16, wqkv[:, d:2 * d]).astype(BF)
    v = dot(nb16, wqkv[:, 2 * d:3 * d]).astype(BF)
    s.qs[rows(j * CHUNK, CHUNK), :] = q
    s.kp[pl.ds(pl.multiple_of(j * CHUNK + BLK, BLK), CHUNK), :] = k
    s.vp[pl.ds(pl.multiple_of(j * CHUNK + BLK, BLK), CHUNK), :] = v
    qt, kt, vt = q.T, k.T, v.T
    for b in range(CHUNK // BLK):
        i = j * (CHUNK // BLK) + b
        s.qst[i] = qt[:, b * BLK:(b + 1) * BLK]
        s.kt[i + 1] = kt[:, b * BLK:(b + 1) * BLK]
        s.vt[i + 1] = vt[:, b * BLK:(b + 1) * BLK]

def split_heads(tile, a, hd):
    def alone(lo):
        parts = [jnp.zeros((n, tile.shape[1]), tile.dtype) for n in (lo, tile.shape[0] - lo - hd)]
        parts = [parts[0], tile[lo:lo + hd], parts[1]]
        return jnp.concatenate([p for p in parts if p.shape[0]], axis=0)
    return jnp.concatenate([alone(a), alone(a + hd)], axis=1)

def stack_heads(tile, a, hd):
    z = jnp.zeros_like(tile)
    lane = lax.broadcasted_iota(jnp.int32, tile.shape, 1)
    top = jnp.where((lane >= a) & (lane < a + hd), tile, z)
    low = jnp.where((lane >= a + hd) & (lane < a + 2 * hd), tile, z)
    return jnp.concatenate([top, low], axis=0)

def pairs_of(d):
    hd = d // HEADS
    per = 128 // (2 * hd)
    return [(p, slice(p // per * 128, p // per * 128 + 128), p % per * 2 * hd, p * 2 * hd) for p in range(HEADS // 2)]

def window(ref, i, lo, n):
    return jnp.concatenate([ref[i, lo:lo + n, :], ref[i + 1, lo:lo + n, :]], axis=1)

def attend(s, blocks, mask_ref):
    d = s.qs.shape[1]
    hd = d // HEADS
    ones = jnp.ones((16, 2 * BLK), BF)
    def scores(i):
        win = pl.ds(pl.multiple_of(i * BLK, BLK), 2 * BLK)
        return [dot(s.kp[win, tile], split_heads(s.qst[i, tile, :], a, hd)) for _, tile, a, _ in pairs_of(d)]
    def soft(i, all_scores):
        mask = mask_ref[i]
        mask = jnp.concatenate([mask, mask], axis=1)
        out = []
        for sc in all_scores:
            sc = sc + mask
            out.append(jnp.exp2(sc - jnp.max(sc, axis=0, keepdims=True)).astype(BF))
        return out
    def values(i, es):
        return [dot(jnp.concatenate([window(s.vt, i, lo, 2 * hd), ones], axis=0), es[p]) for p, _, _, lo in pairs_of(d)]
    es = []
    ready = scores(blocks[0])
    for n, i in enumerate(blocks):
        ahead = scores(blocks[n + 1]) if n + 1 < len(blocks) else None
        es.append(soft(i, ready))
        ready = ahead
    os = [values(i, e) for i, e in zip(blocks, es)]
    for i, e, o in zip(blocks, es, os):
        for p, _, _, lo in pairs_of(d):
            s.e[i, p] = e[p]
            inv = 1.0 / o[p][2 * hd:2 * hd + 1, :]
            s.linv[i, 2 * p:2 * p + 1, :] = inv[:, :BLK]
            s.linv[i, 2 * p + 1:2 * p + 2, :] = inv[:, BLK:]
            s.ht[i, lo:lo + hd, :] = (o[p][0:hd, :BLK] * inv[:, :BLK]).astype(BF)
            s.ht[i, lo + hd:lo + 2 * hd, :] = (o[p][hd:2 * hd, BLK:] * inv[:, BLK:]).astype(BF)

def heads_chunk(s, j):
    return jnp.concatenate([s.ht[j * (CHUNK // BLK) + b] for b in range(CHUNK // BLK)], axis=1)

def mlp(s, j, ent, wout, wup, wdown):
    mid = ent + dot_tn(heads_chunk(s, j), wout[...])
    n, r = ln_fwd(mid)
    nb16 = n.astype(BF)
    at = rows(j * CHUNK, CHUNK)
    s.n2[at, :] = nb16
    s.r2[at, :] = jnp.broadcast_to(r, (CHUNK, 128))
    acc = mid
    for f in range(wup.shape[1] // 256):
        c = slice(f * 256, (f + 1) * 256)
        h = dot(nb16, wup[:, c])
        h2 = h * h
        th = jnp.tanh(h * (GELU_B * h2 + GELU_A))
        sg = 0.5 * th + 0.5
        a = h * sg
        act = a.astype(BF)
        s.act[at, c] = act
        s.gp[at, c] = (sg + a * (1.0 - th) * (3 * GELU_B * h2 + GELU_A)).astype(BF)
        acc = acc + dot(act, wdown[c, :])
    return acc

def mlp_back(s, j, g, wdown_t, wup_t):
    at = rows(j * CHUNK, CHUNK)
    gb = g.astype(BF)
    s.g2[at, :] = gb
    acc = None
    for f in range(wdown_t.shape[1] // 256):
        c = slice(f * 256, (f + 1) * 256)
        dh = (dot(gb, wdown_t[:, c]) * s.gp[at, c].astype(F32)).astype(BF)
        s.dh[at, c] = dh
        part = dot(dh, wup_t[c, :])
        acc = part if acc is None else acc + part
    g = g + ln_bwd(acc, s.n2[at, :].astype(F32), s.r2[at, 0:1])
    s.gm[at, :] = g.astype(BF)
    return g

def attend_back(s, blocks, wout, dk_ref, dv_ref):
    d = s.qs.shape[1]
    hd = d // HEADS
    minus = jnp.full((2 * BLK, 128), -1.0, BF)
    def head_grads(i):
        raw = dot_nt(wout[...], s.gm[rows(i * BLK, BLK), :])
        inv = jnp.concatenate([jnp.broadcast_to(s.linv[i, h:h + 1, :], (hd, BLK)) for h in range(HEADS)], axis=0)
        dost = (raw * inv).astype(BF)
        return dost, (dost.astype(F32) * s.ht[i].astype(F32)).astype(BF), dost.T
    def prob_grads(i, dost, doh):
        win = pl.ds(pl.multiple_of(i * BLK, BLK), 2 * BLK)
        return [dot(jnp.concatenate([s.vp[win, tile], minus], axis=1),
                    jnp.concatenate([split_heads(dost[tile, :], a, hd), split_heads(doh[tile, :], a, hd)], axis=0))
                for _, tile, a, _ in pairs_of(d)]
    def by_keys(lhs, tokens):
        return [dot(lhs[p], stack_heads(tokens[:, tile], a, hd)) for p, tile, a, _ in pairs_of(d)]
    def by_queries(i, dss):
        out = []
        for p, _, _, lo in pairs_of(d):
            dq = dot(window(s.kt, i, lo, 2 * hd), dss[p])
            out += [dq[0:hd, :BLK], dq[hd:2 * hd, BLK:]]
        return (jnp.concatenate(out, axis=0) * hd ** -0.5).astype(BF)
    heads = [head_grads(i) for i in blocks]
    dps = [prob_grads(i, h[0], h[1]) for i, h in zip(blocks, heads)]
    es = [[s.e[i, p] for p in range(HEADS // 2)] for i in blocks]
    dvs = [by_keys(e, h[2]) for e, h in zip(es, heads)]
    dss = [[(x.astype(F32) * y).astype(BF) for x, y in zip(e, dp)] for e, dp in zip(es, dps)]
    dks = [by_keys(ds, s.qs[rows(i * BLK, BLK), :]) for i, ds in zip(blocks, dss)]
    dqs = [by_queries(i, ds) for i, ds in zip(blocks, dss)]
    per = HEADS // 2 // (d // 128)
    for n, i in enumerate(blocks):
        top, low = pl.ds(pl.multiple_of(i * BLK, BLK), BLK), pl.ds(pl.multiple_of(i * BLK + BLK, BLK), BLK)
        for ref, parts in ((dk_ref, dks[n]), (dv_ref, dvs[n])):
            for t in range(d // 128):
                tile = slice(t * 128, (t + 1) * 128)
                total = sum(parts[t * per + 1:(t + 1) * per], parts[t * per])
                ref[top, tile] += total[:BLK]
                ref[low, tile] = total[BLK:]
        s.dpk[rows(i * BLK, BLK), 0:d] = dqs[n].T

def finish_packed(s, j, dk_ref, dv_ref):
    d = s.n1.shape[1]
    at = rows(j * CHUNK, CHUNK)
    pat = pl.ds(pl.multiple_of(j * CHUNK + BLK, BLK), CHUNK)
    s.dpk[at, d:2 * d] = (dk_ref[pat, :] * LN2).astype(BF)
    s.dpk[at, 2 * d:3 * d] = dv_ref[pat, :].astype(BF)

def project_back(s, j, g, wqkv_t):
    at = rows(j * CHUNK, CHUNK)
    return g + ln_bwd(dot(s.dpk[at, :], wqkv_t[...]), s.n1[at, :].astype(F32), s.r1[at, 0:1])

def weigh(cnt_ref, len_ref, j, cot):
    pos = lax.broadcasted_iota(jnp.int32, (CHUNK, 128), 0) + j * CHUNK
    w = jnp.zeros((CHUNK, 128), F32)
    begin = jnp.int32(0)
    for p in range(len_ref.shape[1]):
        w = jnp.where(pos >= begin, 12.0 / cnt_ref[0, p].astype(F32), w)
        begin = begin + len_ref[0, p]
    return cot * jnp.concatenate([w] * (cot.shape[1] // 128), axis=1)

def saved_shapes(t, d, ff):
    nb = t // BLK
    return dict(n1=((t, d), BF), r1=((t, 128), F32), qs=((t, d), BF), kp=((t + BLK, d), BF), vp=((t + BLK, d), BF),
                qst=((nb, d, BLK), BF), kt=((nb + 1, d, BLK), BF), vt=((nb + 1, d, BLK), BF), e=((nb, HEADS // 2, 2 * BLK, 2 * BLK), BF),
                ht=((nb, d, BLK), BF), linv=((nb, HEADS, BLK), F32))
def more_shapes(t, d, ff):
    return dict(n2=((t, d), BF), r2=((t, 128), F32), act=((t, ff), BF), gp=((t, ff), BF),
                g2=((t, d), BF), gm=((t, d), BF), dh=((t, ff), BF), dpk=((t, 3 * d), BF))

class Memory:
    def __init__(self, ins, outs, load_sems, store_sems, hbm_in, hbm_out, parts):
        self.ins, self.outs = ins, outs
        self.load_sems, self.store_sems, self.hbm_in, self.hbm_out, self.parts = load_sems, store_sems, hbm_in, hbm_out, parts
        self.used, self.started = 0, []

    def _load(self, n, c):
        size = self.ins[n].shape[0] // self.parts[n][0]
        where = pl.ds(c * size, size)
        return pltpu.make_async_copy(self.hbm_in[n].at[where], self.ins[n].at[where], self.load_sems.at[self.parts[n][1] + c])

    def start(self, *which):
        for n in which or sorted(self.parts):
            for c in range(self.parts[n][0]):
                self._load(n, c).start()

    def wait(self, *which, part=None):
        for n in which:
            for c in range(self.parts[n][0]) if part is None else (part,):
                self._load(n, c).wait()

    def put(self, n, entry=None):
        src, dst = self.outs[n], self.hbm_out[n]
        if entry is not None:
            src, dst = src.at[entry], dst.at[entry]
        copy = pltpu.make_async_copy(src, dst, self.store_sems.at[self.used])
        copy.start()
        self.started.append(copy)
        self.used += 1

def call(kernel, outs, args, scratch, name, flops, puts=0):
    spec = dict(vmem=pl.BlockSpec(memory_space=pltpu.VMEM), smem=pl.BlockSpec(memory_space=pltpu.SMEM), any=pl.BlockSpec(memory_space=pl.ANY))
    spec["load"] = spec["store"] = spec["any"]
    n_in, n_out, n_scratch = len(args), len(outs), len(scratch)
    parts, total = {}, 0
    for n, a in enumerate(args):
        if a[0] == "load":
            parts[n] = (a[2] if len(a) > 2 else 1, total)
            total += parts[n][0]
    stores = [n for n, o in enumerate(outs) if o[0] == "store"]
    puts = max(puts, len(stores))
    buffers = [pltpu.VMEM(args[n][1].shape, args[n][1].dtype) for n in parts] + [pltpu.VMEM(outs[n][1], outs[n][2]) for n in stores]
    sems = [pltpu.SemaphoreType.DMA((max(total, 1),)), pltpu.SemaphoreType.DMA((max(puts, 1),))]
    def run(*refs):
        ins, results, rest = list(refs[:n_in]), list(refs[n_in:n_in + n_out]), refs[n_in + n_out:]
        s = types.SimpleNamespace(**dict(zip(scratch, rest)))
        rest = rest[n_scratch:]
        hbm_in, hbm_out = dict(enumerate(ins)), dict(enumerate(results))
        for n, r in zip(parts, rest):
            ins[n] = r
        for n, r in zip(stores, rest[len(parts):]):
            results[n] = r
        memory = Memory(ins, results, rest[-2], rest[-1], hbm_in, hbm_out, parts)
        kernel(memory, s)
        for copy in memory.started:
            copy.wait()
    return pl.pallas_call(
        run, out_shape=tuple(jax.ShapeDtypeStruct(o[1], o[2]) for o in outs),
        in_specs=[spec[a[0]] for a in args], out_specs=tuple(spec[o[0]] for o in outs),
        scratch_shapes=[v if hasattr(v, "dtype") else pltpu.VMEM(*v) for v in scratch.values()] + buffers + sems,
        compiler_params=pltpu.CompilerParams(vmem_limit_bytes=62 << 20), name=name,
        cost_estimate=pl.CostEstimate(flops=flops, bytes_accessed=1 << 20, transcendentals=0))(*[a[1] for a in args])

def place_qkv(me, parts, wqkv):
    r = wqkv.shape[0] // len(parts)
    for x, p in enumerate(parts):
        wqkv[rows((me ^ x) * r, r), :] = p[...]

def place_rest(me, parts, wout, wup, wdown):
    r, rd = wout.shape[0] // len(parts), wdown.shape[0] // len(parts)
    for x, p in enumerate(parts):
        at = rows((me ^ x) * r, r)
        wout[at, :] = p[0:r, :]
        for c in range(wup.shape[1] // 256):
            wup[at, c * 256:(c + 1) * 256] = p[(c + 1) * r:(c + 2) * r, :]
        lo = r * (1 + wup.shape[1] // 256)
        wdown[rows((me ^ x) * rd, rd), :] = p[lo:lo + rd, :]

def hand_out(me, parts, mats, keep, send, wide):
    for x in range(parts):
        dst = send if x % 2 else keep
        lo = 0
        for m in mats:
            r = m.shape[0] // parts
            at = rows((me ^ x) * r, r)
            if wide:
                dst[x // 2] = m[at, :]
                continue
            for c in range(m.shape[1] // 256):
                dst[x // 2, lo:lo + r, :] = m[at, c * 256:(c + 1) * 256]
                lo += r

SAVED = ("e", "n1", "r1", "qs", "vp", "kt", "ht", "linv")

def first_attention(me, lengths, states, inject, qkv_parts, ff):
    t, d = states.shape
    nb, nc = t // BLK, t // CHUNK
    shapes = saved_shapes(t, d, ff)
    scratch = dict({k: v for k, v in shapes.items() if k not in SAVED}, mask=((nb, 2 * BLK, BLK), F32))
    def kernel(m, s):
        me_ref, len_ref, st, inj = m.ins[:4]
        m.start(*range(4, len(m.ins)))
        m.start(2, 3)
        vars(s).update(zip(SAVED, m.outs))
        wqkv = m.outs[-1]
        make_masks(len_ref, s.mask, nb)
        pad_zero(s)
        m.wait(*range(4, len(m.ins)))
        place_qkv(me_ref[0], m.ins[4:], wqkv)
        for j in range(nc):
            m.wait(2, 3, part=j)
            project(s, j, st[j * CHUNK:(j + 1) * CHUNK, :] + inj[j * CHUNK:(j + 1) * CHUNK, :], wqkv)
        for name in ("n1", "r1", "qs", "vp", "kt"):
            m.put(SAVED.index(name))
        m.put(len(SAVED))
        for i in range(0, nb, 2):
            attend(s, (i, i + 1), s.mask)
            m.put(SAVED.index("e"), i)
            m.put(SAVED.index("e"), i + 1)
        m.put(SAVED.index("ht"))
        m.put(SAVED.index("linv"))
    outs = [("store",) + shapes[k] for k in SAVED] + [("store", (d, 3 * d), BF)]
    args = [("smem", me), ("smem", lengths), ("load", states, nc), ("load", inject, nc)] + [("load", p) for p in qkv_parts]
    got = call(kernel, outs, args, scratch, "first_attention", FLOPS_FIRST, puts=len(SAVED) + nb)
    return dict(zip(SAVED, got)), got[-1]

def middle_part(me, lengths, counts, states, inject, cot, wqkv, ht, rest_parts, ff):
    t, d = states.shape
    nb, nc = t // BLK, t // CHUNK
    parts = len(rest_parts)
    sh = {"a_" + k: v for k, v in more_shapes(t, d, ff).items() if k != "dpk"}
    sh.update({"b_" + k: v for k, v in {**saved_shapes(t, d, ff), **more_shapes(t, d, ff)}.items()})
    sh.update(mask=((nb, 2 * BLK, BLK), F32), state=((t, d), F32), dk=((t + BLK, d), F32), dv=((t + BLK, d), F32),
              wqkv_t=((3 * d, d), BF), wup_t=((ff, d), BF), wdown_t=((d, ff), BF), tr=((2, d, t), BF),
              wup=((d, ff), BF), wdown=((ff, d), BF), mout=((d, d), BF), mup=((d, ff), BF), mdown_t=((d, ff), BF), mdown=((ff, d), BF))
    def kernel(m, x):
        me_ref, len_ref, cnt_ref, st, inj, ct, wqkv_ref, ht_ref = m.ins[:8]
        final, g, ginj, gm, wout, mqkv, keep, send = m.outs
        m.start(*range(8, len(m.ins)))
        m.start(7, 3, 4, 6, 5)
        its = [types.SimpleNamespace(**{k[2:]: v for k, v in vars(x).items() if k.startswith(p)}) for p in ("a_", "b_")]
        its[0].ht, its[0].gm = ht_ref, gm
        make_masks(len_ref, x.mask, nb)
        m.wait(*range(8, len(m.ins)))
        place_rest(me_ref[0], m.ins[8:], wout, x.wup, x.wdown)
        m.put(4)
        x.wup_t[...] = x.wup[...].T
        x.wdown_t[...] = x.wdown[...].T
        pad_zero(its[1])
        m.wait(3, 4, 6, 7)
        x.wqkv_t[...] = wqkv_ref[...].T
        def forward(s, src, dst):
            def chunk(j):
                at = rows(j * CHUNK, CHUNK)
                dst[at, :] = mlp(s, j, src[at, :] + inj[at, :], wout, x.wup, x.wdown)
            loop(nc, chunk)
        forward(its[0], st, x.state)
        loop(nc, lambda j: project(its[1], j, x.state[rows(j * CHUNK, CHUNK), :] + inj[rows(j * CHUNK, CHUNK), :], wqkv_ref))
        loop(nb // 2, lambda i: attend(its[1], (2 * i, 2 * i + 1), x.mask))
        forward(its[1], x.state, final)
        m.put(0)
        m.wait(5)
        def back_two(j):
            at = rows(j * CHUNK, CHUNK)
            g[at, :] = mlp_back(its[1], j, weigh(cnt_ref, len_ref, j, ct[at, :]), x.wdown_t, x.wup_t)
        loop(nc, back_two)
        x.dk[0:BLK, :] = jnp.zeros((BLK, d), F32)
        x.dv[0:BLK, :] = jnp.zeros((BLK, d), F32)
        loop(nb // 2, lambda i: attend_back(its[1], (2 * i, 2 * i + 1), wout, x.dk, x.dv))
        def back_one(j):
            at = rows(j * CHUNK, CHUNK)
            finish_packed(its[1], j, x.dk, x.dv)
            new = project_back(its[1], j, g[at, :], x.wqkv_t)
            ginj[at, :] = new
            g[at, :] = mlp_back(its[0], j, new, x.wdown_t, x.wup_t)
        loop(nc, back_one)
        for n in (1, 2, 3):
            m.put(n)
        def weight_grad(lefts, rights, dst):
            for n, left in enumerate(lefts):
                x.tr[n] = left[...].T
            def tile(c):
                cc = pl.ds(pl.multiple_of(c * 256, 256), 256)
                total = dot(x.tr[0], rights[0][:, cc])
                for n in range(1, len(rights)):
                    total = total + dot(x.tr[n], rights[n][:, cc])
                dst[:, cc] = total.astype(dst.dtype)
            loop(dst.shape[1] // 256, tile)
        weight_grad([s.g2 for s in its], [s.act for s in its], x.mdown_t)
        x.mdown[...] = x.mdown_t[...].T
        weight_grad([s.n2 for s in its], [s.dh for s in its], x.mup)
        weight_grad([its[1].n1], [its[1].dpk], mqkv)
        m.put(5)
        total = None
        for s in its:
            for b in range(nb):
                part = dot(s.ht[b], s.gm[b * BLK:(b + 1) * BLK, :])
                total = part if total is None else total + part
        x.mout[...] = total.astype(BF)
        hand_out(me_ref[0], parts, (x.mout, x.mup, x.mdown), keep, send, False)
        m.put(7)
        m.put(6)
    piece = ("store", (max(parts // 2, 1), (d + ff) // parts + ff // parts, d), BF)
    outs = [("store", (t, d), F32)] * 3 + [("store", (t, d), BF), ("store", (d, d), BF), ("store", (d, 3 * d), F32)] + [piece] * 2
    args = [("smem", me), ("smem", lengths), ("smem", counts)] + [("load", v) for v in (states, inject, cot, wqkv, ht, *rest_parts)]
    return call(kernel, outs, args, sh, "middle_part", 25 * 10 ** 9)

def last_part(me, saved, gm, wout, wqkv, mqkv, g, ginj, parts, ff, first):
    t, d = gm.shape
    nb, nc = t // BLK, t // CHUNK
    scratch = dict(dk=((t + BLK, d), F32), dv=((t + BLK, d), F32), tr=((d, t), BF), mat=((d, 3 * d), BF), wt=((3 * d, d), BF), dpk=((t, 3 * d), BF))
    def kernel(m, s):
        me_ref, s.gm, wout_ref, w_ref, m_ref, g_ref, gi_ref = m.ins[:7]
        vars(s).update(zip(SAVED, m.ins[7:]))
        keep, send, grad, grad_inject = m.outs
        at = {name: n + 7 for n, name in enumerate(SAVED)}
        head = [1, 2] + [at[k] for k in ("linv", "ht", "vp", "kt", "qs")]
        tail = [at["n1"], 3, 4, at["r1"], 5, 6]
        m.start(*head)
        m.start(at["e"])
        m.start(*tail)
        s.dk[0:BLK, :] = jnp.zeros((BLK, d), F32)
        s.dv[0:BLK, :] = jnp.zeros((BLK, d), F32)
        m.wait(*head)
        for i in range(0, nb, 2):
            m.wait(at["e"], part=i)
            m.wait(at["e"], part=i + 1)
            attend_back(s, (i, i + 1), wout_ref, s.dk, s.dv)
        m.wait(*tail)
        s.tr[...] = s.n1[...].T
        s.wt[...] = w_ref[...].T
        loop(nc, lambda j: finish_packed(s, j, s.dk, s.dv))
        def tile(c):
            cc = pl.ds(pl.multiple_of(c * 256, 256), 256)
            s.mat[:, cc] = (m_ref[:, cc] + dot(s.tr[...], s.dpk[:, cc])).astype(BF)
        loop(3, tile)
        hand_out(me_ref[0], parts, (s.mat,), keep, send, True)
        m.put(1)
        m.put(0)
        def chunk(j):
            at = rows(j * CHUNK, CHUNK)
            new = project_back(s, j, g_ref[at, :], s.wt)
            grad[at, :] = new
            grad_inject[at, :] = new + gi_ref[at, :]
        loop(nc, chunk)
        m.put(2)
        m.put(3)
    outs = [("store", (max(parts // 2, 1), d // parts, 3 * d), BF)] * 2 + [("store", (t, d), F32)] * 2
    args = [("smem", me)] + [("load", v) for v in (gm, wout, wqkv, mqkv, g, ginj)]
    args += [("load", saved[k], nb if k == "e" else 1) for k in SAVED] + [("any", v) for v in first]
    return call(kernel, outs, args, scratch, "last_part", FLOPS_LAST)

def to_column(row):
    n = row.shape[1]
    eye = lax.broadcasted_iota(jnp.int32, (n, n), 0) == lax.broadcasted_iota(jnp.int32, (n, n), 1)
    return jnp.sum(jnp.where(eye, jnp.broadcast_to(row, (n, n)), 0.0), axis=1, keepdims=True)

def to_row(column):
    n = column.shape[0]
    eye = lax.broadcasted_iota(jnp.int32, (n, n), 0) == lax.broadcasted_iota(jnp.int32, (n, n), 1)
    return jnp.sum(jnp.where(eye, jnp.broadcast_to(column, (n, n)), 0.0), axis=0, keepdims=True)

def pack_qkv(w_qkv, gain):
    def kernel(m, s):
        m.start()
        m.wait(0, 1)
        m.outs[0][...] = (m.ins[0][...].astype(F32) * to_column(m.ins[1][...].astype(F32))).astype(BF)
        m.put(0)
    return call(kernel, [("store", w_qkv.shape, BF)], [("load", w_qkv), ("load", gain.reshape(1, -1))], {}, "pack_qkv", 10 ** 6)[0]

def pack_rest(w_out, w_up, w_down, gain):
    r, d = w_out.shape
    n = w_up.shape[1] // d
    def kernel(m, s):
        out, up, down, g = m.ins[:4]
        m.start()
        m.wait(0, 1, 2, 3)
        m.outs[0][0:r, :] = out[...]
        col = to_column(g[...].astype(F32))
        for c in range(n):
            m.outs[0][(c + 1) * r:(c + 2) * r, :] = (up[:, c * d:(c + 1) * d].astype(F32) * col).astype(BF)
        m.outs[0][(n + 1) * r:, :] = down[...]
        m.put(0)
    args = [("load", v) for v in (w_out, w_up, w_down, gain.reshape(1, -1))]
    return call(kernel, [("store", ((n + 1) * r + w_down.shape[0], d), BF)], args, {}, "pack_rest", 10 ** 6)[0]

def sum_parts(parts, lo, size):
    acc = parts[0][lo:lo + size, :].astype(F32)
    for p in parts[1:]:
        acc = acc + p[lo:lo + size, :].astype(F32)
    return acc

def finished(shares, weight, gain, lead, tail):
    r, cols = weight.shape
    d = shares[0].shape[1]
    n = cols // d
    def kernel(m, s):
        m.start()
        m.wait(*range(len(m.ins)))
        w, g, parts = m.ins[0], to_column(m.ins[1][...].astype(F32)), m.ins[2:]
        along = jnp.zeros((r, 1), F32)
        for c in range(n):
            v = sum_parts(parts, lead + c * r, r)
            m.outs[0][:, c * d:(c + 1) * d] = v * g
            along = along + jnp.sum(v * w[:, c * d:(c + 1) * d].astype(F32), axis=1, keepdims=True)
        m.put(0)
        m.outs[1][...] = to_row(along)
        m.put(1)
        m.outs[2][...] = sum_parts(parts, 0, lead)
        m.outs[3][...] = sum_parts(parts, lead + n * r, tail)
        m.put(2)
        m.put(3)
    outs = [("store", (r, cols), F32), ("store", (1, r), F32), ("store", (lead, d), F32), ("store", (tail, d), F32)]
    got = call(kernel, outs, [("load", weight), ("load", gain.reshape(1, -1))] + [("load", v) for v in shares], {}, "finished", 10 ** 6)
    return [got[0], got[1].reshape(r)] + list(got[2:])

def after(values, *others):
    return lax.optimization_barrier((values, others))[0]

def exchange(x, axis, size, step):
    return lax.ppermute(x, axis, [(i, i ^ step) for i in range(size)])

def far_parts(x, size):
    return [x] + [exchange(x, "fsdp", size, 2 * k) for k in range(1, size // 2)]

def with_near(far, size):
    return [v for x in far for v in (x, exchange(x, "fsdp", size, 1))]

def sum_near(keep, near, then):
    total = keep.astype(F32) + near.astype(F32) + then
    return [total[k].astype(BF) for k in range(keep.shape[0])]

def send_far(summed, size):
    return [exchange(summed[k], "fsdp", size, 2 * k) for k in range(1, size // 2)]

def nothing(value):
    return jnp.minimum(jnp.abs(value[(0,) * value.ndim].astype(F32)), 0.0)

def along_dp(share, size):
    return [share] + [exchange(share, "dp", size, k) for k in range(1, size)]

def send_near(pieces, size):
    return [exchange(p, "fsdp", size, 1) for p in pieces[1::2]]

def send_far(summed, size):
    return [exchange(summed[k], "fsdp", size, 2 * k) for k in range(1, size // 2)]

def reduce_whole(whole, sizes):
    out, lo = [], 0
    for n in sizes:
        share = lax.psum_scatter(whole[lo:lo + n], "fsdp", scatter_dimension=0, tiled=True)
        out.append(lax.psum(share, "dp").astype(F32))
        lo += n
    return jnp.concatenate(out, axis=0)

def on_device(n_dp, n_fsdp, states, inject, ln1_gain, w_qkv, w_out, ln2_gain, w_up, w_down, prompt_lengths, loop_counts, cotangent):
    d = states.shape[1]
    r, ff = w_up.shape
    direct = r % 16 == 0
    if direct:
        me = lax.axis_index("fsdp").astype(jnp.int32).reshape(1)
        qkv_far = far_parts(pack_qkv(w_qkv, ln1_gain), n_fsdp)
        rest_far = far_parts(pack_rest(w_out, w_up, w_down, ln2_gain), n_fsdp)
        qkv_parts = with_near(qkv_far, n_fsdp)
    else:
        me = jnp.zeros((1,), jnp.int32)
        full = lambda v: lax.all_gather(v, "fsdp", axis=0, tiled=True)
        up = full((w_up.astype(F32) * ln2_gain.astype(F32)[:, None]).astype(BF))
        qkv_parts = [full((w_qkv.astype(F32) * ln1_gain.astype(F32)[:, None]).astype(BF))]
        rest_parts = [jnp.concatenate([full(w_out)] + [up[:, c:c + d] for c in range(0, ff, d)] + [full(w_down)], axis=0)]
    parts = len(qkv_parts)
    saved, wqkv = first_attention(me, prompt_lengths, states, inject, qkv_parts, ff)
    if direct:
        rest_parts = with_near(after(rest_far, wqkv), n_fsdp)
    final, g, ginj, gm, wout, mqkv, keep, send = middle_part(
        me, prompt_lengths, loop_counts, states, inject, cotangent, wqkv, saved["ht"], rest_parts, ff)
    summed = []
    if direct:
        summed = sum_near(keep, exchange(send, "fsdp", n_fsdp, 1), 0.0)
        far = send_far(summed, n_fsdp)
    else:
        shares = [reduce_whole(keep[0], [d] * (1 + ff // d) + [ff])]
    keep_qkv, send_qkv, grad_states, grad_inject = last_part(me, saved, gm, wout, wqkv, mqkv, g, ginj, parts, ff, summed)
    if direct:
        near = exchange(send_qkv, "fsdp", n_fsdp, 1)
        share = (sum_parts([summed[0], *far], 0, summed[0].shape[0]) + nothing(keep_qkv)).astype(BF)
        shares = along_dp(share, n_dp)
        summed = sum_near(keep_qkv, near, nothing(share))
        shares_qkv = along_dp(sum_parts([summed[0], *send_far(summed, n_fsdp)], 0, r).astype(BF), n_dp)
    else:
        shares_qkv = [reduce_whole(keep_qkv[0], [d])]
    d_up, d_gain_two, d_out, d_down = finished(shares, w_up, ln2_gain, r, w_down.shape[0])
    m_qkv = sum_parts(shares_qkv, 0, r)
    d_qkv = m_qkv * ln1_gain.astype(F32)[:, None]
    d_gain_one = jnp.sum(m_qkv * w_qkv.astype(F32), axis=1)
    return (final, grad_states, grad_inject, d_gain_one, d_qkv, d_out, d_gain_two, d_up, d_down)

def solution(mesh):
    tok, vec, mat = P(("dp", "fsdp"), None), P("fsdp"), P("fsdp", None)
    return jax.shard_map(
        functools.partial(on_device, mesh.shape["dp"], mesh.shape["fsdp"]), mesh=mesh,
        in_specs=(tok, tok, vec, mat, mat, vec, mat, mat, tok, tok, tok),
        out_specs=(tok, tok, tok, vec, mat, mat, vec, mat, mat), check_vma=False)
```

```python
import functools
import types

import jax
import jax.numpy as jnp
from jax import lax
from jax.experimental import pallas as pl
from jax.experimental.pallas import tpu as pltpu
from jax.sharding import PartitionSpec as P

BF = jnp.bfloat16
F32 = jnp.float32
HEADS = 8
ITERS = 2
BLK = 128
CHUNK = 512
NEG = -1e30
LOG2E = 1.4426950408889634
LN2 = 0.6931471805599453
GELU_A = 0.7978845608028654
GELU_B = GELU_A * 0.044715
FLOPS_FIRST = 10 ** 9
FLOPS_PREPARE = 10 ** 9
FLOPS_LAST = 10 ** 10
LIMIT_MIDDLE = 40
LIMIT_LAST = 16


def dot(a, b):
    return jnp.dot(a, b, preferred_element_type=F32)

def dot_tn(a, b):
    return lax.dot_general(a, b, (((0,), (0,)), ((), ())), preferred_element_type=F32)

def dot_nt(a, b):
    return lax.dot_general(a, b, (((1,), (1,)), ((), ())), preferred_element_type=F32)

def rows(start, size):
    return pl.ds(start, size)

def ln_fwd(x):
    c = x - jnp.mean(x, axis=1, keepdims=True)
    r = lax.rsqrt(jnp.mean(c * c, axis=1, keepdims=True) + 1e-5)
    return c * r, r

def ln_bwd(y, n, r):
    return r * (y - jnp.mean(y, axis=1, keepdims=True) - n * jnp.mean(y * n, axis=1, keepdims=True))

def loop(n, body):
    for i in range(n):
        body(i)

def make_masks(len_ref, mask_ref, nb):
    pos = lax.broadcasted_iota(jnp.int32, (1, BLK), 1)
    ends = []
    total = jnp.int32(0)
    for p in range(len_ref.shape[1]):
        total = total + len_ref[0, p]
        ends.append(total)

    def block(i, _):
        q = pos + i * BLK
        start = jnp.zeros((1, BLK), jnp.int32)
        for e in ends:
            start = jnp.where(q >= e, e, start)
        k = lax.broadcasted_iota(jnp.int32, (2 * BLK, BLK), 0) + (i - 1) * BLK
        mask_ref[i] = jnp.where((k >= start) & (k <= q), 0.0, NEG).astype(F32)
        return 0

    lax.fori_loop(0, nb, block, 0)

def pad_zero(s):
    s.kp[0:BLK, :] = jnp.zeros((BLK, s.kp.shape[1]), BF)
    s.vp[0:BLK, :] = jnp.zeros((BLK, s.vp.shape[1]), BF)
    s.kt[0] = jnp.zeros(s.kt.shape[1:], BF)
    s.vt[0] = jnp.zeros(s.vt.shape[1:], BF)

def project(s, j, ent, wqkv):
    n, r = ln_fwd(ent)
    nb16 = n.astype(BF)
    s.n1[rows(j * CHUNK, CHUNK), :] = nb16
    s.r1[rows(j * CHUNK, CHUNK), :] = jnp.broadcast_to(r, (CHUNK, 128))
    pack_heads(s, j, nb16, wqkv)

def pack_heads(s, j, nb16, wqkv):
    d = nb16.shape[1]
    scale = LOG2E * (d // HEADS) ** -0.5
    q = (dot(nb16, wqkv[:, 0:d]) * scale).astype(BF)
    k = dot(nb16, wqkv[:, d:2 * d]).astype(BF)
    v = dot(nb16, wqkv[:, 2 * d:3 * d]).astype(BF)
    s.qs[rows(j * CHUNK, CHUNK), :] = q
    s.kp[pl.ds(j * CHUNK + BLK, CHUNK), :] = k
    s.vp[pl.ds(j * CHUNK + BLK, CHUNK), :] = v
    qt, kt, vt = q.T, k.T, v.T
    for b in range(CHUNK // BLK):
        i = j * (CHUNK // BLK) + b
        s.qst[i] = qt[:, b * BLK:(b + 1) * BLK]
        s.kt[i + 1] = kt[:, b * BLK:(b + 1) * BLK]
        s.vt[i + 1] = vt[:, b * BLK:(b + 1) * BLK]

def split_heads(tile, a, hd):
    def alone(lo):
        parts = [jnp.zeros((n, tile.shape[1]), tile.dtype) for n in (lo, tile.shape[0] - lo - hd)]
        parts = [parts[0], tile[lo:lo + hd], parts[1]]
        return jnp.concatenate([p for p in parts if p.shape[0]], axis=0)
    return jnp.concatenate([alone(a), alone(a + hd)], axis=1)

def stack_heads(tile, a, hd):
    z = jnp.zeros_like(tile)
    lane = lax.broadcasted_iota(jnp.int32, tile.shape, 1)
    top = jnp.where((lane >= a) & (lane < a + hd), tile, z)
    low = jnp.where((lane >= a + hd) & (lane < a + 2 * hd), tile, z)
    return jnp.concatenate([top, low], axis=0)

def pairs_of(d):
    hd = d // HEADS
    per = 128 // (2 * hd)
    return [(p, slice(p // per * 128, p // per * 128 + 128), p % per * 2 * hd, p * 2 * hd) for p in range(HEADS // 2)]

def window(ref, i, lo, n):
    return jnp.concatenate([ref[i, lo:lo + n, :], ref[i + 1, lo:lo + n, :]], axis=1)

def attend(s, blocks, mask_ref):
    d = s.qs.shape[1]
    hd = d // HEADS
    ones = jnp.ones((16, 2 * BLK), BF)
    def scores(i):
        win = pl.ds(i * BLK, 2 * BLK)
        return [dot(s.kp[win, tile], split_heads(s.qst[i, tile, :], a, hd)) for _, tile, a, _ in pairs_of(d)]
    def soft(i, all_scores):
        mask = mask_ref[i]
        mask = jnp.concatenate([mask, mask], axis=1)
        out = []
        for sc in all_scores:
            sc = sc + mask
            out.append(jnp.exp2(sc - jnp.max(sc, axis=0, keepdims=True)).astype(BF))
        return out
    def values(i, es):
        return [dot(jnp.concatenate([window(s.vt, i, lo, 2 * hd), ones], axis=0), es[p]) for p, _, _, lo in pairs_of(d)]
    es = []
    ready = scores(blocks[0])
    for n, i in enumerate(blocks):
        ahead = scores(blocks[n + 1]) if n + 1 < len(blocks) else None
        es.append(soft(i, ready))
        ready = ahead
    os = [values(i, e) for i, e in zip(blocks, es)]
    for i, e, o in zip(blocks, es, os):
        for p, _, _, lo in pairs_of(d):
            s.e[i, p] = e[p]
            inv = 1.0 / o[p][2 * hd:2 * hd + 1, :]
            s.linv[i, 2 * p:2 * p + 1, :] = inv[:, :BLK]
            s.linv[i, 2 * p + 1:2 * p + 2, :] = inv[:, BLK:]
            s.ht[i, lo:lo + hd, :] = (o[p][0:hd, :BLK] * inv[:, :BLK]).astype(BF)
            s.ht[i, lo + hd:lo + 2 * hd, :] = (o[p][hd:2 * hd, BLK:] * inv[:, BLK:]).astype(BF)

def heads_chunk(s, j):
    return jnp.concatenate([s.ht[j * (CHUNK // BLK) + b] for b in range(CHUNK // BLK)], axis=1)

def mlp(s, j, ent, wout, wup, wdown):
    mid = ent + dot_tn(heads_chunk(s, j), wout[...])
    n, r = ln_fwd(mid)
    nb16 = n.astype(BF)
    at = rows(j * CHUNK, CHUNK)
    s.n2[at, :] = nb16
    s.r2[at, :] = jnp.broadcast_to(r, (CHUNK, 128))
    acc = mid
    for f in range(wup.shape[1] // 256):
        c = slice(f * 256, (f + 1) * 256)
        h = dot(nb16, wup[:, c]).astype(BF)
        h2 = h * h
        sg = 0.5 * jnp.tanh(h * (GELU_B * h2 + GELU_A)) + 0.5
        act = h * sg
        s.act[at, c] = act
        s.gp[at, c] = sg + act * (2.0 - 2.0 * sg) * (3 * GELU_B * h2 + GELU_A)
        acc = acc + dot(act, wdown[c, :])
    return acc

def mlp_back(s, j, g, wdown_t, wup_t):
    at = rows(j * CHUNK, CHUNK)
    gb = g.astype(BF)
    s.g2[at, :] = gb
    acc = None
    for f in range(wdown_t.shape[1] // 256):
        c = slice(f * 256, (f + 1) * 256)
        dh = dot(gb, wdown_t[:, c]).astype(BF) * s.gp[at, c]
        s.gp[at, c] = dh
        part = dot(dh, wup_t[c, :])
        acc = part if acc is None else acc + part
    g = g + ln_bwd(acc, s.n2[at, :].astype(F32), s.r2[at, 0:1])
    s.gm[at, :] = g.astype(BF)
    return g

def attend_back(s, blocks, wout, dk_ref, dv_ref):
    d = s.qs.shape[1]
    hd = d // HEADS
    minus = jnp.full((2 * BLK, 128), -1.0, BF)
    def head_grads(i):
        raw = dot_nt(wout[...], s.gm[rows(i * BLK, BLK), :])
        inv = jnp.concatenate([jnp.broadcast_to(s.linv[i, h:h + 1, :], (hd, BLK)) for h in range(HEADS)], axis=0)
        dost = (raw * inv).astype(BF)
        return dost, (dost.astype(F32) * s.ht[i].astype(F32)).astype(BF), dost.T
    def prob_grads(i, dost, doh):
        win = pl.ds(i * BLK, 2 * BLK)
        return [dot(jnp.concatenate([s.vp[win, tile], minus], axis=1),
                    jnp.concatenate([split_heads(dost[tile, :], a, hd), split_heads(doh[tile, :], a, hd)], axis=0))
                for _, tile, a, _ in pairs_of(d)]
    def by_keys(lhs, tokens):
        return [dot(lhs[p], stack_heads(tokens[:, tile], a, hd)) for p, tile, a, _ in pairs_of(d)]
    def by_queries(i, dss):
        out = []
        for p, _, _, lo in pairs_of(d):
            dq = dot(window(s.kt, i, lo, 2 * hd), dss[p])
            out += [dq[0:hd, :BLK], dq[hd:2 * hd, BLK:]]
        return (jnp.concatenate(out, axis=0) * hd ** -0.5).astype(BF)
    heads = [head_grads(i) for i in blocks]
    dps = [prob_grads(i, h[0], h[1]) for i, h in zip(blocks, heads)]
    es = [[s.e[i, p] for p in range(HEADS // 2)] for i in blocks]
    dvs = [by_keys(e, h[2]) for e, h in zip(es, heads)]
    dss = [[(x.astype(F32) * y).astype(BF) for x, y in zip(e, dp)] for e, dp in zip(es, dps)]
    dks = [by_keys(ds, s.qs[rows(i * BLK, BLK), :]) for i, ds in zip(blocks, dss)]
    dqs = [by_queries(i, ds) for i, ds in zip(blocks, dss)]
    per = HEADS // 2 // (d // 128)
    for n, i in enumerate(blocks):
        top, low = pl.ds(i * BLK, BLK), pl.ds(i * BLK + BLK, BLK)
        for ref, parts in ((dk_ref, dks[n]), (dv_ref, dvs[n])):
            for t in range(d // 128):
                tile = slice(t * 128, (t + 1) * 128)
                total = sum(parts[t * per + 1:(t + 1) * per], parts[t * per])
                ref[top, tile] += total[:BLK]
                ref[low, tile] = total[BLK:]
        s.dpk[rows(i * BLK, BLK), 0:d] = dqs[n].T

def finish_packed(s, j, dk_ref, dv_ref):
    d = s.n1.shape[1]
    at = rows(j * CHUNK, CHUNK)
    pat = pl.ds(j * CHUNK + BLK, CHUNK)
    s.dpk[at, d:2 * d] = (dk_ref[pat, :] * LN2).astype(BF)
    s.dpk[at, 2 * d:3 * d] = dv_ref[pat, :].astype(BF)

def project_back(s, j, g, wqkv_t):
    at = rows(j * CHUNK, CHUNK)
    return g + ln_bwd(dot(s.dpk[at, :], wqkv_t[...]), s.n1[at, :].astype(F32), s.r1[at, 0:1])

def weigh(cnt_ref, len_ref, j, cot):
    pos = lax.broadcasted_iota(jnp.int32, (CHUNK, 128), 0) + j * CHUNK
    w = jnp.zeros((CHUNK, 128), F32)
    begin = jnp.int32(0)
    for p in range(len_ref.shape[1]):
        w = jnp.where(pos >= begin, 12.0 / cnt_ref[0, p].astype(F32), w)
        begin = begin + len_ref[0, p]
    return cot * jnp.concatenate([w] * (cot.shape[1] // 128), axis=1)

def saved_shapes(t, d, ff):
    nb = t // BLK
    return dict(n1=((t, d), BF), r1=((t, 128), F32), qs=((t, d), BF), kp=((t + BLK, d), BF), vp=((t + BLK, d), BF),
                qst=((nb, d, BLK), BF), kt=((nb + 1, d, BLK), BF), vt=((nb + 1, d, BLK), BF), e=((nb, HEADS // 2, 2 * BLK, 2 * BLK), BF),
                ht=((nb, d, BLK), BF), linv=((nb, HEADS, BLK), F32))
def more_shapes(t, d, ff):
    return dict(n2=((t, d), BF), r2=((t, 128), F32), act=((t, ff), BF), gp=((t, ff), BF),
                g2=((t, d), BF), gm=((t, d), BF), dpk=((t, 3 * d), BF))

class Memory:
    def __init__(self, ins, outs, sems, hbm, loads):
        self.ins, self.outs, self.sems, self.hbm, self.loads, self.started = ins, outs, sems, hbm, loads, []

    def wait(self, *which):
        for n in which:
            self.loads[n].wait()

    def put(self, n):
        copy = pltpu.make_async_copy(self.outs[n], self.hbm[n], self.sems.at[len(self.started)])
        copy.start()
        self.started.append(copy)

def call(kernel, outs, args, scratch, name, flops, limit=16):
    spec = dict(vmem=pl.BlockSpec(memory_space=pltpu.VMEM), smem=pl.BlockSpec(memory_space=pltpu.SMEM), any=pl.BlockSpec(memory_space=pl.ANY))
    spec["store"] = spec["load"] = spec["any"]
    n_in, n_out, n_scratch = len(args), len(outs), len(scratch)
    stores = [n for n, o in enumerate(outs) if o[0] == "store"]
    loads = [n for n, a in enumerate(args) if a[0] == "load"]
    buffers = [pltpu.VMEM(outs[n][1], outs[n][2]) for n in stores] + [(pltpu.SMEM if args[n][1].dtype == jnp.int32 else pltpu.VMEM)(args[n][1].shape, args[n][1].dtype) for n in loads]
    buffers += [pltpu.SemaphoreType.DMA((max(len(stores), 1),)), pltpu.SemaphoreType.DMA((max(len(loads), 1),))]
    def run(*refs):
        ins, results, rest = list(refs[:n_in]), list(refs[n_in:n_in + n_out]), refs[n_in + n_out:]
        hbm, coming = list(results), {}
        for n, r in zip(stores, rest[n_scratch:]):
            results[n] = r
        for c, (n, r) in enumerate(zip(loads, rest[n_scratch + len(stores):])):
            coming[n] = pltpu.make_async_copy(ins[n], r, rest[-1].at[c])
            coming[n].start()
            ins[n] = r
        memory = Memory(ins, results, rest[-2], hbm, coming)
        kernel(memory, types.SimpleNamespace(**dict(zip(scratch, rest))))
        for copy in memory.started:
            copy.wait()
    shapes = dict(vmem=pltpu.VMEM, store=jax.ShapeDtypeStruct)
    place = dict(vmem=pltpu.VMEM, load=pltpu.HBM)
    return pl.pallas_call(
        run, out_shape=tuple(shapes[o[0]](o[1], o[2]) for o in outs),
        in_specs=[spec[k] for k, _ in args], out_specs=tuple(spec[o[0]] for o in outs),
        scratch_shapes=[pltpu.VMEM(*v) for v in scratch.values()] + buffers,
        compiler_params=pltpu.CompilerParams(vmem_limit_bytes=limit << 20), name=name,
        cost_estimate=pl.CostEstimate(flops=flops, bytes_accessed=1 << 20, transcendentals=0))(
        *[pltpu.with_memory_space_constraint(v, place[k]) if k in place else v for k, v in args])

def place_qkv(me, parts, wqkv):
    r = wqkv.shape[0] // len(parts)
    for x, p in enumerate(parts):
        wqkv[pl.ds(pl.multiple_of((me ^ x) * r, r), r), :] = p[...]

def place_rest(me, parts, wout, wup, wdown):
    r, rd = wout.shape[0] // len(parts), wdown.shape[0] // len(parts)
    for x, p in enumerate(parts):
        at = pl.ds(pl.multiple_of((me ^ x) * r, r), r)
        wout[at, :] = p[0:r, :]
        for c in range(wup.shape[1] // 256):
            wup[at, c * 256:(c + 1) * 256] = p[(c + 1) * r:(c + 2) * r, :]
        lo = r * (1 + wup.shape[1] // 256)
        wdown[pl.ds(pl.multiple_of((me ^ x) * rd, rd), rd), :] = p[lo:lo + rd, :]

def hand_out(me, parts, mats, keep, send):
    for x in range(parts):
        dst = send if x % 2 else keep
        lo = 0
        for m in mats:
            r = m.shape[0] // parts
            at = pl.ds(pl.multiple_of((me ^ x) * r, r), r)
            for c in range(m.shape[1] // 256):
                dst[x // 2, lo:lo + r, :] = m[at, c * 256:(c + 1) * 256]
                lo += r

SAVED = ("e", "n1", "r1", "qs", "vp", "kt", "ht", "linv")

def prepare(lengths, counts, states, inject, cot):
    t, d = states.shape
    nb, nc = t // BLK, t // CHUNK
    def kernel(m, s):
        len_ref, cnt_ref, st, inj, ct = m.ins
        ent, inj_out, g, n1, r1, mask = m.outs
        m.wait(0, 1)
        make_masks(len_ref, mask, nb)
        m.wait(2, 3)
        for j in range(nc):
            at = slice(j * CHUNK, (j + 1) * CHUNK)
            x = st[at, :] + inj[at, :]
            ent[at, :] = x
            inj_out[at, :] = inj[at, :]
            n, r = ln_fwd(x)
            n1[at, :] = n.astype(BF)
            r1[at, :] = jnp.broadcast_to(r, (CHUNK, 128))
        m.wait(4)
        for j in range(nc):
            at = slice(j * CHUNK, (j + 1) * CHUNK)
            g[at, :] = weigh(cnt_ref, len_ref, j, ct[at, :])
    outs = [("vmem", (t, d), F32)] * 3 + [("vmem", (t, d), BF), ("vmem", (t, 128), F32), ("vmem", (nb, 2 * BLK, BLK), F32)]
    args = [("load", v) for v in (lengths, counts, states, inject, cot)]
    return call(kernel, outs, args, {}, "prepare", FLOPS_PREPARE)

def first_attention(me, n1, mask, qkv_parts, ff):
    t, d = n1.shape
    nb, nc = t // BLK, t // CHUNK
    shapes = saved_shapes(t, d, ff)
    made = [k for k in SAVED if k not in ("n1", "r1")]
    scratch = {k: v for k, v in shapes.items() if k not in SAVED}
    def kernel(m, s):
        me_ref, n1_ref, mask_ref = m.ins[:3]
        vars(s).update(zip(made, m.outs))
        wqkv = m.outs[-1]
        pad_zero(s)
        place_qkv(me_ref[0], m.ins[3:], wqkv)
        for j in range(nc):
            pack_heads(s, j, n1_ref[j * CHUNK:(j + 1) * CHUNK, :], wqkv)
        for i in range(0, nb, 2):
            attend(s, (i, i + 1), mask_ref)
    outs = [("vmem",) + shapes[k] for k in made] + [("vmem", (d, 3 * d), BF)]
    args = [("smem", me), ("vmem", n1), ("vmem", mask)] + [("vmem", p) for p in qkv_parts]
    got = call(kernel, outs, args, scratch, "first_attention", FLOPS_FIRST)
    return dict(zip(made, got)), got[-1]

def middle_part(me, ent, inject, weighed, mask, wqkv, ht, rest_parts, ff):
    t, d = ent.shape
    nb, nc = t // BLK, t // CHUNK
    parts = len(rest_parts)
    sh = {"a_" + k: v for k, v in more_shapes(t, d, ff).items() if k not in ("dpk", "gm")}
    sh.update({"b_" + k: v for k, v in {**saved_shapes(t, d, ff), **more_shapes(t, d, ff)}.items()})
    sh.update(state=((t, d), F32), dk=((t + BLK, d), F32), dv=((t + BLK, d), F32),
              wqkv_t=((3 * d, d), BF), wup_t=((ff, d), BF), wdown_t=((d, ff), BF), tr=((2, d, t), BF),
              wup=((d, ff), BF), wdown=((ff, d), BF), mout=((d, d), BF), mup=((d, ff), BF), mdown_t=((d, ff), BF), mdown=((ff, d), BF))
    def kernel(m, x):
        me_ref, ent_ref, inj, weighed_ref, x.mask, wqkv_ref, ht_ref = m.ins[:7]
        final, g, ginj, gm, wout, mqkv, keep, send = m.outs
        its = [types.SimpleNamespace(**{k[2:]: v for k, v in vars(x).items() if k.startswith(p)}) for p in ("a_", "b_")]
        its[0].ht, its[0].gm = ht_ref, gm
        place_rest(me_ref[0], m.ins[7:], wout, x.wup, x.wdown)
        x.wup_t[...] = x.wup[...].T
        x.wdown_t[...] = x.wdown[...].T
        pad_zero(its[1])
        x.wqkv_t[...] = wqkv_ref[...].T
        def rows_of(j):
            return slice(j * CHUNK, (j + 1) * CHUNK)
        def mlp_of(n, j, src, dst):
            at = rows_of(j)
            entered = src[at, :] + inj[at, :] if n else src[at, :]
            dst[at, :] = mlp(its[n], j, entered, wout, x.wup, x.wdown)
        def project_of(j):
            project(its[1], j, x.state[rows_of(j), :] + inj[rows_of(j), :], wqkv_ref)
        def blocks_of(j):
            n = CHUNK // BLK
            return [tuple(range(j * n + b, min(j * n + b + 2, j * n + n))) for b in range(0, n, 2)]
        def attend_of(j):
            for blocks in blocks_of(j):
                attend(its[1], blocks, x.mask)
        def back_two(j):
            at = rows_of(j)
            g[at, :] = mlp_back(its[1], j, weighed_ref[at, :], x.wdown_t, x.wup_t)
        def attend_back_of(j):
            for blocks in blocks_of(j):
                attend_back(its[1], blocks, wout, x.dk, x.dv)
        def back_one(j):
            at = rows_of(j)
            finish_packed(its[1], j, x.dk, x.dv)
            new = project_back(its[1], j, g[at, :], x.wqkv_t)
            ginj[at, :] = new
            g[at, :] = mlp_back(its[0], j, new, x.wdown_t, x.wup_t)
        x.dk[0:BLK, :] = jnp.zeros((BLK, d), F32)
        x.dv[0:BLK, :] = jnp.zeros((BLK, d), F32)
        for j in range(nc): mlp_of(0, j, ent_ref, x.state)
        for j in range(nc): project_of(j)
        for j in range(nc): attend_of(j)
        for j in range(nc): mlp_of(1, j, x.state, final)
        m.put(0)
        for j in range(nc): back_two(j)
        for j in range(nc): attend_back_of(j)
        for j in range(nc): back_one(j)

        def weight_grad(lefts, rights, dst):
            for n, left in enumerate(lefts):
                x.tr[n] = left[...].T
            def tile(c):
                cc = pl.ds(c * 256, 256)
                total = dot(x.tr[0], rights[0][:, cc])
                for n in range(1, len(rights)):
                    total = total + dot(x.tr[n], rights[n][:, cc])
                dst[:, cc] = total.astype(dst.dtype)
            loop(dst.shape[1] // 256, tile)
        weight_grad([s.g2 for s in its], [s.act for s in its], x.mdown_t)
        x.mdown[...] = x.mdown_t[...].T
        weight_grad([s.n2 for s in its], [s.gp for s in its], x.mup)
        weight_grad([its[1].n1], [its[1].dpk], mqkv)
        total = None
        for s in its:
            for b in range(nb):
                part = dot(s.ht[b], s.gm[b * BLK:(b + 1) * BLK, :])
                total = part if total is None else total + part
        x.mout[...] = total.astype(BF)
        hand_out(me_ref[0], parts, (x.mout, x.mup, x.mdown), keep, send)
    piece = ("vmem", (max(parts // 2, 1), (d + ff) // parts + ff // parts, d), BF)
    outs = [("store", (t, d), F32)] + [("vmem", (t, d), F32)] * 2 + [("vmem", (t, d), BF), ("vmem", (d, d), BF), ("vmem", (d, 3 * d), F32)] + [piece] * 2
    args = [("smem", me)] + [("vmem", v) for v in (ent, inject, weighed, mask, wqkv, ht, *rest_parts)]
    return call(kernel, outs, args, sh, "middle_part", 25 * 10 ** 9, limit=LIMIT_MIDDLE)

def last_part(me, saved, gm, wout, wqkv, mqkv, g, ginj, parts, ff, first):
    t, d = gm.shape
    nb, nc = t // BLK, t // CHUNK
    scratch = dict(dk=((t + BLK, d), F32), dv=((t + BLK, d), F32), tr=((d, t), BF), mat=((d, 3 * d), BF), wt=((3 * d, d), BF), dpk=((t, 3 * d), BF))
    def kernel(m, s):
        me_ref, s.gm, wout_ref, w_ref, m_ref, g_ref, gi_ref = m.ins[:7]
        vars(s).update(zip(SAVED, m.ins[7:]))
        keep, send, grad, grad_inject = m.outs
        s.dk[0:BLK, :] = jnp.zeros((BLK, d), F32)
        s.dv[0:BLK, :] = jnp.zeros((BLK, d), F32)
        for i in range(0, nb, 2):
            attend_back(s, (i, i + 1), wout_ref, s.dk, s.dv)
        s.tr[...] = s.n1[...].T
        s.wt[...] = w_ref[...].T
        loop(nc, lambda j: finish_packed(s, j, s.dk, s.dv))
        def tile(c):
            cc = slice(c * 256, (c + 1) * 256)
            s.mat[:, cc] = (m_ref[:, cc] + dot(s.tr[...], s.dpk[:, cc])).astype(BF)
        loop(3, tile)
        hand_out(me_ref[0], parts, (s.mat,), keep, send)
        def chunk(j):
            at = rows(j * CHUNK, CHUNK)
            new = project_back(s, j, g_ref[at, :], s.wt)
            grad[at, :] = new
            grad_inject[at, :] = new + gi_ref[at, :]
        loop(nc, chunk)
        m.put(2)
        m.put(3)
    outs = [("vmem", (max(parts // 2, 1), 3 * d // parts, d), BF)] * 2 + [("store", (t, d), F32)] * 2
    args = [("smem", me)] + [("vmem", v) for v in (gm, wout, wqkv, mqkv, g, ginj)]
    args += [("vmem", saved[k]) for k in SAVED] + [("any", v) for v in first]
    return call(kernel, outs, args, scratch, "last_part", FLOPS_LAST, limit=LIMIT_LAST)

def to_column(row):
    n = row.shape[1]
    eye = lax.broadcasted_iota(jnp.int32, (n, n), 0) == lax.broadcasted_iota(jnp.int32, (n, n), 1)
    return jnp.sum(jnp.where(eye, jnp.broadcast_to(row, (n, n)), 0.0), axis=1, keepdims=True)

def to_row(column):
    n = column.shape[0]
    eye = lax.broadcasted_iota(jnp.int32, (n, n), 0) == lax.broadcasted_iota(jnp.int32, (n, n), 1)
    return jnp.sum(jnp.where(eye, jnp.broadcast_to(column, (n, n)), 0.0), axis=0, keepdims=True)

def pack_weights(w_qkv, gain_one, w_out, w_up, w_down, gain_two):
    r, d = w_out.shape
    n = w_up.shape[1] // d
    def kernel(m, s):
        qkv, g_one, out, up, down, g_two = m.ins
        m.wait(0, 1)
        m.outs[0][...] = (qkv[...].astype(F32) * to_column(g_one[...].astype(F32))).astype(BF)
        m.wait(2, 3, 4, 5)
        m.outs[1][0:r, :] = out[...]
        col = to_column(g_two[...].astype(F32))
        for c in range(n):
            m.outs[1][(c + 1) * r:(c + 2) * r, :] = (up[:, c * d:(c + 1) * d].astype(F32) * col).astype(BF)
        m.outs[1][(n + 1) * r:, :] = down[...]
    args = [("load", v) for v in (w_qkv, gain_one.reshape(1, -1), w_out, w_up, w_down, gain_two.reshape(1, -1))]
    return call(kernel, [("vmem", w_qkv.shape, BF), ("vmem", ((n + 1) * r + w_down.shape[0], d), BF)], args, {}, "pack_weights", 10 ** 6)

def sum_parts(parts, lo, size):
    acc = parts[0][lo:lo + size, :].astype(F32)
    for p in parts[1:]:
        acc = acc + p[lo:lo + size, :].astype(F32)
    return acc

def finished(shares, weight, gain, lead, tail, name):
    r, cols = weight.shape
    d = shares[0].shape[1]
    n = cols // d
    def kernel(m, s):
        w, g, parts = m.ins[0], to_column(m.ins[1][...].astype(F32)), m.ins[2:]
        along = jnp.zeros((r, 1), F32)
        for c in range(n):
            v = sum_parts(parts, lead + c * r, r)
            m.outs[0][:, c * d:(c + 1) * d] = v * g
            along = along + jnp.sum(v * w[:, c * d:(c + 1) * d].astype(F32), axis=1, keepdims=True)
        m.put(0)
        m.outs[1][...] = to_row(along)
        m.put(1)
        if lead:
            m.outs[2][...] = sum_parts(parts, 0, lead)
            m.outs[3][...] = sum_parts(parts, lead + n * r, tail)
            m.put(2)
            m.put(3)
    outs = [("store", (r, cols), F32), ("store", (1, r), F32)] + ([("store", (lead, d), F32), ("store", (tail, d), F32)] if lead else [])
    got = call(kernel, outs, [("vmem", v) for v in (weight, gain.reshape(1, -1), *shares)], {}, name, 10 ** 6)
    return [got[0], got[1].reshape(r)] + list(got[2:])

def after(values, *others):
    return lax.optimization_barrier((values, others))[0]

def exchange(x, axis, size, step):
    return lax.ppermute(x, axis, [(i, i ^ step) for i in range(size)])

def far_parts(x, size):
    return [x] + [exchange(x, "fsdp", size, 2 * k) for k in range(1, size // 2)]

def with_near(far, size):
    return [v for x in far for v in (x, exchange(x, "fsdp", size, 1))]

def sum_near(keep, near, then=None):
    total = keep.astype(F32) + near.astype(F32)
    if then is not None:
        total = total + jnp.minimum(jnp.abs(then[:keep.shape[1]].astype(F32)), 0.0)
    return [total[k].astype(BF) for k in range(keep.shape[0])]

def send_far(summed, size):
    return [exchange(summed[k], "fsdp", size, 2 * k) for k in range(1, size // 2)]

def along_dp(share, size):
    return [share] + [exchange(share, "dp", size, k) for k in range(1, size)]

def send_near(pieces, size):
    return [exchange(p, "fsdp", size, 1) for p in pieces[1::2]]

def send_far(summed, size):
    return [exchange(summed[k], "fsdp", size, 2 * k) for k in range(1, size // 2)]

def reduce_whole(whole, sizes):
    out, lo = [], 0
    for n in sizes:
        share = lax.psum_scatter(whole[lo:lo + n], "fsdp", scatter_dimension=0, tiled=True)
        out.append(lax.psum(share, "dp").astype(F32))
        lo += n
    return jnp.concatenate(out, axis=0)

def on_device(n_dp, n_fsdp, states, inject, ln1_gain, w_qkv, w_out, ln2_gain, w_up, w_down, prompt_lengths, loop_counts, cotangent):
    d = states.shape[1]
    r, ff = w_up.shape
    direct = r % 16 == 0
    if direct:
        me = lax.axis_index("fsdp").astype(jnp.int32).reshape(1)
        own_qkv, own_rest = pack_weights(w_qkv, ln1_gain, w_out, w_up, w_down, ln2_gain)
        qkv_far = far_parts(own_qkv, n_fsdp)
        rest_far = far_parts(own_rest, n_fsdp)
        qkv_parts = with_near(qkv_far, n_fsdp)
    else:
        me = jnp.zeros((1,), jnp.int32)
        full = lambda v: lax.all_gather(v, "fsdp", axis=0, tiled=True)
        up = full((w_up.astype(F32) * ln2_gain.astype(F32)[:, None]).astype(BF))
        qkv_parts = [full((w_qkv.astype(F32) * ln1_gain.astype(F32)[:, None]).astype(BF))]
        rest_parts = [jnp.concatenate([full(w_out)] + [up[:, c:c + d] for c in range(0, ff, d)] + [full(w_down)], axis=0)]
    parts = len(qkv_parts)
    ent, inject, weighed, n1, r1, mask = prepare(prompt_lengths, loop_counts, states, inject, cotangent)
    saved, wqkv = first_attention(me, n1, mask, qkv_parts, ff)
    saved.update(n1=n1, r1=r1)
    if direct:
        rest_parts = with_near(after(rest_far, wqkv), n_fsdp)
    final, g, ginj, gm, wout, mqkv, keep, send = middle_part(
        me, ent, inject, weighed, mask, wqkv, saved["ht"], rest_parts, ff)
    summed = []
    if direct:
        summed = sum_near(keep, exchange(send, "fsdp", n_fsdp, 1))
        far = send_far(summed, n_fsdp)
    else:
        shares = [reduce_whole(keep[0], [d] * (1 + ff // d) + [ff])]
    keep_qkv, send_qkv, grad_states, grad_inject = last_part(me, saved, gm, wout, wqkv, mqkv, g, ginj, parts, ff, summed)
    if direct:
        near = exchange(send_qkv, "fsdp", n_fsdp, 1)
        share = sum_parts([summed[0], *far], 0, summed[0].shape[0]).astype(BF)
        shares = along_dp(share, n_dp)
        summed = sum_near(keep_qkv, near, share)
        shares_qkv = along_dp(sum_parts([summed[0], *send_far(summed, n_fsdp)], 0, 3 * r).astype(BF), n_dp)
    else:
        shares_qkv = [reduce_whole(keep_qkv[0], [d] * 3)]
    d_up, d_gain_two, d_out, d_down = finished(shares, w_up, ln2_gain, r, w_down.shape[0], "finished_rest")
    d_qkv, d_gain_one = finished(shares_qkv, w_qkv, ln1_gain, 0, 0, "finished_qkv")
    return (final, grad_states, grad_inject, d_gain_one, d_qkv, d_out, d_gain_two, d_up, d_down)

def solution(mesh):
    tok, vec, mat = P(("dp", "fsdp"), None), P("fsdp"), P("fsdp", None)
    return jax.shard_map(
        functools.partial(on_device, mesh.shape["dp"], mesh.shape["fsdp"]), mesh=mesh,
        in_specs=(tok, tok, vec, mat, mat, vec, mat, mat, tok, tok, tok),
        out_specs=(tok, tok, tok, vec, mat, mat, vec, mat, mat), check_vma=False)
```

```python
import functools
import types

import jax
import jax.numpy as jnp
from jax import lax
from jax.experimental import pallas as pl
from jax.experimental.pallas import tpu as pltpu
from jax.sharding import PartitionSpec as P

BF = jnp.bfloat16
F32 = jnp.float32
HEADS = 8
ITERS = 2
BLK = 128
CHUNK = 512
NEG = -1e30
LOG2E = 1.4426950408889634
LN2 = 0.6931471805599453
GELU_A = 0.7978845608028654
GELU_B = GELU_A * 0.044715
FLOPS_FIRST = 10 ** 6
FLOPS_PREPARE = 10 ** 6
FLOPS_LAST = 10 ** 10
LIMIT_MIDDLE = 40
LIMIT_LAST = 16


def dot(a, b):
    return jnp.dot(a, b, preferred_element_type=F32)

def dot_tn(a, b):
    return lax.dot_general(a, b, (((0,), (0,)), ((), ())), preferred_element_type=F32)

def dot_nt(a, b):
    return lax.dot_general(a, b, (((1,), (1,)), ((), ())), preferred_element_type=F32)

def rows(start, size):
    return pl.ds(start, size)

def ln_fwd(x):
    c = x - jnp.mean(x, axis=1, keepdims=True)
    r = lax.rsqrt(jnp.mean(c * c, axis=1, keepdims=True) + 1e-5)
    return c * r, r

def ln_bwd(y, n, r):
    return r * (y - jnp.mean(y, axis=1, keepdims=True) - n * jnp.mean(y * n, axis=1, keepdims=True))

def loop(n, body):
    for i in range(n):
        body(i)

def make_masks(len_ref, mask_ref, nb):
    pos = lax.broadcasted_iota(jnp.int32, (1, BLK), 1)
    ends = []
    total = jnp.int32(0)
    for p in range(len_ref.shape[1]):
        total = total + len_ref[0, p]
        ends.append(total)

    def block(i, _):
        q = pos + i * BLK
        start = jnp.zeros((1, BLK), jnp.int32)
        for e in ends:
            start = jnp.where(q >= e, e, start)
        k = lax.broadcasted_iota(jnp.int32, (2 * BLK, BLK), 0) + (i - 1) * BLK
        mask_ref[i] = jnp.where((k >= start) & (k <= q), 0.0, NEG).astype(F32)
        return 0

    lax.fori_loop(0, nb, block, 0)

def pad_zero(s):
    s.kp[0:BLK, :] = jnp.zeros((BLK, s.kp.shape[1]), BF)
    s.vp[0:BLK, :] = jnp.zeros((BLK, s.vp.shape[1]), BF)
    s.kt[0] = jnp.zeros(s.kt.shape[1:], BF)
    s.vt[0] = jnp.zeros(s.vt.shape[1:], BF)

def project(s, j, ent, wqkv):
    n, r = ln_fwd(ent)
    nb16 = n.astype(BF)
    s.n1[rows(j * CHUNK, CHUNK), :] = nb16
    s.r1[rows(j * CHUNK, CHUNK), :] = jnp.broadcast_to(r, (CHUNK, 128))
    pack_heads(s, j, nb16, wqkv)

def pack_heads(s, j, nb16, wqkv):
    d = nb16.shape[1]
    scale = LOG2E * (d // HEADS) ** -0.5
    q = (dot(nb16, wqkv[:, 0:d]) * scale).astype(BF)
    k = dot(nb16, wqkv[:, d:2 * d]).astype(BF)
    v = dot(nb16, wqkv[:, 2 * d:3 * d]).astype(BF)
    s.qs[rows(j * CHUNK, CHUNK), :] = q
    s.kp[pl.ds(j * CHUNK + BLK, CHUNK), :] = k
    s.vp[pl.ds(j * CHUNK + BLK, CHUNK), :] = v
    qt, kt, vt = q.T, k.T, v.T
    for b in range(CHUNK // BLK):
        i = j * (CHUNK // BLK) + b
        s.qst[i] = qt[:, b * BLK:(b + 1) * BLK]
        s.kt[i + 1] = kt[:, b * BLK:(b + 1) * BLK]
        s.vt[i + 1] = vt[:, b * BLK:(b + 1) * BLK]

def split_heads(tile, a, hd):
    def alone(lo):
        parts = [jnp.zeros((n, tile.shape[1]), tile.dtype) for n in (lo, tile.shape[0] - lo - hd)]
        parts = [parts[0], tile[lo:lo + hd], parts[1]]
        return jnp.concatenate([p for p in parts if p.shape[0]], axis=0)
    return jnp.concatenate([alone(a), alone(a + hd)], axis=1)

def stack_heads(tile, a, hd):
    z = jnp.zeros_like(tile)
    lane = lax.broadcasted_iota(jnp.int32, tile.shape, 1)
    top = jnp.where((lane >= a) & (lane < a + hd), tile, z)
    low = jnp.where((lane >= a + hd) & (lane < a + 2 * hd), tile, z)
    return jnp.concatenate([top, low], axis=0)

def pairs_of(d):
    hd = d // HEADS
    per = 128 // (2 * hd)
    return [(p, slice(p // per * 128, p // per * 128 + 128), p % per * 2 * hd, p * 2 * hd) for p in range(HEADS // 2)]

def window(ref, i, lo, n):
    return jnp.concatenate([ref[i, lo:lo + n, :], ref[i + 1, lo:lo + n, :]], axis=1)

def attend(s, blocks, mask_ref):
    d = s.qs.shape[1]
    hd = d // HEADS
    ones = jnp.ones((16, 2 * BLK), BF)
    def scores(i):
        win = pl.ds(i * BLK, 2 * BLK)
        return [dot(s.kp[win, tile], split_heads(s.qst[i, tile, :], a, hd)) for _, tile, a, _ in pairs_of(d)]
    def soft(i, all_scores):
        mask = mask_ref[i]
        mask = jnp.concatenate([mask, mask], axis=1)
        out = []
        for sc in all_scores:
            sc = sc + mask
            out.append(jnp.exp2(sc - jnp.max(sc, axis=0, keepdims=True)).astype(BF))
        return out
    def values(i, es):
        return [dot(jnp.concatenate([window(s.vt, i, lo, 2 * hd), ones], axis=0), es[p]) for p, _, _, lo in pairs_of(d)]
    es = []
    ready = scores(blocks[0])
    for n, i in enumerate(blocks):
        ahead = scores(blocks[n + 1]) if n + 1 < len(blocks) else None
        es.append(soft(i, ready))
        ready = ahead
    os = [values(i, e) for i, e in zip(blocks, es)]
    for i, e, o in zip(blocks, es, os):
        for p, _, _, lo in pairs_of(d):
            s.e[i, p] = e[p]
            inv = 1.0 / o[p][2 * hd:2 * hd + 1, :]
            s.linv[i, 2 * p:2 * p + 1, :] = inv[:, :BLK]
            s.linv[i, 2 * p + 1:2 * p + 2, :] = inv[:, BLK:]
            s.ht[i, lo:lo + hd, :] = (o[p][0:hd, :BLK] * inv[:, :BLK]).astype(BF)
            s.ht[i, lo + hd:lo + 2 * hd, :] = (o[p][hd:2 * hd, BLK:] * inv[:, BLK:]).astype(BF)

def heads_chunk(s, j):
    return jnp.concatenate([s.ht[j * (CHUNK // BLK) + b] for b in range(CHUNK // BLK)], axis=1)

def mlp(s, j, ent, wout, wup, wdown):
    mid = ent + dot_tn(heads_chunk(s, j), wout[...])
    n, r = ln_fwd(mid)
    nb16 = n.astype(BF)
    at = rows(j * CHUNK, CHUNK)
    s.n2[at, :] = nb16
    s.r2[at, :] = jnp.broadcast_to(r, (CHUNK, 128))
    acc = mid
    for f in range(wup.shape[1] // 256):
        c = slice(f * 256, (f + 1) * 256)
        h = dot(nb16, wup[:, c]).astype(BF)
        h2 = h * h
        sg = 0.5 * jnp.tanh(h * (GELU_B * h2 + GELU_A)) + 0.5
        act = h * sg
        s.act[at, c] = act
        s.gp[at, c] = sg + act * (2.0 - 2.0 * sg) * (3 * GELU_B * h2 + GELU_A)
        acc = acc + dot(act, wdown[c, :])
    return acc

def mlp_back(s, j, g, wdown_t, wup_t):
    at = rows(j * CHUNK, CHUNK)
    gb = g.astype(BF)
    s.g2[at, :] = gb
    acc = None
    for f in range(wdown_t.shape[1] // 256):
        c = slice(f * 256, (f + 1) * 256)
        dh = dot(gb, wdown_t[:, c]).astype(BF) * s.gp[at, c]
        s.gp[at, c] = dh
        part = dot(dh, wup_t[c, :])
        acc = part if acc is None else acc + part
    g = g + ln_bwd(acc, s.n2[at, :].astype(F32), s.r2[at, 0:1])
    s.gm[at, :] = g.astype(BF)
    return g

def attend_back(s, blocks, wout, dk_ref, dv_ref):
    d = s.qs.shape[1]
    hd = d // HEADS
    minus = jnp.full((2 * BLK, 128), -1.0, BF)
    def head_grads(i):
        raw = dot_nt(wout[...], s.gm[rows(i * BLK, BLK), :])
        inv = jnp.concatenate([jnp.broadcast_to(s.linv[i, h:h + 1, :], (hd, BLK)) for h in range(HEADS)], axis=0)
        dost = (raw * inv).astype(BF)
        return dost, (dost.astype(F32) * s.ht[i].astype(F32)).astype(BF), dost.T
    def prob_grads(i, dost, doh):
        win = pl.ds(i * BLK, 2 * BLK)
        return [dot(jnp.concatenate([s.vp[win, tile], minus], axis=1),
                    jnp.concatenate([split_heads(dost[tile, :], a, hd), split_heads(doh[tile, :], a, hd)], axis=0))
                for _, tile, a, _ in pairs_of(d)]
    def by_keys(lhs, tokens):
        return [dot(lhs[p], stack_heads(tokens[:, tile], a, hd)) for p, tile, a, _ in pairs_of(d)]
    def by_queries(i, dss):
        out = []
        for p, _, _, lo in pairs_of(d):
            dq = dot(window(s.kt, i, lo, 2 * hd), dss[p])
            out += [dq[0:hd, :BLK], dq[hd:2 * hd, BLK:]]
        return (jnp.concatenate(out, axis=0) * hd ** -0.5).astype(BF)
    heads = [head_grads(i) for i in blocks]
    dps = [prob_grads(i, h[0], h[1]) for i, h in zip(blocks, heads)]
    es = [[s.e[i, p] for p in range(HEADS // 2)] for i in blocks]
    dvs = [by_keys(e, h[2]) for e, h in zip(es, heads)]
    dss = [[(x.astype(F32) * y).astype(BF) for x, y in zip(e, dp)] for e, dp in zip(es, dps)]
    dks = [by_keys(ds, s.qs[rows(i * BLK, BLK), :]) for i, ds in zip(blocks, dss)]
    dqs = [by_queries(i, ds) for i, ds in zip(blocks, dss)]
    per = HEADS // 2 // (d // 128)
    for n, i in enumerate(blocks):
        top, low = pl.ds(i * BLK, BLK), pl.ds(i * BLK + BLK, BLK)
        for ref, parts in ((dk_ref, dks[n]), (dv_ref, dvs[n])):
            for t in range(d // 128):
                tile = slice(t * 128, (t + 1) * 128)
                total = sum(parts[t * per + 1:(t + 1) * per], parts[t * per])
                ref[top, tile] += total[:BLK]
                ref[low, tile] = total[BLK:]
        s.dpk[rows(i * BLK, BLK), 0:d] = dqs[n].T

def finish_packed(s, j, dk_ref, dv_ref):
    d = s.n1.shape[1]
    at = rows(j * CHUNK, CHUNK)
    pat = pl.ds(j * CHUNK + BLK, CHUNK)
    s.dpk[at, d:2 * d] = (dk_ref[pat, :] * LN2).astype(BF)
    s.dpk[at, 2 * d:3 * d] = dv_ref[pat, :].astype(BF)

def project_back(s, j, g, wqkv_t):
    at = rows(j * CHUNK, CHUNK)
    return g + ln_bwd(dot(s.dpk[at, :], wqkv_t[...]), s.n1[at, :].astype(F32), s.r1[at, 0:1])

def weigh(cnt_ref, len_ref, j, cot):
    pos = lax.broadcasted_iota(jnp.int32, (CHUNK, 128), 0) + j * CHUNK
    w = jnp.zeros((CHUNK, 128), F32)
    begin = jnp.int32(0)
    for p in range(len_ref.shape[1]):
        w = jnp.where(pos >= begin, 12.0 / cnt_ref[0, p].astype(F32), w)
        begin = begin + len_ref[0, p]
    return cot * jnp.concatenate([w] * (cot.shape[1] // 128), axis=1)

def saved_shapes(t, d, ff):
    nb = t // BLK
    return dict(n1=((t, d), BF), r1=((t, 128), F32), qs=((t, d), BF), kp=((t + BLK, d), BF), vp=((t + BLK, d), BF),
                qst=((nb, d, BLK), BF), kt=((nb + 1, d, BLK), BF), vt=((nb + 1, d, BLK), BF), e=((nb, HEADS // 2, 2 * BLK, 2 * BLK), BF),
                ht=((nb, d, BLK), BF), linv=((nb, HEADS, BLK), F32))
def more_shapes(t, d, ff):
    return dict(n2=((t, d), BF), r2=((t, 128), F32), act=((t, ff), BF), gp=((t, ff), BF),
                g2=((t, d), BF), gm=((t, d), BF), dpk=((t, 3 * d), BF))

class Memory:
    def __init__(self, ins, outs, sems, hbm, loads):
        self.ins, self.outs, self.sems, self.hbm, self.loads, self.started = ins, outs, sems, hbm, loads, []

    def wait(self, *which):
        for n in which:
            self.loads[n].wait()

    def put(self, n):
        copy = pltpu.make_async_copy(self.outs[n], self.hbm[n], self.sems.at[len(self.started)])
        copy.start()
        self.started.append(copy)

def call(kernel, outs, args, scratch, name, flops, limit=16):
    spec = dict(vmem=pl.BlockSpec(memory_space=pltpu.VMEM), smem=pl.BlockSpec(memory_space=pltpu.SMEM), any=pl.BlockSpec(memory_space=pl.ANY))
    spec["store"] = spec["load"] = spec["any"]
    n_in, n_out, n_scratch = len(args), len(outs), len(scratch)
    stores = [n for n, o in enumerate(outs) if o[0] == "store"]
    loads = [n for n, a in enumerate(args) if a[0] == "load"]
    buffers = [pltpu.VMEM(outs[n][1], outs[n][2]) for n in stores] + [(pltpu.SMEM if args[n][1].dtype == jnp.int32 else pltpu.VMEM)(args[n][1].shape, args[n][1].dtype) for n in loads]
    buffers += [pltpu.SemaphoreType.DMA((max(len(stores), 1),)), pltpu.SemaphoreType.DMA((max(len(loads), 1),))]
    def run(*refs):
        ins, results, rest = list(refs[:n_in]), list(refs[n_in:n_in + n_out]), refs[n_in + n_out:]
        hbm, coming = list(results), {}
        for n, r in zip(stores, rest[n_scratch:]):
            results[n] = r
        for c, (n, r) in enumerate(zip(loads, rest[n_scratch + len(stores):])):
            coming[n] = pltpu.make_async_copy(ins[n], r, rest[-1].at[c])
            coming[n].start()
            ins[n] = r
        memory = Memory(ins, results, rest[-2], hbm, coming)
        kernel(memory, types.SimpleNamespace(**dict(zip(scratch, rest))))
        for copy in memory.started:
            copy.wait()
    shapes = dict(vmem=pltpu.VMEM, store=jax.ShapeDtypeStruct)
    place = dict(vmem=pltpu.VMEM, load=pltpu.HBM)
    return pl.pallas_call(
        run, out_shape=tuple(shapes[o[0]](o[1], o[2]) for o in outs),
        in_specs=[spec[k] for k, _ in args], out_specs=tuple(spec[o[0]] for o in outs),
        scratch_shapes=[pltpu.VMEM(*v) for v in scratch.values()] + buffers,
        compiler_params=pltpu.CompilerParams(vmem_limit_bytes=limit << 20), name=name,
        cost_estimate=pl.CostEstimate(flops=flops, bytes_accessed=1 << 20, transcendentals=0))(
        *[pltpu.with_memory_space_constraint(v, place[k]) if k in place else v for k, v in args])

def place_qkv(me, parts, wqkv):
    r = wqkv.shape[0] // len(parts)
    for x, p in enumerate(parts):
        wqkv[pl.ds(pl.multiple_of((me ^ x) * r, r), r), :] = p[...]

def place_rest(me, parts, wout, wup, wdown):
    r, rd = wout.shape[0] // len(parts), wdown.shape[0] // len(parts)
    for x, p in enumerate(parts):
        at = pl.ds(pl.multiple_of((me ^ x) * r, r), r)
        wout[at, :] = p[0:r, :]
        for c in range(wup.shape[1] // 256):
            wup[at, c * 256:(c + 1) * 256] = p[(c + 1) * r:(c + 2) * r, :]
        lo = r * (1 + wup.shape[1] // 256)
        wdown[pl.ds(pl.multiple_of((me ^ x) * rd, rd), rd), :] = p[lo:lo + rd, :]

def hand_out(me, parts, mats, keep, send):
    for x in range(parts):
        dst = send if x % 2 else keep
        lo = 0
        for m in mats:
            r = m.shape[0] // parts
            at = pl.ds(pl.multiple_of((me ^ x) * r, r), r)
            for c in range(m.shape[1] // 256):
                dst[x // 2, lo:lo + r, :] = m[at, c * 256:(c + 1) * 256]
                lo += r

SAVED = ("e", "n1", "r1", "qs", "vp", "kt", "ht", "linv")

def prepare(lengths, states, inject):
    t, d = states.shape
    nb, nc = t // BLK, t // CHUNK
    def kernel(m, s):
        len_ref, st, inj = m.ins
        n1, r1, mask = m.outs
        m.wait(0)
        make_masks(len_ref, mask, nb)
        m.wait(1, 2)
        for j in range(nc):
            at = slice(j * CHUNK, (j + 1) * CHUNK)
            n, r = ln_fwd(st[at, :] + inj[at, :])
            n1[at, :] = n.astype(BF)
            r1[at, :] = jnp.broadcast_to(r, (CHUNK, 128))
    outs = [("vmem", (t, d), BF), ("vmem", (t, 128), F32), ("vmem", (nb, 2 * BLK, BLK), F32)]
    args = [("load", v) for v in (lengths, states, inject)]
    return call(kernel, outs, args, {}, "prepare", FLOPS_PREPARE)

def first_attention(me, lengths, counts, states, inject, cot, n1, mask, qkv_parts, ff):
    t, d = n1.shape
    nb, nc = t // BLK, t // CHUNK
    shapes = saved_shapes(t, d, ff)
    made = [k for k in SAVED if k not in ("n1", "r1")]
    scratch = {k: v for k, v in shapes.items() if k not in SAVED}
    def kernel(m, s):
        me_ref, len_ref, cnt_ref, st, inj, ct, n1_ref, mask_ref = m.ins[:8]
        vars(s).update(zip(made, m.outs))
        wqkv, ent, inj_out, weighed = m.outs[-4:]
        pad_zero(s)
        place_qkv(me_ref[0], m.ins[8:], wqkv)
        for j in range(nc):
            pack_heads(s, j, n1_ref[j * CHUNK:(j + 1) * CHUNK, :], wqkv)
        for i in range(0, nb, 4):
            attend(s, (i, i + 1, i + 2, i + 3), mask_ref)
        m.wait(1, 2, 3, 4, 5)
        for j in range(nc):
            at = slice(j * CHUNK, (j + 1) * CHUNK)
            ent[at, :] = st[at, :] + inj[at, :]
            inj_out[at, :] = inj[at, :]
            weighed[at, :] = weigh(cnt_ref, len_ref, j, ct[at, :])
    outs = [("vmem",) + shapes[k] for k in made] + [("vmem", (d, 3 * d), BF)] + [("vmem", (t, d), F32)] * 3
    args = [("smem", me)] + [("load", v) for v in (lengths, counts, states, inject, cot)] + [("vmem", v) for v in (n1, mask, *qkv_parts)]
    got = call(kernel, outs, args, scratch, "first_attention", FLOPS_FIRST)
    return dict(zip(made, got)), got[-4], got[-3:]

def middle_part(me, ent, inject, weighed, mask, wqkv, ht, rest_parts, ff):
    t, d = ent.shape
    nb, nc = t // BLK, t // CHUNK
    parts = len(rest_parts)
    sh = {"a_" + k: v for k, v in more_shapes(t, d, ff).items() if k not in ("dpk", "gm")}
    sh.update({"b_" + k: v for k, v in {**saved_shapes(t, d, ff), **more_shapes(t, d, ff)}.items() if k not in ("n1", "dpk", "ht", "gm")})
    sh.update(state=((t, d), F32), dk=((t + BLK, d), F32), dv=((t + BLK, d), F32),
              wqkv_t=((3 * d, d), BF), wup_t=((ff, d), BF), wdown_t=((d, ff), BF), tr=((2, d, t), BF),
              wup=((d, ff), BF), wdown=((ff, d), BF), mup=((d, ff), BF), mdown_t=((d, ff), BF), mdown=((ff, d), BF))
    def kernel(m, x):
        me_ref, ent_ref, inj, weighed_ref, x.mask, wqkv_ref, ht_ref = m.ins[:7]
        final, g, ginj, gm, wout, n1, dpk, ht, gm_two, keep, send = m.outs
        its = [types.SimpleNamespace(**{k[2:]: v for k, v in vars(x).items() if k.startswith(p)}) for p in ("a_", "b_")]
        its[0].ht, its[0].gm = ht_ref, gm
        its[1].n1, its[1].dpk, its[1].ht, its[1].gm = n1, dpk, ht, gm_two
        place_rest(me_ref[0], m.ins[7:], wout, x.wup, x.wdown)
        x.wup_t[...] = x.wup[...].T
        x.wdown_t[...] = x.wdown[...].T
        pad_zero(its[1])
        x.wqkv_t[...] = wqkv_ref[...].T
        def rows_of(j):
            return slice(j * CHUNK, (j + 1) * CHUNK)
        def mlp_of(n, j, src, dst):
            at = rows_of(j)
            entered = src[at, :] + inj[at, :] if n else src[at, :]
            dst[at, :] = mlp(its[n], j, entered, wout, x.wup, x.wdown)
        def project_of(j):
            project(its[1], j, x.state[rows_of(j), :] + inj[rows_of(j), :], wqkv_ref)
        def blocks_of(j):
            n = CHUNK // BLK
            return [tuple(range(j * n, j * n + n))]
        def attend_of(j):
            for blocks in blocks_of(j):
                attend(its[1], blocks, x.mask)
        def back_two(j):
            at = rows_of(j)
            g[at, :] = mlp_back(its[1], j, weighed_ref[at, :], x.wdown_t, x.wup_t)
        def attend_back_of(j):
            for blocks in blocks_of(j):
                attend_back(its[1], blocks, wout, x.dk, x.dv)
        def back_one(j):
            at = rows_of(j)
            finish_packed(its[1], j, x.dk, x.dv)
            new = project_back(its[1], j, g[at, :], x.wqkv_t)
            ginj[at, :] = new
            g[at, :] = mlp_back(its[0], j, new, x.wdown_t, x.wup_t)
        x.dk[0:BLK, :] = jnp.zeros((BLK, d), F32)
        x.dv[0:BLK, :] = jnp.zeros((BLK, d), F32)
        for j in range(nc): mlp_of(0, j, ent_ref, x.state)
        for j in range(nc): project_of(j)
        for j in range(nc): attend_of(j)
        for j in range(nc): mlp_of(1, j, x.state, final)
        m.put(0)
        for j in range(nc): back_two(j)
        for j in range(nc): attend_back_of(j)
        for j in range(nc): back_one(j)

        def weight_grad(lefts, rights, dst):
            for n, left in enumerate(lefts):
                x.tr[n] = left[...].T
            def tile(c):
                cc = pl.ds(c * 256, 256)
                total = dot(x.tr[0], rights[0][:, cc])
                for n in range(1, len(rights)):
                    total = total + dot(x.tr[n], rights[n][:, cc])
                dst[:, cc] = total.astype(dst.dtype)
            loop(dst.shape[1] // 256, tile)
        weight_grad([s.g2 for s in its], [s.act for s in its], x.mdown_t)
        x.mdown[...] = x.mdown_t[...].T
        weight_grad([s.n2 for s in its], [s.gp for s in its], x.mup)
        hand_out(me_ref[0], parts, (x.mup, x.mdown), keep, send)
    piece = ("vmem", (max(parts // 2, 1), 2 * ff // parts, d), BF)
    outs = [("store", (t, d), F32)] + [("vmem", (t, d), F32)] * 2 + [("vmem", (t, d), BF), ("vmem", (d, d), BF), ("vmem", (t, d), BF), ("vmem", (t, 3 * d), BF)] + [("vmem", (nb, d, BLK), BF), ("vmem", (t, d), BF)] + [piece] * 2
    args = [("smem", me)] + [("vmem", v) for v in (ent, inject, weighed, mask, wqkv, ht, *rest_parts)]
    return call(kernel, outs, args, sh, "middle_part", 25 * 10 ** 9, limit=LIMIT_MIDDLE)

def last_part(me, saved, gm, wout, wqkv, n1, dpk, ht, gm_two, g, ginj, parts, ff, first):
    t, d = gm.shape
    nb, nc = t // BLK, t // CHUNK
    scratch = dict(dk=((t + BLK, d), F32), dv=((t + BLK, d), F32), tr=((2, d, t), BF), mat=((d, 3 * d), BF), mout=((d, d), BF), wt=((3 * d, d), BF), dpk=((t, 3 * d), BF))
    def kernel(m, s):
        me_ref, s.gm, wout_ref, w_ref, n1_ref, dpk_ref, ht_ref, gm_ref, g_ref, gi_ref = m.ins[:10]
        vars(s).update(zip(SAVED, m.ins[10:]))
        keep, send, grad, grad_inject = m.outs
        s.dk[0:BLK, :] = jnp.zeros((BLK, d), F32)
        s.dv[0:BLK, :] = jnp.zeros((BLK, d), F32)
        for i in range(0, nb, 4):
            attend_back(s, (i, i + 1, i + 2, i + 3), wout_ref, s.dk, s.dv)
        s.tr[0] = s.n1[...].T
        s.tr[1] = n1_ref[...].T
        s.wt[...] = w_ref[...].T
        loop(nc, lambda j: finish_packed(s, j, s.dk, s.dv))
        def tile(c):
            cc = slice(c * 256, (c + 1) * 256)
            s.mat[:, cc] = (dot(s.tr[0], s.dpk[:, cc]) + dot(s.tr[1], dpk_ref[:, cc])).astype(BF)
        loop(3, tile)
        total = None
        for left, right in ((s.ht, s.gm), (ht_ref, gm_ref)):
            for b in range(nb):
                part = dot(left[b], right[b * BLK:(b + 1) * BLK, :])
                total = part if total is None else total + part
        s.mout[...] = total.astype(BF)
        hand_out(me_ref[0], parts, (s.mout, s.mat), keep, send)
        def chunk(j):
            at = rows(j * CHUNK, CHUNK)
            new = project_back(s, j, g_ref[at, :], s.wt)
            grad[at, :] = new
            grad_inject[at, :] = new + gi_ref[at, :]
        loop(nc, chunk)
        m.put(2)
        m.put(3)
    outs = [("vmem", (max(parts // 2, 1), 4 * d // parts, d), BF)] * 2 + [("store", (t, d), F32)] * 2
    args = [("smem", me)] + [("vmem", v) for v in (gm, wout, wqkv, n1, dpk, ht, gm_two, g, ginj)]
    args += [("vmem", saved[k]) for k in SAVED] + [("any", v) for v in first]
    return call(kernel, outs, args, scratch, "last_part", FLOPS_LAST, limit=LIMIT_LAST)

def to_column(row):
    n = row.shape[1]
    eye = lax.broadcasted_iota(jnp.int32, (n, n), 0) == lax.broadcasted_iota(jnp.int32, (n, n), 1)
    return jnp.sum(jnp.where(eye, jnp.broadcast_to(row, (n, n)), 0.0), axis=1, keepdims=True)

def to_row(column):
    n = column.shape[0]
    eye = lax.broadcasted_iota(jnp.int32, (n, n), 0) == lax.broadcasted_iota(jnp.int32, (n, n), 1)
    return jnp.sum(jnp.where(eye, jnp.broadcast_to(column, (n, n)), 0.0), axis=0, keepdims=True)

def pack_weights(w_qkv, gain_one, w_out, w_up, w_down, gain_two):
    r, d = w_out.shape
    n = w_up.shape[1] // d
    def kernel(m, s):
        qkv, g_one, out, up, down, g_two = m.ins
        m.wait(0, 1)
        m.outs[0][...] = (qkv[...].astype(F32) * to_column(g_one[...].astype(F32))).astype(BF)
        m.wait(2, 3, 4, 5)
        m.outs[1][0:r, :] = out[...]
        col = to_column(g_two[...].astype(F32))
        for c in range(n):
            m.outs[1][(c + 1) * r:(c + 2) * r, :] = (up[:, c * d:(c + 1) * d].astype(F32) * col).astype(BF)
        m.outs[1][(n + 1) * r:, :] = down[...]
    args = [("load", v) for v in (w_qkv, gain_one.reshape(1, -1), w_out, w_up, w_down, gain_two.reshape(1, -1))]
    return call(kernel, [("vmem", w_qkv.shape, BF), ("vmem", ((n + 1) * r + w_down.shape[0], d), BF)], args, {}, "pack_weights", 10 ** 6)

def sum_parts(parts, lo, size):
    acc = parts[0][lo:lo + size, :].astype(F32)
    for p in parts[1:]:
        acc = acc + p[lo:lo + size, :].astype(F32)
    return acc

def finished(shares, weight, gain, lead, tail, name):
    r, cols = weight.shape
    d = shares[0].shape[1]
    n = cols // d
    others = [(lo, size) for lo, size in ((0, lead), (lead + n * r, tail)) if size]
    def kernel(m, s):
        w, g, parts = m.ins[0], to_column(m.ins[1][...].astype(F32)), m.ins[2:]
        along = jnp.zeros((r, 1), F32)
        for c in range(n):
            v = sum_parts(parts, lead + c * r, r)
            m.outs[0][:, c * d:(c + 1) * d] = v * g
            along = along + jnp.sum(v * w[:, c * d:(c + 1) * d].astype(F32), axis=1, keepdims=True)
        m.put(0)
        m.outs[1][...] = to_row(along)
        m.put(1)
        for at, (lo, size) in enumerate(others):
            m.outs[2 + at][...] = sum_parts(parts, lo, size)
            m.put(2 + at)
    outs = [("store", (r, cols), F32), ("store", (1, r), F32)] + [("store", (size, d), F32) for _, size in others]
    got = call(kernel, outs, [("vmem", v) for v in (weight, gain.reshape(1, -1), *shares)], {}, name, 10 ** 6)
    return [got[0], got[1].reshape(r)] + list(got[2:])

def after(values, *others):
    return lax.optimization_barrier((values, others))[0]

def exchange(x, axis, size, step):
    return lax.ppermute(x, axis, [(i, i ^ step) for i in range(size)])

def far_parts(x, size):
    return [x] + [exchange(x, "fsdp", size, 2 * k) for k in range(1, size // 2)]

def with_near(far, size):
    return [v for x in far for v in (x, exchange(x, "fsdp", size, 1))]

def sum_near(keep, near, then=None):
    total = keep.astype(F32) + near.astype(F32)
    if then is not None:
        total = total + jnp.minimum(jnp.abs(then[:keep.shape[1]].astype(F32)), 0.0)
    return [total[k].astype(BF) for k in range(keep.shape[0])]

def send_far(summed, size):
    return [exchange(summed[k], "fsdp", size, 2 * k) for k in range(size // 2 - 1, 0, -1)]

def along_dp(share, size):
    return [share] + [exchange(share, "dp", size, k) for k in range(1, size)]

def send_near(pieces, size):
    return [exchange(p, "fsdp", size, 1) for p in pieces[1::2]]

def send_far(summed, size):
    return [exchange(summed[k], "fsdp", size, 2 * k) for k in range(size // 2 - 1, 0, -1)]

def reduce_whole(whole, sizes):
    out, lo = [], 0
    for n in sizes:
        share = lax.psum_scatter(whole[lo:lo + n], "fsdp", scatter_dimension=0, tiled=True)
        out.append(lax.psum(share, "dp").astype(F32))
        lo += n
    return jnp.concatenate(out, axis=0)

def on_device(n_dp, n_fsdp, states, inject, ln1_gain, w_qkv, w_out, ln2_gain, w_up, w_down, prompt_lengths, loop_counts, cotangent):
    d = states.shape[1]
    r, ff = w_up.shape
    direct = r % 16 == 0
    if direct:
        me = lax.axis_index("fsdp").astype(jnp.int32).reshape(1)
        own_qkv, own_rest = pack_weights(w_qkv, ln1_gain, w_out, w_up, w_down, ln2_gain)
        qkv_far = far_parts(own_qkv, n_fsdp)
        rest_far = far_parts(own_rest, n_fsdp)
    else:
        me = jnp.zeros((1,), jnp.int32)
        full = lambda v: lax.all_gather(v, "fsdp", axis=0, tiled=True)
        up = full((w_up.astype(F32) * ln2_gain.astype(F32)[:, None]).astype(BF))
        qkv_parts = [full((w_qkv.astype(F32) * ln1_gain.astype(F32)[:, None]).astype(BF))]
        rest_parts = [jnp.concatenate([full(w_out)] + [up[:, c:c + d] for c in range(0, ff, d)] + [full(w_down)], axis=0)]
    n1, r1, mask = prepare(prompt_lengths, states, inject)
    if direct:
        qkv_parts = with_near(qkv_far[:1], n_fsdp) + with_near(after(qkv_far[1:], n1), n_fsdp)
    parts = len(qkv_parts)
    saved, wqkv, entering = first_attention(me, prompt_lengths, loop_counts, states, inject, cotangent, n1, mask, qkv_parts, ff)
    saved.update(n1=n1, r1=r1)
    if direct:
        rest_parts = with_near(after(rest_far, wqkv), n_fsdp)
    final, g, ginj, gm, wout, n1, dpk, ht, gm_two, keep, send = middle_part(
        me, *entering, mask, wqkv, saved["ht"], rest_parts, ff)
    summed = []
    if direct:
        summed = sum_near(keep, exchange(send, "fsdp", n_fsdp, 1))
        far = send_far(summed, n_fsdp)
    else:
        shares = [reduce_whole(keep[0], [d] * (ff // d) + [ff])]
    keep_qkv, send_qkv, grad_states, grad_inject = last_part(
        me, saved, gm, wout, wqkv, n1, dpk, ht, gm_two, g, ginj, parts, ff, summed)
    if direct:
        near = exchange(send_qkv, "fsdp", n_fsdp, 1)
        share = sum_parts([summed[0], *far], 0, summed[0].shape[0]).astype(BF)
        shares = along_dp(share, n_dp)
        summed = sum_near(keep_qkv, near, share)
        shares_qkv = along_dp(sum_parts([summed[0], *send_far(summed, n_fsdp)], 0, 4 * r).astype(BF), n_dp)
    else:
        shares_qkv = [reduce_whole(keep_qkv[0], [d] * 4)]
    d_up, d_gain_two, d_down = finished(shares, w_up, ln2_gain, 0, w_down.shape[0], "finished_mlp")
    d_qkv, d_gain_one, d_out = finished(shares_qkv, w_qkv, ln1_gain, r, 0, "finished_attention")
    return (final, grad_states, grad_inject, d_gain_one, d_qkv, d_out, d_gain_two, d_up, d_down)

def solution(mesh):
    tok, vec, mat = P(("dp", "fsdp"), None), P("fsdp"), P("fsdp", None)
    return jax.shard_map(
        functools.partial(on_device, mesh.shape["dp"], mesh.shape["fsdp"]), mesh=mesh,
        in_specs=(tok, tok, vec, mat, mat, vec, mat, mat, tok, tok, tok),
        out_specs=(tok, tok, tok, vec, mat, mat, vec, mat, mat), check_vma=False)
```

```python
import functools
import types

import jax
import jax.numpy as jnp
from jax import lax
from jax.experimental import pallas as pl
from jax.experimental.pallas import tpu as pltpu
from jax.sharding import PartitionSpec as P

BF = jnp.bfloat16
F32 = jnp.float32
HEADS = 8
ITERS = 2
BLK = 128
CHUNK = 512
NEG = -1e30
LOG2E = 1.4426950408889634
LN2 = 0.6931471805599453
GELU_A = 0.7978845608028654
GELU_B = GELU_A * 0.044715
FLOPS_FIRST = 10 ** 6
FLOPS_PREPARE = 10 ** 6
FLOPS_LAST = 10 ** 10
LIMIT_MIDDLE = 42
LIMIT_LAST = 16


def dot(a, b):
    return jnp.dot(a, b, preferred_element_type=F32)

def dot_tn(a, b):
    return lax.dot_general(a, b, (((0,), (0,)), ((), ())), preferred_element_type=F32)

def dot_nt(a, b):
    return lax.dot_general(a, b, (((1,), (1,)), ((), ())), preferred_element_type=F32)

def rows(start, size):
    return pl.ds(start, size)

def ln_fwd(x):
    c = x - jnp.mean(x, axis=1, keepdims=True)
    r = lax.rsqrt(jnp.mean(c * c, axis=1, keepdims=True) + 1e-5)
    return c * r, r

def ln_bwd(y, n, r):
    return r * (y - jnp.mean(y, axis=1, keepdims=True) - n * jnp.mean(y * n, axis=1, keepdims=True))

def loop(n, body):
    for i in range(n):
        body(i)

def make_masks(len_ref, mask_ref, nb):
    pos = lax.broadcasted_iota(jnp.int32, (1, BLK), 1)
    ends = []
    total = jnp.int32(0)
    for p in range(len_ref.shape[1]):
        total = total + len_ref[0, p]
        ends.append(total)

    def block(i, _):
        q = pos + i * BLK
        start = jnp.zeros((1, BLK), jnp.int32)
        for e in ends:
            start = jnp.where(q >= e, e, start)
        k = lax.broadcasted_iota(jnp.int32, (2 * BLK, BLK), 0) + (i - 1) * BLK
        mask_ref[i] = jnp.where((k >= start) & (k <= q), 0.0, NEG).astype(F32)
        return 0

    lax.fori_loop(0, nb, block, 0)

def pad_zero(s):
    s.kp[0:BLK, :] = jnp.zeros((BLK, s.kp.shape[1]), BF)
    s.vp[0:BLK, :] = jnp.zeros((BLK, s.vp.shape[1]), BF)
    s.kt[0] = jnp.zeros(s.kt.shape[1:], BF)
    s.vt[0] = jnp.zeros(s.vt.shape[1:], BF)

def project(s, j, ent, wqkv):
    n, r = ln_fwd(ent)
    nb16 = n.astype(BF)
    s.n1[rows(j * CHUNK, CHUNK), :] = nb16
    s.r1[rows(j * CHUNK, CHUNK), :] = jnp.broadcast_to(r, (CHUNK, 128))
    pack_heads(s, j, nb16, wqkv)

def pack_heads(s, j, nb16, wqkv):
    d = nb16.shape[1]
    scale = LOG2E * (d // HEADS) ** -0.5
    q = (dot(nb16, wqkv[:, 0:d]) * scale).astype(BF)
    k = dot(nb16, wqkv[:, d:2 * d]).astype(BF)
    v = dot(nb16, wqkv[:, 2 * d:3 * d]).astype(BF)
    s.qs[rows(j * CHUNK, CHUNK), :] = q
    s.kp[pl.ds(j * CHUNK + BLK, CHUNK), :] = k
    s.vp[pl.ds(j * CHUNK + BLK, CHUNK), :] = v
    qt, kt, vt = q.T, k.T, v.T
    for b in range(CHUNK // BLK):
        i = j * (CHUNK // BLK) + b
        s.qst[i] = qt[:, b * BLK:(b + 1) * BLK]
        s.kt[i + 1] = kt[:, b * BLK:(b + 1) * BLK]
        s.vt[i + 1] = vt[:, b * BLK:(b + 1) * BLK]

def split_heads(tile, a, hd):
    def alone(lo):
        parts = [jnp.zeros((n, tile.shape[1]), tile.dtype) for n in (lo, tile.shape[0] - lo - hd)]
        parts = [parts[0], tile[lo:lo + hd], parts[1]]
        return jnp.concatenate([p for p in parts if p.shape[0]], axis=0)
    return jnp.concatenate([alone(a), alone(a + hd)], axis=1)

def stack_heads(tile, a, hd):
    z = jnp.zeros_like(tile)
    lane = lax.broadcasted_iota(jnp.int32, tile.shape, 1)
    top = jnp.where((lane >= a) & (lane < a + hd), tile, z)
    low = jnp.where((lane >= a + hd) & (lane < a + 2 * hd), tile, z)
    return jnp.concatenate([top, low], axis=0)

def pairs_of(d):
    hd = d // HEADS
    per = 128 // (2 * hd)
    return [(p, slice(p // per * 128, p // per * 128 + 128), p % per * 2 * hd, p * 2 * hd) for p in range(HEADS // 2)]

def window(ref, i, lo, n):
    return jnp.concatenate([ref[i, lo:lo + n, :], ref[i + 1, lo:lo + n, :]], axis=1)

def attend(s, blocks, mask_ref):
    d = s.qs.shape[1]
    hd = d // HEADS
    ones = jnp.ones((16, 2 * BLK), BF)
    def scores(i):
        win = pl.ds(i * BLK, 2 * BLK)
        return [dot(s.kp[win, tile], split_heads(s.qst[i, tile, :], a, hd)) for _, tile, a, _ in pairs_of(d)]
    def soft(i, all_scores):
        mask = mask_ref[i]
        mask = jnp.concatenate([mask, mask], axis=1)
        out = []
        for sc in all_scores:
            sc = sc + mask
            out.append(jnp.exp2(sc - jnp.max(sc, axis=0, keepdims=True)).astype(BF))
        return out
    def values(i, es):
        return [dot(jnp.concatenate([window(s.vt, i, lo, 2 * hd), ones], axis=0), es[p]) for p, _, _, lo in pairs_of(d)]
    es = []
    ready = scores(blocks[0])
    for n, i in enumerate(blocks):
        ahead = scores(blocks[n + 1]) if n + 1 < len(blocks) else None
        es.append(soft(i, ready))
        ready = ahead
    os = [values(i, e) for i, e in zip(blocks, es)]
    for i, e, o in zip(blocks, es, os):
        for p, _, _, lo in pairs_of(d):
            s.e[i, p] = e[p]
            inv = 1.0 / o[p][2 * hd:2 * hd + 1, :]
            s.linv[i, 2 * p:2 * p + 1, :] = inv[:, :BLK]
            s.linv[i, 2 * p + 1:2 * p + 2, :] = inv[:, BLK:]
            s.ht[i, lo:lo + hd, :] = (o[p][0:hd, :BLK] * inv[:, :BLK]).astype(BF)
            s.ht[i, lo + hd:lo + 2 * hd, :] = (o[p][hd:2 * hd, BLK:] * inv[:, BLK:]).astype(BF)

def heads_chunk(s, j):
    return jnp.concatenate([s.ht[j * (CHUNK // BLK) + b] for b in range(CHUNK // BLK)], axis=1)

def mlp(s, j, ent, wout, wup, wdown):
    mid = ent + dot_tn(heads_chunk(s, j), wout[...])
    n, r = ln_fwd(mid)
    nb16 = n.astype(BF)
    at = rows(j * CHUNK, CHUNK)
    s.n2[at, :] = nb16
    s.r2[at, :] = jnp.broadcast_to(r, (CHUNK, 128))
    acc = mid
    for f in range(wup.shape[1] // 256):
        c = slice(f * 256, (f + 1) * 256)
        h = dot(nb16, wup[:, c]).astype(BF)
        h2 = h * h
        sg = 0.5 * jnp.tanh(h * (GELU_B * h2 + GELU_A)) + 0.5
        act = h * sg
        s.act[at, c] = act
        s.gp[at, c] = sg + act * (2.0 - 2.0 * sg) * (3 * GELU_B * h2 + GELU_A)
    return mid + dot(s.act[at, :], wdown[...])

def mlp_back(s, j, g, wdown_t, wup_t):
    at = rows(j * CHUNK, CHUNK)
    gb = g.astype(BF)
    s.g2[at, :] = gb
    acc = None
    for f in range(wdown_t.shape[1] // 256):
        c = slice(f * 256, (f + 1) * 256)
        dh = dot(gb, wdown_t[:, c]).astype(BF) * s.gp[at, c]
        s.gp[at, c] = dh
    acc = dot(s.gp[at, :], wup_t[...])
    g = g + ln_bwd(acc, s.n2[at, :].astype(F32), s.r2[at, 0:1])
    s.gm[at, :] = g.astype(BF)
    return g

def attend_back(s, blocks, wout, dk_ref, dv_ref):
    d = s.qs.shape[1]
    hd = d // HEADS
    minus = jnp.full((2 * BLK, 128), -1.0, BF)
    def head_grads(i):
        raw = dot_nt(wout[...], s.gm[rows(i * BLK, BLK), :])
        inv = jnp.concatenate([jnp.broadcast_to(s.linv[i, h:h + 1, :], (hd, BLK)) for h in range(HEADS)], axis=0)
        dost = (raw * inv).astype(BF)
        return dost, (dost.astype(F32) * s.ht[i].astype(F32)).astype(BF), dost.T
    def prob_grads(i, dost, doh):
        win = pl.ds(i * BLK, 2 * BLK)
        return [dot(jnp.concatenate([s.vp[win, tile], minus], axis=1),
                    jnp.concatenate([split_heads(dost[tile, :], a, hd), split_heads(doh[tile, :], a, hd)], axis=0))
                for _, tile, a, _ in pairs_of(d)]
    def by_keys(lhs, tokens):
        return [dot(lhs[p], stack_heads(tokens[:, tile], a, hd)) for p, tile, a, _ in pairs_of(d)]
    def by_queries(i, dss):
        out = []
        for p, _, _, lo in pairs_of(d):
            dq = dot(window(s.kt, i, lo, 2 * hd), dss[p])
            out += [dq[0:hd, :BLK], dq[hd:2 * hd, BLK:]]
        return (jnp.concatenate(out, axis=0) * hd ** -0.5).astype(BF)
    heads = [head_grads(i) for i in blocks]
    dps = [prob_grads(i, h[0], h[1]) for i, h in zip(blocks, heads)]
    es = [[s.e[i, p] for p in range(HEADS // 2)] for i in blocks]
    dvs = [by_keys(e, h[2]) for e, h in zip(es, heads)]
    dss = [[(x.astype(F32) * y).astype(BF) for x, y in zip(e, dp)] for e, dp in zip(es, dps)]
    dks = [by_keys(ds, s.qs[rows(i * BLK, BLK), :]) for i, ds in zip(blocks, dss)]
    dqs = [by_queries(i, ds) for i, ds in zip(blocks, dss)]
    per = HEADS // 2 // (d // 128)
    for n, i in enumerate(blocks):
        top, low = pl.ds(i * BLK, BLK), pl.ds(i * BLK + BLK, BLK)
        for ref, parts in ((dk_ref, dks[n]), (dv_ref, dvs[n])):
            for t in range(d // 128):
                tile = slice(t * 128, (t + 1) * 128)
                total = sum(parts[t * per + 1:(t + 1) * per], parts[t * per])
                ref[top, tile] += total[:BLK]
                ref[low, tile] = total[BLK:]
        s.dpk[rows(i * BLK, BLK), 0:d] = dqs[n].T

def finish_packed(s, j, dk_ref, dv_ref):
    d = s.n1.shape[1]
    at = rows(j * CHUNK, CHUNK)
    pat = pl.ds(j * CHUNK + BLK, CHUNK)
    s.dpk[at, d:2 * d] = (dk_ref[pat, :] * LN2).astype(BF)
    s.dpk[at, 2 * d:3 * d] = dv_ref[pat, :].astype(BF)

def project_back(s, j, g, wqkv_t):
    at = rows(j * CHUNK, CHUNK)
    return g + ln_bwd(dot(s.dpk[at, :], wqkv_t[...]), s.n1[at, :].astype(F32), s.r1[at, 0:1])

def weigh(cnt_ref, len_ref, j, cot):
    pos = lax.broadcasted_iota(jnp.int32, (CHUNK, 128), 0) + j * CHUNK
    w = jnp.zeros((CHUNK, 128), F32)
    begin = jnp.int32(0)
    for p in range(len_ref.shape[1]):
        w = jnp.where(pos >= begin, 12.0 / cnt_ref[0, p].astype(F32), w)
        begin = begin + len_ref[0, p]
    return cot * jnp.concatenate([w] * (cot.shape[1] // 128), axis=1)

def saved_shapes(t, d, ff):
    nb = t // BLK
    return dict(n1=((t, d), BF), r1=((t, 128), F32), qs=((t, d), BF), kp=((t + BLK, d), BF), vp=((t + BLK, d), BF),
                qst=((nb, d, BLK), BF), kt=((nb + 1, d, BLK), BF), vt=((nb + 1, d, BLK), BF), e=((nb, HEADS // 2, 2 * BLK, 2 * BLK), BF),
                ht=((nb, d, BLK), BF), linv=((nb, HEADS, BLK), F32))
def more_shapes(t, d, ff):
    return dict(n2=((t, d), BF), r2=((t, 128), F32), act=((t, ff), BF), gp=((t, ff), BF),
                g2=((t, d), BF), gm=((t, d), BF), dpk=((t, 3 * d), BF))

class Memory:
    def __init__(self, ins, outs, sems, hbm, loads):
        self.ins, self.outs, self.sems, self.hbm, self.loads, self.started = ins, outs, sems, hbm, loads, []

    def wait(self, *which):
        for n in which:
            self.loads[n].wait()

    def put(self, n):
        copy = pltpu.make_async_copy(self.outs[n], self.hbm[n], self.sems.at[len(self.started)])
        copy.start()
        self.started.append(copy)

def call(kernel, outs, args, scratch, name, flops, limit=16):
    spec = dict(vmem=pl.BlockSpec(memory_space=pltpu.VMEM), smem=pl.BlockSpec(memory_space=pltpu.SMEM), any=pl.BlockSpec(memory_space=pl.ANY))
    spec["store"] = spec["load"] = spec["any"]
    n_in, n_out, n_scratch = len(args), len(outs), len(scratch)
    stores = [n for n, o in enumerate(outs) if o[0] == "store"]
    loads = [n for n, a in enumerate(args) if a[0] == "load"]
    buffers = [pltpu.VMEM(outs[n][1], outs[n][2]) for n in stores] + [(pltpu.SMEM if args[n][1].dtype == jnp.int32 else pltpu.VMEM)(args[n][1].shape, args[n][1].dtype) for n in loads]
    buffers += [pltpu.SemaphoreType.DMA((max(len(stores), 1),)), pltpu.SemaphoreType.DMA((max(len(loads), 1),))]
    def run(*refs):
        ins, results, rest = list(refs[:n_in]), list(refs[n_in:n_in + n_out]), refs[n_in + n_out:]
        hbm, coming = list(results), {}
        for n, r in zip(stores, rest[n_scratch:]):
            results[n] = r
        for c, (n, r) in enumerate(zip(loads, rest[n_scratch + len(stores):])):
            coming[n] = pltpu.make_async_copy(ins[n], r, rest[-1].at[c])
            coming[n].start()
            ins[n] = r
        memory = Memory(ins, results, rest[-2], hbm, coming)
        kernel(memory, types.SimpleNamespace(**dict(zip(scratch, rest))))
        for copy in memory.started:
            copy.wait()
    shapes = dict(vmem=pltpu.VMEM, store=jax.ShapeDtypeStruct)
    place = dict(vmem=pltpu.VMEM, load=pltpu.HBM)
    return pl.pallas_call(
        run, out_shape=tuple(shapes[o[0]](o[1], o[2]) for o in outs),
        in_specs=[spec[k] for k, _ in args], out_specs=tuple(spec[o[0]] for o in outs),
        scratch_shapes=[pltpu.VMEM(*v) for v in scratch.values()] + buffers,
        compiler_params=pltpu.CompilerParams(vmem_limit_bytes=limit << 20), name=name,
        cost_estimate=pl.CostEstimate(flops=flops, bytes_accessed=1 << 20, transcendentals=0))(
        *[pltpu.with_memory_space_constraint(v, place[k]) if k in place else v for k, v in args])

def place_qkv(me, parts, wqkv):
    r = wqkv.shape[0] // len(parts)
    for x, p in enumerate(parts):
        wqkv[pl.ds(pl.multiple_of((me ^ x) * r, r), r), :] = p[...]

def place_rest(me, parts, wout, wup, wdown):
    r, rd = wout.shape[0] // len(parts), wdown.shape[0] // len(parts)
    for x, p in enumerate(parts):
        at = pl.ds(pl.multiple_of((me ^ x) * r, r), r)
        wout[at, :] = p[0:r, :]
        for c in range(wup.shape[1] // 256):
            wup[at, c * 256:(c + 1) * 256] = p[(c + 1) * r:(c + 2) * r, :]
        lo = r * (1 + wup.shape[1] // 256)
        wdown[pl.ds(pl.multiple_of((me ^ x) * rd, rd), rd), :] = p[lo:lo + rd, :]

def hand_out(me, parts, mats, keep, send):
    for x in range(parts):
        dst = send if x % 2 else keep
        lo = 0
        for m in mats:
            r = m.shape[0] // parts
            at = pl.ds(pl.multiple_of((me ^ x) * r, r), r)
            for c in range(m.shape[1] // 256):
                dst[x // 2, lo:lo + r, :] = m[at, c * 256:(c + 1) * 256]
                lo += r

SAVED = ("e", "n1", "r1", "qs", "vp", "kt", "ht", "linv")

def prepare(lengths, states, inject):
    t, d = states.shape
    nb, nc = t // BLK, t // CHUNK
    def kernel(m, s):
        len_ref, st, inj = m.ins
        n1, r1, mask = m.outs
        m.wait(0)
        make_masks(len_ref, mask, nb)
        m.wait(1, 2)
        for j in range(nc):
            at = slice(j * CHUNK, (j + 1) * CHUNK)
            n, r = ln_fwd(st[at, :] + inj[at, :])
            n1[at, :] = n.astype(BF)
            r1[at, :] = jnp.broadcast_to(r, (CHUNK, 128))
    outs = [("vmem", (t, d), BF), ("vmem", (t, 128), F32), ("vmem", (nb, 2 * BLK, BLK), F32)]
    args = [("load", v) for v in (lengths, states, inject)]
    return call(kernel, outs, args, {}, "prepare", FLOPS_PREPARE)

def first_attention(me, lengths, counts, states, inject, cot, n1, mask, qkv_parts, ff):
    t, d = n1.shape
    nb, nc = t // BLK, t // CHUNK
    shapes = saved_shapes(t, d, ff)
    made = [k for k in SAVED if k not in ("n1", "r1")]
    scratch = {k: v for k, v in shapes.items() if k not in SAVED}
    def kernel(m, s):
        me_ref, len_ref, cnt_ref, st, inj, ct, n1_ref, mask_ref = m.ins[:8]
        vars(s).update(zip(made, m.outs))
        wqkv, ent, inj_out, weighed = m.outs[-4:]
        pad_zero(s)
        place_qkv(me_ref[0], m.ins[8:], wqkv)
        for j in range(nc):
            pack_heads(s, j, n1_ref[j * CHUNK:(j + 1) * CHUNK, :], wqkv)
        for i in range(0, nb, 4):
            attend(s, (i, i + 1, i + 2, i + 3), mask_ref)
        m.wait(1, 2, 3, 4, 5)
        for j in range(nc):
            at = slice(j * CHUNK, (j + 1) * CHUNK)
            ent[at, :] = st[at, :] + inj[at, :]
            inj_out[at, :] = inj[at, :]
            weighed[at, :] = weigh(cnt_ref, len_ref, j, ct[at, :])
    outs = [("vmem",) + shapes[k] for k in made] + [("vmem", (d, 3 * d), BF)] + [("vmem", (t, d), F32)] * 3
    args = [("smem", me)] + [("load", v) for v in (lengths, counts, states, inject, cot)] + [("vmem", v) for v in (n1, mask, *qkv_parts)]
    got = call(kernel, outs, args, scratch, "first_attention", FLOPS_FIRST)
    return dict(zip(made, got)), got[-4], got[-3:]

def middle_part(me, ent, inject, weighed, mask, wqkv, ht, rest_parts, ff):
    t, d = ent.shape
    nb, nc = t // BLK, t // CHUNK
    parts = len(rest_parts)
    sh = {"a_" + k: v for k, v in more_shapes(t, d, ff).items() if k not in ("dpk", "gm")}
    sh.update({"b_" + k: v for k, v in {**saved_shapes(t, d, ff), **more_shapes(t, d, ff)}.items() if k not in ("n1", "dpk", "ht", "gm")})
    sh.update(state=((t, d), F32), dk=((t + BLK, d), F32), dv=((t + BLK, d), F32),
              wqkv_t=((3 * d, d), BF), wup_t=((ff, d), BF), wdown_t=((d, ff), BF), tr=((2, d, t), BF),
              wup=((d, ff), BF), wdown=((ff, d), BF), mup=((d, ff), BF), mdown_t=((d, ff), BF), mdown=((ff, d), BF))
    def kernel(m, x):
        me_ref, ent_ref, inj, weighed_ref, x.mask, wqkv_ref, ht_ref = m.ins[:7]
        final, g, ginj, gm, wout, n1, dpk, ht, gm_two, keep, send = m.outs
        its = [types.SimpleNamespace(**{k[2:]: v for k, v in vars(x).items() if k.startswith(p)}) for p in ("a_", "b_")]
        its[0].ht, its[0].gm = ht_ref, gm
        its[1].n1, its[1].dpk, its[1].ht, its[1].gm = n1, dpk, ht, gm_two
        place_rest(me_ref[0], m.ins[7:], wout, x.wup, x.wdown)
        pad_zero(its[1])
        def rows_of(j):
            return slice(j * CHUNK, (j + 1) * CHUNK)
        def mlp_of(n, j, src, dst):
            at = rows_of(j)
            entered = src[at, :] + inj[at, :] if n else src[at, :]
            dst[at, :] = mlp(its[n], j, entered, wout, x.wup, x.wdown)
        def project_of(j):
            project(its[1], j, x.state[rows_of(j), :] + inj[rows_of(j), :], wqkv_ref)
        def blocks_of(j):
            n = CHUNK // BLK
            return [tuple(range(j * n, j * n + n))]
        def attend_of(j):
            for blocks in blocks_of(j):
                attend(its[1], blocks, x.mask)
        def back_two(j):
            at = rows_of(j)
            g[at, :] = mlp_back(its[1], j, weighed_ref[at, :], x.wdown_t, x.wup_t)
        def attend_back_of(j):
            for blocks in blocks_of(j):
                attend_back(its[1], blocks, wout, x.dk, x.dv)
        def back_one(j):
            at = rows_of(j)
            finish_packed(its[1], j, x.dk, x.dv)
            new = project_back(its[1], j, g[at, :], x.wqkv_t)
            ginj[at, :] = new
            g[at, :] = mlp_back(its[0], j, new, x.wdown_t, x.wup_t)
        x.dk[0:BLK, :] = jnp.zeros((BLK, d), F32)
        x.dv[0:BLK, :] = jnp.zeros((BLK, d), F32)
        for j in range(nc): mlp_of(0, j, ent_ref, x.state)
        for j in range(nc): project_of(j)
        for j in range(nc): attend_of(j)
        for j in range(nc):
            mlp_of(1, j, x.state, final)
            if j == 0:
                x.wup_t[...] = x.wup[...].T
                x.wdown_t[...] = x.wdown[...].T
                x.wqkv_t[...] = wqkv_ref[...].T
        m.put(0)
        for j in range(nc): back_two(j)
        for j in range(nc): attend_back_of(j)
        for j in range(nc): back_one(j)

        def weight_grad(lefts, rights, dst):
            for n, left in enumerate(lefts):
                x.tr[n] = left[...].T
            def tile(c):
                cc = pl.ds(c * 256, 256)
                total = dot(x.tr[0], rights[0][:, cc])
                for n in range(1, len(rights)):
                    total = total + dot(x.tr[n], rights[n][:, cc])
                dst[:, cc] = total.astype(dst.dtype)
            loop(dst.shape[1] // 256, tile)
        weight_grad([s.g2 for s in its], [s.act for s in its], x.mdown_t)
        x.mdown[...] = x.mdown_t[...].T
        weight_grad([s.n2 for s in its], [s.gp for s in its], x.mup)
        hand_out(me_ref[0], parts, (x.mup, x.mdown), keep, send)
    piece = ("vmem", (max(parts // 2, 1), 2 * ff // parts, d), BF)
    outs = [("store", (t, d), F32)] + [("vmem", (t, d), F32)] * 2 + [("vmem", (t, d), BF), ("vmem", (d, d), BF), ("vmem", (t, d), BF), ("vmem", (t, 3 * d), BF)] + [("vmem", (nb, d, BLK), BF), ("vmem", (t, d), BF)] + [piece] * 2
    args = [("smem", me)] + [("vmem", v) for v in (ent, inject, weighed, mask, wqkv, ht, *rest_parts)]
    return call(kernel, outs, args, sh, "middle_part", 25 * 10 ** 9, limit=LIMIT_MIDDLE)

def last_part(me, saved, gm, wout, wqkv, n1, dpk, ht, gm_two, g, ginj, parts, ff, first):
    t, d = gm.shape
    nb, nc = t // BLK, t // CHUNK
    scratch = dict(dk=((t + BLK, d), F32), dv=((t + BLK, d), F32), tr=((2, d, t), BF), mat=((d, 3 * d), BF), mout=((d, d), BF), wt=((3 * d, d), BF), dpk=((t, 3 * d), BF))
    def kernel(m, s):
        me_ref, s.gm, wout_ref, w_ref, n1_ref, dpk_ref, ht_ref, gm_ref, g_ref, gi_ref = m.ins[:10]
        vars(s).update(zip(SAVED, m.ins[10:]))
        keep, send, grad, grad_inject = m.outs
        s.dk[0:BLK, :] = jnp.zeros((BLK, d), F32)
        s.dv[0:BLK, :] = jnp.zeros((BLK, d), F32)
        for i in range(0, nb, 4):
            attend_back(s, (i, i + 1, i + 2, i + 3), wout_ref, s.dk, s.dv)
        s.tr[0] = s.n1[...].T
        s.tr[1] = n1_ref[...].T
        s.wt[...] = w_ref[...].T
        loop(nc, lambda j: finish_packed(s, j, s.dk, s.dv))
        def tile(c):
            cc = slice(c * 256, (c + 1) * 256)
            s.mat[:, cc] = (dot(s.tr[0], s.dpk[:, cc]) + dot(s.tr[1], dpk_ref[:, cc])).astype(BF)
        loop(3, tile)
        total = None
        for left, right in ((s.ht, s.gm), (ht_ref, gm_ref)):
            for b in range(nb):
                part = dot(left[b], right[b * BLK:(b + 1) * BLK, :])
                total = part if total is None else total + part
        s.mout[...] = total.astype(BF)
        hand_out(me_ref[0], parts, (s.mout, s.mat), keep, send)
        def chunk(j):
            at = rows(j * CHUNK, CHUNK)
            new = project_back(s, j, g_ref[at, :], s.wt)
            grad[at, :] = new
            grad_inject[at, :] = new + gi_ref[at, :]
        loop(nc, chunk)
        m.put(2)
        m.put(3)
    outs = [("vmem", (max(parts // 2, 1), 4 * d // parts, d), BF)] * 2 + [("store", (t, d), F32)] * 2
    args = [("smem", me)] + [("vmem", v) for v in (gm, wout, wqkv, n1, dpk, ht, gm_two, g, ginj)]
    args += [("vmem", saved[k]) for k in SAVED] + [("any", v) for v in first]
    return call(kernel, outs, args, scratch, "last_part", FLOPS_LAST, limit=LIMIT_LAST)

def to_column(row):
    n = row.shape[1]
    eye = lax.broadcasted_iota(jnp.int32, (n, n), 0) == lax.broadcasted_iota(jnp.int32, (n, n), 1)
    return jnp.sum(jnp.where(eye, jnp.broadcast_to(row, (n, n)), 0.0), axis=1, keepdims=True)

def to_row(column):
    n = column.shape[0]
    eye = lax.broadcasted_iota(jnp.int32, (n, n), 0) == lax.broadcasted_iota(jnp.int32, (n, n), 1)
    return jnp.sum(jnp.where(eye, jnp.broadcast_to(column, (n, n)), 0.0), axis=0, keepdims=True)

def pack_weights(w_qkv, gain_one, w_out, w_up, w_down, gain_two):
    r, d = w_out.shape
    n = w_up.shape[1] // d
    def kernel(m, s):
        qkv, g_one, out, up, down, g_two = m.ins
        m.wait(0, 1)
        m.outs[0][...] = (qkv[...].astype(F32) * to_column(g_one[...].astype(F32))).astype(BF)
        m.wait(2, 3, 4, 5)
        m.outs[1][0:r, :] = out[...]
        col = to_column(g_two[...].astype(F32))
        for c in range(n):
            m.outs[1][(c + 1) * r:(c + 2) * r, :] = (up[:, c * d:(c + 1) * d].astype(F32) * col).astype(BF)
        m.outs[1][(n + 1) * r:, :] = down[...]
    args = [("load", v) for v in (w_qkv, gain_one.reshape(1, -1), w_out, w_up, w_down, gain_two.reshape(1, -1))]
    return call(kernel, [("vmem", w_qkv.shape, BF), ("vmem", ((n + 1) * r + w_down.shape[0], d), BF)], args, {}, "pack_weights", 10 ** 6)

def sum_parts(parts, lo, size):
    acc = parts[0][lo:lo + size, :].astype(F32)
    for p in parts[1:]:
        acc = acc + p[lo:lo + size, :].astype(F32)
    return acc

def finished(shares, weight, gain, lead, tail, name):
    r, cols = weight.shape
    d = shares[0].shape[1]
    n = cols // d
    others = [(lo, size) for lo, size in ((0, lead), (lead + n * r, tail)) if size]
    def kernel(m, s):
        w, g, parts = m.ins[0], to_column(m.ins[1][...].astype(F32)), m.ins[2:]
        along = jnp.zeros((r, 1), F32)
        for c in range(n):
            v = sum_parts(parts, lead + c * r, r)
            m.outs[0][:, c * d:(c + 1) * d] = v * g
            along = along + jnp.sum(v * w[:, c * d:(c + 1) * d].astype(F32), axis=1, keepdims=True)
        m.put(0)
        m.outs[1][...] = to_row(along)
        m.put(1)
        for at, (lo, size) in enumerate(others):
            m.outs[2 + at][...] = sum_parts(parts, lo, size)
            m.put(2 + at)
    outs = [("store", (r, cols), F32), ("store", (1, r), F32)] + [("store", (size, d), F32) for _, size in others]
    got = call(kernel, outs, [("vmem", v) for v in (weight, gain.reshape(1, -1), *shares)], {}, name, 10 ** 6)
    return [got[0], got[1].reshape(r)] + list(got[2:])

def after(values, *others):
    return lax.optimization_barrier((values, others))[0]

def exchange(x, axis, size, step):
    return lax.ppermute(x, axis, [(i, i ^ step) for i in range(size)])

def far_parts(x, size):
    return [x] + [exchange(x, "fsdp", size, 2 * k) for k in range(1, size // 2)]

def with_near(far, size):
    return [v for x in far for v in (x, exchange(x, "fsdp", size, 1))]

def sum_near(keep, near, then=None):
    total = keep.astype(F32) + near.astype(F32)
    if then is not None:
        total = total + jnp.minimum(jnp.abs(then[:keep.shape[1]].astype(F32)), 0.0)
    return [total[k].astype(BF) for k in range(keep.shape[0])]

def send_far(summed, size):
    return [exchange(summed[k], "fsdp", size, 2 * k) for k in range(size // 2 - 1, 0, -1)]

def along_dp(share, size):
    return [share] + [exchange(share, "dp", size, k) for k in range(1, size)]

def send_near(pieces, size):
    return [exchange(p, "fsdp", size, 1) for p in pieces[1::2]]

def send_far(summed, size):
    return [exchange(summed[k], "fsdp", size, 2 * k) for k in range(size // 2 - 1, 0, -1)]

def reduce_whole(whole, sizes):
    out, lo = [], 0
    for n in sizes:
        share = lax.psum_scatter(whole[lo:lo + n], "fsdp", scatter_dimension=0, tiled=True)
        out.append(lax.psum(share, "dp").astype(F32))
        lo += n
    return jnp.concatenate(out, axis=0)

def on_device(n_dp, n_fsdp, states, inject, ln1_gain, w_qkv, w_out, ln2_gain, w_up, w_down, prompt_lengths, loop_counts, cotangent):
    d = states.shape[1]
    r, ff = w_up.shape
    direct = r % 16 == 0
    if direct:
        me = lax.axis_index("fsdp").astype(jnp.int32).reshape(1)
        own_qkv, own_rest = pack_weights(w_qkv, ln1_gain, w_out, w_up, w_down, ln2_gain)
        qkv_far = far_parts(own_qkv, n_fsdp)
        rest_far = far_parts(own_rest, n_fsdp)
    else:
        me = jnp.zeros((1,), jnp.int32)
        full = lambda v: lax.all_gather(v, "fsdp", axis=0, tiled=True)
        up = full((w_up.astype(F32) * ln2_gain.astype(F32)[:, None]).astype(BF))
        qkv_parts = [full((w_qkv.astype(F32) * ln1_gain.astype(F32)[:, None]).astype(BF))]
        rest_parts = [jnp.concatenate([full(w_out)] + [up[:, c:c + d] for c in range(0, ff, d)] + [full(w_down)], axis=0)]
    n1, r1, mask = prepare(prompt_lengths, states, inject)
    if direct:
        qkv_parts = with_near(qkv_far[:1], n_fsdp) + with_near(after(qkv_far[1:], n1), n_fsdp)
    parts = len(qkv_parts)
    saved, wqkv, entering = first_attention(me, prompt_lengths, loop_counts, states, inject, cotangent, n1, mask, qkv_parts, ff)
    saved.update(n1=n1, r1=r1)
    if direct:
        rest_parts = with_near(rest_far[:1], n_fsdp) + with_near(after(rest_far[1:], wqkv), n_fsdp)
    final, g, ginj, gm, wout, n1, dpk, ht, gm_two, keep, send = middle_part(
        me, *entering, mask, wqkv, saved["ht"], rest_parts, ff)
    summed = []
    if direct:
        summed = sum_near(keep, exchange(send, "fsdp", n_fsdp, 1))
        far = send_far(summed, n_fsdp)
    else:
        shares = [reduce_whole(keep[0], [d] * (ff // d) + [ff])]
    keep_qkv, send_qkv, grad_states, grad_inject = last_part(
        me, saved, gm, wout, wqkv, n1, dpk, ht, gm_two, g, ginj, parts, ff, summed)
    if direct:
        near = exchange(send_qkv, "fsdp", n_fsdp, 1)
        share = sum_parts([summed[0], *far], 0, summed[0].shape[0]).astype(BF)
        shares = along_dp(share, n_dp)
        summed = sum_near(keep_qkv, near, share)
        shares_qkv = along_dp(sum_parts([summed[0], *send_far(summed, n_fsdp)], 0, 4 * r).astype(BF), n_dp)
    else:
        shares_qkv = [reduce_whole(keep_qkv[0], [d] * 4)]
    d_up, d_gain_two, d_down = finished(shares, w_up, ln2_gain, 0, w_down.shape[0], "finished_mlp")
    d_qkv, d_gain_one, d_out = finished(shares_qkv, w_qkv, ln1_gain, r, 0, "finished_attention")
    return (final, grad_states, grad_inject, d_gain_one, d_qkv, d_out, d_gain_two, d_up, d_down)

def solution(mesh):
    tok, vec, mat = P(("dp", "fsdp"), None), P("fsdp"), P("fsdp", None)
    return jax.shard_map(
        functools.partial(on_device, mesh.shape["dp"], mesh.shape["fsdp"]), mesh=mesh,
        in_specs=(tok, tok, vec, mat, mat, vec, mat, mat, tok, tok, tok),
        out_specs=(tok, tok, tok, vec, mat, mat, vec, mat, mat), check_vma=False)
```

```python
import functools
import types

import jax
import jax.numpy as jnp
from jax import lax
from jax.experimental import pallas as pl
from jax.experimental.pallas import tpu as pltpu
from jax.sharding import PartitionSpec as P

BF = jnp.bfloat16
F32 = jnp.float32
HEADS = 8
ITERS = 2
BLK = 128
CHUNK = 512
NEG = -1e30
LOG2E = 1.4426950408889634
LN2 = 0.6931471805599453
GELU_A = 0.7978845608028654
GELU_B = GELU_A * 0.044715
FLOPS_FIRST = 10 ** 6
FLOPS_PREPARE = 10 ** 6
FLOPS_LAST = 10 ** 10
LIMIT_MIDDLE = 42
LIMIT_LAST = 16


def dot(a, b):
    return jnp.dot(a, b, preferred_element_type=F32)

def dot_tn(a, b):
    return lax.dot_general(a, b, (((0,), (0,)), ((), ())), preferred_element_type=F32)

def dot_nt(a, b):
    return lax.dot_general(a, b, (((1,), (1,)), ((), ())), preferred_element_type=F32)

def rows(start, size):
    return pl.ds(start, size)

def ln_fwd(x):
    c = x - jnp.mean(x, axis=1, keepdims=True)
    r = lax.rsqrt(jnp.mean(c * c, axis=1, keepdims=True) + 1e-5)
    return c * r, r

def ln_bwd(y, n, r):
    return r * (y - jnp.mean(y, axis=1, keepdims=True) - n * jnp.mean(y * n, axis=1, keepdims=True))

def loop(n, body):
    for i in range(n):
        body(i)

def make_masks(len_ref, mask_ref, nb):
    pos = lax.broadcasted_iota(jnp.int32, (1, BLK), 1)
    ends = []
    total = jnp.int32(0)
    for p in range(len_ref.shape[1]):
        total = total + len_ref[0, p]
        ends.append(total)

    def block(i, _):
        q = pos + i * BLK
        start = jnp.zeros((1, BLK), jnp.int32)
        for e in ends:
            start = jnp.where(q >= e, e, start)
        k = lax.broadcasted_iota(jnp.int32, (2 * BLK, BLK), 0) + (i - 1) * BLK
        mask_ref[i] = jnp.where((k >= start) & (k <= q), 0.0, NEG).astype(F32)
        return 0

    lax.fori_loop(0, nb, block, 0)

def pad_zero(s):
    s.kp[0:BLK, :] = jnp.zeros((BLK, s.kp.shape[1]), BF)
    s.vp[0:BLK, :] = jnp.zeros((BLK, s.vp.shape[1]), BF)
    s.kt[0] = jnp.zeros(s.kt.shape[1:], BF)
    s.vt[0] = jnp.zeros(s.vt.shape[1:], BF)

def project(s, j, ent, wqkv):
    n, r = ln_fwd(ent)
    nb16 = n.astype(BF)
    s.n1[rows(j * CHUNK, CHUNK), :] = nb16
    s.r1[rows(j * CHUNK, CHUNK), :] = jnp.broadcast_to(r, (CHUNK, 128))
    pack_heads(s, j, nb16, wqkv)

def pack_heads(s, j, nb16, wqkv):
    d = nb16.shape[1]
    scale = LOG2E * (d // HEADS) ** -0.5
    q = (dot(nb16, wqkv[:, 0:d]) * scale).astype(BF)
    k = dot(nb16, wqkv[:, d:2 * d]).astype(BF)
    v = dot(nb16, wqkv[:, 2 * d:3 * d]).astype(BF)
    s.qs[rows(j * CHUNK, CHUNK), :] = q
    s.kp[pl.ds(j * CHUNK + BLK, CHUNK), :] = k
    s.vp[pl.ds(j * CHUNK + BLK, CHUNK), :] = v
    qt, kt, vt = q.T, k.T, v.T
    for b in range(CHUNK // BLK):
        i = j * (CHUNK // BLK) + b
        s.qst[i] = qt[:, b * BLK:(b + 1) * BLK]
        s.kt[i + 1] = kt[:, b * BLK:(b + 1) * BLK]
        s.vt[i + 1] = vt[:, b * BLK:(b + 1) * BLK]

def split_heads(tile, a, hd):
    def alone(lo):
        parts = [jnp.zeros((n, tile.shape[1]), tile.dtype) for n in (lo, tile.shape[0] - lo - hd)]
        parts = [parts[0], tile[lo:lo + hd], parts[1]]
        return jnp.concatenate([p for p in parts if p.shape[0]], axis=0)
    return jnp.concatenate([alone(a), alone(a + hd)], axis=1)

def stack_heads(tile, a, hd):
    z = jnp.zeros_like(tile)
    lane = lax.broadcasted_iota(jnp.int32, tile.shape, 1)
    top = jnp.where((lane >= a) & (lane < a + hd), tile, z)
    low = jnp.where((lane >= a + hd) & (lane < a + 2 * hd), tile, z)
    return jnp.concatenate([top, low], axis=0)

def pairs_of(d):
    hd = d // HEADS
    per = 128 // (2 * hd)
    return [(p, slice(p // per * 128, p // per * 128 + 128), p % per * 2 * hd, p * 2 * hd) for p in range(HEADS // 2)]

def window(ref, i, lo, n):
    return jnp.concatenate([ref[i, lo:lo + n, :], ref[i + 1, lo:lo + n, :]], axis=1)

def attend(s, blocks, mask_ref):
    d = s.qs.shape[1]
    hd = d // HEADS
    ones = jnp.ones((16, 2 * BLK), BF)
    def scores(i):
        win = pl.ds(i * BLK, 2 * BLK)
        return [dot(s.kp[win, tile], split_heads(s.qst[i, tile, :], a, hd)) for _, tile, a, _ in pairs_of(d)]
    def soft(i, all_scores):
        mask = mask_ref[i]
        mask = jnp.concatenate([mask, mask], axis=1)
        out = []
        for sc in all_scores:
            sc = sc + mask
            out.append(jnp.exp2(sc - jnp.max(sc, axis=0, keepdims=True)).astype(BF))
        return out
    def values(i, es):
        return [dot(jnp.concatenate([window(s.vt, i, lo, 2 * hd), ones], axis=0), es[p]) for p, _, _, lo in pairs_of(d)]
    es = []
    ready = scores(blocks[0])
    for n, i in enumerate(blocks):
        ahead = scores(blocks[n + 1]) if n + 1 < len(blocks) else None
        es.append(soft(i, ready))
        ready = ahead
    os = [values(i, e) for i, e in zip(blocks, es)]
    for i, e, o in zip(blocks, es, os):
        for p, _, _, lo in pairs_of(d):
            s.e[i, p] = e[p]
            inv = 1.0 / o[p][2 * hd:2 * hd + 1, :]
            s.linv[i, 2 * p:2 * p + 1, :] = inv[:, :BLK]
            s.linv[i, 2 * p + 1:2 * p + 2, :] = inv[:, BLK:]
            s.ht[i, lo:lo + hd, :] = (o[p][0:hd, :BLK] * inv[:, :BLK]).astype(BF)
            s.ht[i, lo + hd:lo + 2 * hd, :] = (o[p][hd:2 * hd, BLK:] * inv[:, BLK:]).astype(BF)

def heads_chunk(s, j):
    return jnp.concatenate([s.ht[j * (CHUNK // BLK) + b] for b in range(CHUNK // BLK)], axis=1)

def mlp(s, j, ent, wout, wup, wdown):
    mid = ent + dot_tn(heads_chunk(s, j), wout[...])
    n, r = ln_fwd(mid)
    nb16 = n.astype(BF)
    at = rows(j * CHUNK, CHUNK)
    s.n2[at, :] = nb16
    s.r2[at, :] = jnp.broadcast_to(r, (CHUNK, 128))
    acc = mid
    for f in range(wup.shape[1] // 256):
        c = slice(f * 256, (f + 1) * 256)
        h = dot(nb16, wup[:, c]).astype(BF)
        h2 = h * h
        sg = 0.5 * jnp.tanh(h * (GELU_B * h2 + GELU_A)) + 0.5
        act = h * sg
        s.act[at, c] = act
        s.gp[at, c] = sg + act * (2.0 - 2.0 * sg) * (3 * GELU_B * h2 + GELU_A)
    return mid + dot(s.act[at, :], wdown[...])

def mlp_back(s, j, g, wdown_t, wup_t):
    at = rows(j * CHUNK, CHUNK)
    gb = g.astype(BF)
    s.g2[at, :] = gb
    acc = None
    for f in range(wdown_t.shape[1] // 256):
        c = slice(f * 256, (f + 1) * 256)
        dh = dot(gb, wdown_t[:, c]).astype(BF) * s.gp[at, c]
        s.gp[at, c] = dh
    acc = dot(s.gp[at, :], wup_t[...])
    g = g + ln_bwd(acc, s.n2[at, :].astype(F32), s.r2[at, 0:1])
    s.gm[at, :] = g.astype(BF)
    return g

def attend_back(s, blocks, wout, dk_ref, dv_ref):
    d = s.qs.shape[1]
    hd = d // HEADS
    minus = jnp.full((2 * BLK, 128), -1.0, BF)
    def head_grads(i):
        raw = dot_nt(wout[...], s.gm[rows(i * BLK, BLK), :])
        inv = jnp.concatenate([jnp.broadcast_to(s.linv[i, h:h + 1, :], (hd, BLK)) for h in range(HEADS)], axis=0)
        dost = (raw * inv).astype(BF)
        return dost, (dost.astype(F32) * s.ht[i].astype(F32)).astype(BF), dost.T
    def prob_grads(i, dost, doh):
        win = pl.ds(i * BLK, 2 * BLK)
        return [dot(jnp.concatenate([s.vp[win, tile], minus], axis=1),
                    jnp.concatenate([split_heads(dost[tile, :], a, hd), split_heads(doh[tile, :], a, hd)], axis=0))
                for _, tile, a, _ in pairs_of(d)]
    def by_keys(lhs, tokens):
        return [dot(lhs[p], stack_heads(tokens[:, tile], a, hd)) for p, tile, a, _ in pairs_of(d)]
    def by_queries(i, dss):
        out = []
        for p, _, _, lo in pairs_of(d):
            dq = dot(window(s.kt, i, lo, 2 * hd), dss[p])
            out += [dq[0:hd, :BLK], dq[hd:2 * hd, BLK:]]
        return (jnp.concatenate(out, axis=0) * hd ** -0.5).astype(BF)
    heads = [head_grads(i) for i in blocks]
    dps = [prob_grads(i, h[0], h[1]) for i, h in zip(blocks, heads)]
    es = [[s.e[i, p] for p in range(HEADS // 2)] for i in blocks]
    dvs = [by_keys(e, h[2]) for e, h in zip(es, heads)]
    dss = [[(x.astype(F32) * y).astype(BF) for x, y in zip(e, dp)] for e, dp in zip(es, dps)]
    dks = [by_keys(ds, s.qs[rows(i * BLK, BLK), :]) for i, ds in zip(blocks, dss)]
    dqs = [by_queries(i, ds) for i, ds in zip(blocks, dss)]
    per = HEADS // 2 // (d // 128)
    for n, i in enumerate(blocks):
        top, low = pl.ds(i * BLK, BLK), pl.ds(i * BLK + BLK, BLK)
        for ref, parts in ((dk_ref, dks[n]), (dv_ref, dvs[n])):
            for t in range(d // 128):
                tile = slice(t * 128, (t + 1) * 128)
                total = sum(parts[t * per + 1:(t + 1) * per], parts[t * per])
                ref[top, tile] += total[:BLK]
                ref[low, tile] = total[BLK:]
        s.dpk[rows(i * BLK, BLK), 0:d] = dqs[n].T

def finish_packed(s, j, dk_ref, dv_ref):
    d = s.n1.shape[1]
    at = rows(j * CHUNK, CHUNK)
    pat = pl.ds(j * CHUNK + BLK, CHUNK)
    s.dpk[at, d:2 * d] = (dk_ref[pat, :] * LN2).astype(BF)
    s.dpk[at, 2 * d:3 * d] = dv_ref[pat, :].astype(BF)

def project_back(s, j, g, wqkv_t):
    at = rows(j * CHUNK, CHUNK)
    return g + ln_bwd(dot(s.dpk[at, :], wqkv_t[...]), s.n1[at, :].astype(F32), s.r1[at, 0:1])

def weigh(cnt_ref, len_ref, j, cot):
    pos = lax.broadcasted_iota(jnp.int32, (CHUNK, 128), 0) + j * CHUNK
    w = jnp.zeros((CHUNK, 128), F32)
    begin = jnp.int32(0)
    for p in range(len_ref.shape[1]):
        w = jnp.where(pos >= begin, 12.0 / cnt_ref[0, p].astype(F32), w)
        begin = begin + len_ref[0, p]
    return cot * jnp.concatenate([w] * (cot.shape[1] // 128), axis=1)

def saved_shapes(t, d, ff):
    nb = t // BLK
    return dict(n1=((t, d), BF), r1=((t, 128), F32), qs=((t, d), BF), kp=((t + BLK, d), BF), vp=((t + BLK, d), BF),
                qst=((nb, d, BLK), BF), kt=((nb + 1, d, BLK), BF), vt=((nb + 1, d, BLK), BF), e=((nb, HEADS // 2, 2 * BLK, 2 * BLK), BF),
                ht=((nb, d, BLK), BF), linv=((nb, HEADS, BLK), F32))
def more_shapes(t, d, ff):
    return dict(n2=((t, d), BF), r2=((t, 128), F32), act=((t, ff), BF), gp=((t, ff), BF),
                g2=((t, d), BF), gm=((t, d), BF), dpk=((t, 3 * d), BF))

class Memory:
    def __init__(self, ins, outs, sems, hbm, loads):
        self.ins, self.outs, self.sems, self.hbm, self.loads, self.started = ins, outs, sems, hbm, loads, []

    def wait(self, *which):
        for n in which:
            self.loads[n].wait()

    def put(self, n):
        copy = pltpu.make_async_copy(self.outs[n], self.hbm[n], self.sems.at[len(self.started)])
        copy.start()
        self.started.append(copy)

def call(kernel, outs, args, scratch, name, flops, limit=16):
    spec = dict(vmem=pl.BlockSpec(memory_space=pltpu.VMEM), smem=pl.BlockSpec(memory_space=pltpu.SMEM), any=pl.BlockSpec(memory_space=pl.ANY))
    spec["store"] = spec["load"] = spec["any"]
    n_in, n_out, n_scratch = len(args), len(outs), len(scratch)
    stores = [n for n, o in enumerate(outs) if o[0] == "store"]
    loads = [n for n, a in enumerate(args) if a[0] == "load"]
    buffers = [pltpu.VMEM(outs[n][1], outs[n][2]) for n in stores] + [(pltpu.SMEM if args[n][1].dtype == jnp.int32 else pltpu.VMEM)(args[n][1].shape, args[n][1].dtype) for n in loads]
    buffers += [pltpu.SemaphoreType.DMA((max(len(stores), 1),)), pltpu.SemaphoreType.DMA((max(len(loads), 1),))]
    def run(*refs):
        ins, results, rest = list(refs[:n_in]), list(refs[n_in:n_in + n_out]), refs[n_in + n_out:]
        hbm, coming = list(results), {}
        for n, r in zip(stores, rest[n_scratch:]):
            results[n] = r
        for c, (n, r) in enumerate(zip(loads, rest[n_scratch + len(stores):])):
            coming[n] = pltpu.make_async_copy(ins[n], r, rest[-1].at[c])
            coming[n].start()
            ins[n] = r
        memory = Memory(ins, results, rest[-2], hbm, coming)
        kernel(memory, types.SimpleNamespace(**dict(zip(scratch, rest))))
        for copy in memory.started:
            copy.wait()
    shapes = dict(vmem=pltpu.VMEM, store=jax.ShapeDtypeStruct)
    place = dict(vmem=pltpu.VMEM, load=pltpu.HBM)
    return pl.pallas_call(
        run, out_shape=tuple(shapes[o[0]](o[1], o[2]) for o in outs),
        in_specs=[spec[k] for k, _ in args], out_specs=tuple(spec[o[0]] for o in outs),
        scratch_shapes=[pltpu.VMEM(*v) for v in scratch.values()] + buffers,
        compiler_params=pltpu.CompilerParams(vmem_limit_bytes=limit << 20), name=name,
        cost_estimate=pl.CostEstimate(flops=flops, bytes_accessed=1 << 20, transcendentals=0))(
        *[pltpu.with_memory_space_constraint(v, place[k]) if k in place else v for k, v in args])

def place_qkv(me, parts, wqkv):
    r = wqkv.shape[0] // len(parts)
    for x, p in enumerate(parts):
        wqkv[pl.ds(pl.multiple_of((me ^ x) * r, r), r), :] = p[...]

def place_rest(me, parts, wout, wup, wdown):
    r, rd = wout.shape[0] // len(parts), wdown.shape[0] // len(parts)
    for x, p in enumerate(parts):
        at = pl.ds(pl.multiple_of((me ^ x) * r, r), r)
        wout[at, :] = p[0:r, :]
        for c in range(wup.shape[1] // 256):
            wup[at, c * 256:(c + 1) * 256] = p[(c + 1) * r:(c + 2) * r, :]
        lo = r * (1 + wup.shape[1] // 256)
        wdown[pl.ds(pl.multiple_of((me ^ x) * rd, rd), rd), :] = p[lo:lo + rd, :]

def hand_out(me, parts, mats, keep, send):
    for x in range(parts):
        dst = send if x % 2 else keep
        lo = 0
        for m in mats:
            r = m.shape[0] // parts
            at = pl.ds(pl.multiple_of((me ^ x) * r, r), r)
            for c in range(m.shape[1] // 256):
                dst[x // 2, lo:lo + r, :] = m[at, c * 256:(c + 1) * 256]
                lo += r

SAVED = ("e", "n1", "r1", "qs", "vp", "kt", "ht", "linv")

def prepare(lengths, states, inject):
    t, d = states.shape
    nb, nc = t // BLK, t // CHUNK
    def kernel(m, s):
        len_ref, st, inj = m.ins
        n1, r1, mask = m.outs
        m.wait(0)
        make_masks(len_ref, mask, nb)
        m.wait(1, 2)
        for j in range(nc):
            at = slice(j * CHUNK, (j + 1) * CHUNK)
            n, r = ln_fwd(st[at, :] + inj[at, :])
            n1[at, :] = n.astype(BF)
            r1[at, :] = jnp.broadcast_to(r, (CHUNK, 128))
    outs = [("vmem", (t, d), BF), ("vmem", (t, 128), F32), ("vmem", (nb, 2 * BLK, BLK), F32)]
    args = [("load", v) for v in (lengths, states, inject)]
    return call(kernel, outs, args, {}, "prepare", FLOPS_PREPARE)

def first_attention(me, lengths, counts, states, inject, cot, n1, mask, qkv_parts, ff):
    t, d = n1.shape
    nb, nc = t // BLK, t // CHUNK
    shapes = saved_shapes(t, d, ff)
    made = [k for k in SAVED if k not in ("n1", "r1")]
    scratch = {k: v for k, v in shapes.items() if k not in SAVED}
    def kernel(m, s):
        me_ref, len_ref, cnt_ref, st, inj, ct, n1_ref, mask_ref = m.ins[:8]
        vars(s).update(zip(made, m.outs))
        wqkv, ent, inj_out, weighed = m.outs[-4:]
        pad_zero(s)
        place_qkv(me_ref[0], m.ins[8:], wqkv)
        for j in range(nc):
            pack_heads(s, j, n1_ref[j * CHUNK:(j + 1) * CHUNK, :], wqkv)
        for i in range(0, nb, 4):
            attend(s, (i, i + 1, i + 2, i + 3), mask_ref)
        m.wait(1, 2, 3, 4, 5)
        for j in range(nc):
            at = slice(j * CHUNK, (j + 1) * CHUNK)
            ent[at, :] = st[at, :] + inj[at, :]
            inj_out[at, :] = inj[at, :]
            weighed[at, :] = weigh(cnt_ref, len_ref, j, ct[at, :])
    outs = [("vmem",) + shapes[k] for k in made] + [("vmem", (d, 3 * d), BF)] + [("vmem", (t, d), F32)] * 3
    args = [("smem", me)] + [("load", v) for v in (lengths, counts, states, inject, cot)] + [("vmem", v) for v in (n1, mask, *qkv_parts)]
    got = call(kernel, outs, args, scratch, "first_attention", FLOPS_FIRST)
    return dict(zip(made, got)), got[-4], got[-3:]

def middle_part(me, ent, inject, weighed, mask, wqkv, ht, rest_parts, ff):
    t, d = ent.shape
    nb, nc = t // BLK, t // CHUNK
    parts = len(rest_parts)
    sh = {"a_" + k: v for k, v in more_shapes(t, d, ff).items() if k not in ("dpk", "gm")}
    sh.update({"b_" + k: v for k, v in {**saved_shapes(t, d, ff), **more_shapes(t, d, ff)}.items() if k not in ("n1", "dpk", "ht", "gm")})
    sh.update(state=((t, d), F32), dk=((t + BLK, d), F32), dv=((t + BLK, d), F32),
              wqkv_t=((3 * d, d), BF), wup_t=((ff, d), BF), wdown_t=((d, ff), BF), tr=((2, d, t), BF),
              wup=((d, ff), BF), wdown=((ff, d), BF), mup=((d, ff), BF), mdown_t=((d, ff), BF), mdown=((ff, d), BF))
    def kernel(m, x):
        me_ref, ent_ref, inj, weighed_ref, x.mask, wqkv_ref, ht_ref = m.ins[:7]
        final, g, ginj, gm, wout, n1, dpk, ht, gm_two, keep, send = m.outs
        its = [types.SimpleNamespace(**{k[2:]: v for k, v in vars(x).items() if k.startswith(p)}) for p in ("a_", "b_")]
        its[0].ht, its[0].gm = ht_ref, gm
        its[1].n1, its[1].dpk, its[1].ht, its[1].gm = n1, dpk, ht, gm_two
        place_rest(me_ref[0], m.ins[7:], wout, x.wup, x.wdown)
        pad_zero(its[1])
        def rows_of(j):
            return slice(j * CHUNK, (j + 1) * CHUNK)
        def mlp_of(n, j, src, dst):
            at = rows_of(j)
            entered = src[at, :] + inj[at, :] if n else src[at, :]
            dst[at, :] = mlp(its[n], j, entered, wout, x.wup, x.wdown)
        def project_of(j):
            project(its[1], j, x.state[rows_of(j), :] + inj[rows_of(j), :], wqkv_ref)
        def blocks_of(j):
            n = CHUNK // BLK
            return [tuple(range(j * n, j * n + n))]
        def attend_of(j):
            for blocks in blocks_of(j):
                attend(its[1], blocks, x.mask)
        def back_two(j):
            at = rows_of(j)
            g[at, :] = mlp_back(its[1], j, weighed_ref[at, :], x.wdown_t, x.wup_t)
        def attend_back_of(j):
            for blocks in blocks_of(j):
                attend_back(its[1], blocks, wout, x.dk, x.dv)
        def back_one(j):
            at = rows_of(j)
            finish_packed(its[1], j, x.dk, x.dv)
            new = project_back(its[1], j, g[at, :], x.wqkv_t)
            ginj[at, :] = new
            g[at, :] = mlp_back(its[0], j, new, x.wdown_t, x.wup_t)
        x.dk[0:BLK, :] = jnp.zeros((BLK, d), F32)
        x.dv[0:BLK, :] = jnp.zeros((BLK, d), F32)
        for j in range(nc): mlp_of(0, j, ent_ref, x.state)
        for j in range(nc): project_of(j)
        for j in range(nc): attend_of(j)
        for j in range(nc):
            mlp_of(1, j, x.state, final)
            if j == 0:
                x.wup_t[...] = x.wup[...].T
                x.wdown_t[...] = x.wdown[...].T
                x.wqkv_t[...] = wqkv_ref[...].T
        m.put(0)
        for j in range(nc): back_two(j)
        for j in range(nc): attend_back_of(j)
        for j in range(nc): back_one(j)

        def weight_grad(lefts, rights, dst):
            for n, left in enumerate(lefts):
                x.tr[n] = left[...].T
            def tile(c):
                cc = pl.ds(c * 256, 256)
                total = dot(x.tr[0], rights[0][:, cc])
                for n in range(1, len(rights)):
                    total = total + dot(x.tr[n], rights[n][:, cc])
                dst[:, cc] = total.astype(dst.dtype)
            loop(dst.shape[1] // 256, tile)
        weight_grad([s.g2 for s in its], [s.act for s in its], x.mdown_t)
        x.mdown[...] = x.mdown_t[...].T
        weight_grad([s.n2 for s in its], [s.gp for s in its], x.mup)
        hand_out(me_ref[0], parts, (x.mup, x.mdown), keep, send)
    piece = ("vmem", (max(parts // 2, 1), 2 * ff // parts, d), BF)
    outs = [("store", (t, d), F32)] + [("vmem", (t, d), F32)] * 2 + [("vmem", (t, d), BF), ("vmem", (d, d), BF), ("vmem", (t, d), BF), ("vmem", (t, 3 * d), BF)] + [("vmem", (nb, d, BLK), BF), ("vmem", (t, d), BF)] + [piece] * 2
    args = [("smem", me)] + [("vmem", v) for v in (ent, inject, weighed, mask, wqkv, ht, *rest_parts)]
    return call(kernel, outs, args, sh, "middle_part", 25 * 10 ** 9, limit=LIMIT_MIDDLE)

def last_part(me, saved, gm, wout, wqkv, n1, dpk, ht, gm_two, g, ginj, parts, ff, first):
    t, d = gm.shape
    nb, nc = t // BLK, t // CHUNK
    scratch = dict(dk=((t + BLK, d), F32), dv=((t + BLK, d), F32), tr=((2, d, t), BF), mat=((d, 3 * d), BF), mout=((d, d), BF), wt=((3 * d, d), BF), dpk=((t, 3 * d), BF))
    def kernel(m, s):
        me_ref, s.gm, wout_ref, w_ref, n1_ref, dpk_ref, ht_ref, gm_ref, g_ref, gi_ref = m.ins[:10]
        vars(s).update(zip(SAVED, m.ins[10:]))
        keep, send, grad, grad_inject = m.outs
        s.dk[0:BLK, :] = jnp.zeros((BLK, d), F32)
        s.dv[0:BLK, :] = jnp.zeros((BLK, d), F32)
        for i in range(0, nb, 4):
            attend_back(s, (i, i + 1, i + 2, i + 3), wout_ref, s.dk, s.dv)
        s.tr[0] = s.n1[...].T
        s.tr[1] = n1_ref[...].T
        s.wt[...] = w_ref[...].T
        loop(nc, lambda j: finish_packed(s, j, s.dk, s.dv))
        def tile(c):
            cc = slice(c * 256, (c + 1) * 256)
            s.mat[:, cc] = (dot(s.tr[0], s.dpk[:, cc]) + dot(s.tr[1], dpk_ref[:, cc])).astype(BF)
        loop(3, tile)
        total = None
        for left, right in ((s.ht, s.gm), (ht_ref, gm_ref)):
            for b in range(nb):
                part = dot(left[b], right[b * BLK:(b + 1) * BLK, :])
                total = part if total is None else total + part
        s.mout[...] = total.astype(BF)
        hand_out(me_ref[0], parts, (s.mout, s.mat), keep, send)
        def chunk(j):
            at = rows(j * CHUNK, CHUNK)
            new = project_back(s, j, g_ref[at, :], s.wt)
            grad[at, :] = new
            grad_inject[at, :] = new + gi_ref[at, :]
        loop(nc, chunk)
        m.put(2)
        m.put(3)
    outs = [("vmem", (max(parts // 2, 1), 4 * d // parts, d), BF)] * 2 + [("store", (t, d), F32)] * 2
    args = [("smem", me)] + [("vmem", v) for v in (gm, wout, wqkv, n1, dpk, ht, gm_two, g, ginj)]
    args += [("vmem", saved[k]) for k in SAVED] + [("any", v) for v in first]
    return call(kernel, outs, args, scratch, "last_part", FLOPS_LAST, limit=LIMIT_LAST)

def to_column(row):
    n = row.shape[1]
    eye = lax.broadcasted_iota(jnp.int32, (n, n), 0) == lax.broadcasted_iota(jnp.int32, (n, n), 1)
    return jnp.sum(jnp.where(eye, jnp.broadcast_to(row, (n, n)), 0.0), axis=1, keepdims=True)

def to_row(column):
    n = column.shape[0]
    eye = lax.broadcasted_iota(jnp.int32, (n, n), 0) == lax.broadcasted_iota(jnp.int32, (n, n), 1)
    return jnp.sum(jnp.where(eye, jnp.broadcast_to(column, (n, n)), 0.0), axis=0, keepdims=True)

def pack_weights(w_qkv, gain_one, w_out, w_up, w_down, gain_two):
    r, d = w_out.shape
    n = w_up.shape[1] // d
    def kernel(m, s):
        qkv, g_one, out, up, down, g_two = m.ins
        m.wait(0, 1)
        m.outs[0][...] = (qkv[...].astype(F32) * to_column(g_one[...].astype(F32))).astype(BF)
        m.wait(2, 3, 4, 5)
        m.outs[1][0:r, :] = out[...]
        col = to_column(g_two[...].astype(F32))
        for c in range(n):
            m.outs[1][(c + 1) * r:(c + 2) * r, :] = (up[:, c * d:(c + 1) * d].astype(F32) * col).astype(BF)
        m.outs[1][(n + 1) * r:, :] = down[...]
    args = [("load", v) for v in (w_qkv, gain_one.reshape(1, -1), w_out, w_up, w_down, gain_two.reshape(1, -1))]
    return call(kernel, [("vmem", w_qkv.shape, BF), ("vmem", ((n + 1) * r + w_down.shape[0], d), BF)], args, {}, "pack_weights", 10 ** 6)

def sum_parts(parts, lo, size):
    acc = parts[0][lo:lo + size, :].astype(F32)
    for p in parts[1:]:
        acc = acc + p[lo:lo + size, :].astype(F32)
    return acc

def finished(shares, weight, gain, lead, tail, name):
    r, cols = weight.shape
    d = shares[0].shape[1]
    n = cols // d
    others = [(lo, size) for lo, size in ((0, lead), (lead + n * r, tail)) if size]
    def kernel(m, s):
        w, g, parts = m.ins[0], to_column(m.ins[1][...].astype(F32)), m.ins[2:]
        along = jnp.zeros((r, 1), F32)
        for c in range(n):
            v = sum_parts(parts, lead + c * r, r)
            m.outs[0][:, c * d:(c + 1) * d] = v * g
            along = along + jnp.sum(v * w[:, c * d:(c + 1) * d].astype(F32), axis=1, keepdims=True)
        m.put(0)
        m.outs[1][...] = to_row(along)
        m.put(1)
        for at, (lo, size) in enumerate(others):
            m.outs[2 + at][...] = sum_parts(parts, lo, size)
            m.put(2 + at)
    outs = [("store", (r, cols), F32), ("store", (1, r), F32)] + [("store", (size, d), F32) for _, size in others]
    got = call(kernel, outs, [("vmem", v) for v in (weight, gain.reshape(1, -1), *shares)], {}, name, 10 ** 6)
    return [got[0], got[1].reshape(r)] + list(got[2:])

def after(values, *others):
    return lax.optimization_barrier((values, others))[0]

def exchange(x, axis, size, step):
    return lax.ppermute(x, axis, [(i, i ^ step) for i in range(size)])

def far_parts(x, size):
    return [x] + [exchange(x, "fsdp", size, 2 * k) for k in range(1, size // 2)]

def with_near(far, size):
    return [v for x in far for v in (x, exchange(x, "fsdp", size, 1))]

def sum_near(keep, near, then=None):
    total = keep.astype(F32) + near.astype(F32)
    if then is not None:
        total = total + jnp.minimum(jnp.abs(then[:keep.shape[1]].astype(F32)), 0.0)
    return [total[k].astype(BF) for k in range(keep.shape[0])]

def send_far(summed, size):
    return [exchange(summed[k], "fsdp", size, 2 * k) for k in range(size // 2 - 1, 0, -1)]

def along_dp(share, size):
    return [share] + [exchange(share, "dp", size, k) for k in range(1, size)]

def send_near(pieces, size):
    return [exchange(p, "fsdp", size, 1) for p in pieces[1::2]]

def send_far(summed, size):
    return [exchange(summed[k], "fsdp", size, 2 * k) for k in range(size // 2 - 1, 0, -1)]

def reduce_whole(whole, sizes):
    out, lo = [], 0
    for n in sizes:
        share = lax.psum_scatter(whole[lo:lo + n], "fsdp", scatter_dimension=0, tiled=True)
        out.append(lax.psum(share, "dp").astype(F32))
        lo += n
    return jnp.concatenate(out, axis=0)

def on_device(n_dp, n_fsdp, states, inject, ln1_gain, w_qkv, w_out, ln2_gain, w_up, w_down, prompt_lengths, loop_counts, cotangent):
    d = states.shape[1]
    r, ff = w_up.shape
    direct = r % 16 == 0
    if direct:
        me = lax.axis_index("fsdp").astype(jnp.int32).reshape(1)
        own_qkv, own_rest = pack_weights(w_qkv, ln1_gain, w_out, w_up, w_down, ln2_gain)
        qkv_far = far_parts(own_qkv, n_fsdp)
        rest_far = far_parts(own_rest, n_fsdp)
    else:
        me = jnp.zeros((1,), jnp.int32)
        full = lambda v: lax.all_gather(v, "fsdp", axis=0, tiled=True)
        up = full((w_up.astype(F32) * ln2_gain.astype(F32)[:, None]).astype(BF))
        qkv_parts = [full((w_qkv.astype(F32) * ln1_gain.astype(F32)[:, None]).astype(BF))]
        rest_parts = [jnp.concatenate([full(w_out)] + [up[:, c:c + d] for c in range(0, ff, d)] + [full(w_down)], axis=0)]
    n1, r1, mask = prepare(prompt_lengths, states, inject)
    if direct:
        qkv_parts = with_near(qkv_far[:1], n_fsdp) + with_near(after(qkv_far[1:], n1), n_fsdp)
    parts = len(qkv_parts)
    saved, wqkv, entering = first_attention(me, prompt_lengths, loop_counts, states, inject, cotangent, n1, mask, qkv_parts, ff)
    saved.update(n1=n1, r1=r1)
    if direct:
        late = with_near(after(rest_far[:0:-1], wqkv), n_fsdp)
        rest_parts = with_near(rest_far[:1], n_fsdp) + [v for x in range(len(late) - 2, -1, -2) for v in late[x:x + 2]]
    final, g, ginj, gm, wout, n1, dpk, ht, gm_two, keep, send = middle_part(
        me, *entering, mask, wqkv, saved["ht"], rest_parts, ff)
    summed = []
    if direct:
        summed = sum_near(keep, exchange(send, "fsdp", n_fsdp, 1))
        far = send_far(summed, n_fsdp)
    else:
        shares = [reduce_whole(keep[0], [d] * (ff // d) + [ff])]
    keep_qkv, send_qkv, grad_states, grad_inject = last_part(
        me, saved, gm, wout, wqkv, n1, dpk, ht, gm_two, g, ginj, parts, ff, summed)
    if direct:
        near = exchange(send_qkv, "fsdp", n_fsdp, 1)
        share = sum_parts([summed[0], *far], 0, summed[0].shape[0]).astype(BF)
        shares = along_dp(share, n_dp)
        summed = sum_near(keep_qkv, near, share)
        shares_qkv = along_dp(sum_parts([summed[0], *send_far(summed, n_fsdp)], 0, 4 * r).astype(BF), n_dp)
    else:
        shares_qkv = [reduce_whole(keep_qkv[0], [d] * 4)]
    d_up, d_gain_two, d_down = finished(shares, w_up, ln2_gain, 0, w_down.shape[0], "finished_mlp")
    d_qkv, d_gain_one, d_out = finished(shares_qkv, w_qkv, ln1_gain, r, 0, "finished_attention")
    return (final, grad_states, grad_inject, d_gain_one, d_qkv, d_out, d_gain_two, d_up, d_down)

def solution(mesh):
    tok, vec, mat = P(("dp", "fsdp"), None), P("fsdp"), P("fsdp", None)
    return jax.shard_map(
        functools.partial(on_device, mesh.shape["dp"], mesh.shape["fsdp"]), mesh=mesh,
        in_specs=(tok, tok, vec, mat, mat, vec, mat, mat, tok, tok, tok),
        out_specs=(tok, tok, tok, vec, mat, mat, vec, mat, mat), check_vma=False)
```

```python
import functools
import types

import jax
import jax.numpy as jnp
from jax import lax
from jax.experimental import pallas as pl
from jax.experimental.pallas import tpu as pltpu
from jax.sharding import PartitionSpec as P

BF = jnp.bfloat16
F32 = jnp.float32
HEADS = 8
ITERS = 2
BLK = 128
CHUNK = 512
NEG = -1e30
LOG2E = 1.4426950408889634
LN2 = 0.6931471805599453
GELU_A = 0.7978845608028654
GELU_B = GELU_A * 0.044715
FLOPS_FIRST = 10 ** 6
FLOPS_PREPARE = 10 ** 6
FLOPS_LAST = 10 ** 10
LIMIT_MIDDLE = 42
LIMIT_LAST = 16


def dot(a, b):
    return jnp.dot(a, b, preferred_element_type=F32)

def dot_tn(a, b):
    return lax.dot_general(a, b, (((0,), (0,)), ((), ())), preferred_element_type=F32)

def dot_nt(a, b):
    return lax.dot_general(a, b, (((1,), (1,)), ((), ())), preferred_element_type=F32)

def rows(start, size):
    return pl.ds(start, size)

def ln_fwd(x):
    c = x - jnp.mean(x, axis=1, keepdims=True)
    r = lax.rsqrt(jnp.mean(c * c, axis=1, keepdims=True) + 1e-5)
    return c * r, r

def ln_bwd(y, n, r):
    return r * (y - jnp.mean(y, axis=1, keepdims=True) - n * jnp.mean(y * n, axis=1, keepdims=True))

def loop(n, body):
    for i in range(n):
        body(i)

def make_masks(len_ref, mask_ref, nb):
    pos = lax.broadcasted_iota(jnp.int32, (1, BLK), 1)
    ends = []
    total = jnp.int32(0)
    for p in range(len_ref.shape[1]):
        total = total + len_ref[0, p]
        ends.append(total)

    def block(i, _):
        q = pos + i * BLK
        start = jnp.zeros((1, BLK), jnp.int32)
        for e in ends:
            start = jnp.where(q >= e, e, start)
        k = lax.broadcasted_iota(jnp.int32, (2 * BLK, BLK), 0) + (i - 1) * BLK
        mask_ref[i] = jnp.where((k >= start) & (k <= q), 0.0, NEG).astype(F32)
        return 0

    lax.fori_loop(0, nb, block, 0)

def pad_zero(s):
    s.kp[0:BLK, :] = jnp.zeros((BLK, s.kp.shape[1]), BF)
    s.vp[0:BLK, :] = jnp.zeros((BLK, s.vp.shape[1]), BF)
    s.kt[0] = jnp.zeros(s.kt.shape[1:], BF)
    s.vt[0] = jnp.zeros(s.vt.shape[1:], BF)

def project(s, j, ent, wqkv):
    n, r = ln_fwd(ent)
    nb16 = n.astype(BF)
    s.n1[rows(j * CHUNK, CHUNK), :] = nb16
    s.r1[rows(j * CHUNK, CHUNK), :] = jnp.broadcast_to(r, (CHUNK, 128))
    pack_heads(s, j, nb16, wqkv)

def pack_heads(s, j, nb16, wqkv):
    d = nb16.shape[1]
    scale = LOG2E * (d // HEADS) ** -0.5
    q = (dot(nb16, wqkv[:, 0:d]) * scale).astype(BF)
    k = dot(nb16, wqkv[:, d:2 * d]).astype(BF)
    v = dot(nb16, wqkv[:, 2 * d:3 * d]).astype(BF)
    s.qs[rows(j * CHUNK, CHUNK), :] = q
    s.kp[pl.ds(j * CHUNK + BLK, CHUNK), :] = k
    s.vp[pl.ds(j * CHUNK + BLK, CHUNK), :] = v
    qt, kt, vt = q.T, k.T, v.T
    for b in range(CHUNK // BLK):
        i = j * (CHUNK // BLK) + b
        s.qst[i] = qt[:, b * BLK:(b + 1) * BLK]
        s.kt[i + 1] = kt[:, b * BLK:(b + 1) * BLK]
        s.vt[i + 1] = vt[:, b * BLK:(b + 1) * BLK]

def split_heads(tile, a, hd):
    def alone(lo):
        parts = [jnp.zeros((n, tile.shape[1]), tile.dtype) for n in (lo, tile.shape[0] - lo - hd)]
        parts = [parts[0], tile[lo:lo + hd], parts[1]]
        return jnp.concatenate([p for p in parts if p.shape[0]], axis=0)
    return jnp.concatenate([alone(a), alone(a + hd)], axis=1)

def stack_heads(tile, a, hd):
    z = jnp.zeros_like(tile)
    lane = lax.broadcasted_iota(jnp.int32, tile.shape, 1)
    top = jnp.where((lane >= a) & (lane < a + hd), tile, z)
    low = jnp.where((lane >= a + hd) & (lane < a + 2 * hd), tile, z)
    return jnp.concatenate([top, low], axis=0)

def pairs_of(d):
    hd = d // HEADS
    per = 128 // (2 * hd)
    return [(p, slice(p // per * 128, p // per * 128 + 128), p % per * 2 * hd, p * 2 * hd) for p in range(HEADS // 2)]

def window(ref, i, lo, n):
    return jnp.concatenate([ref[i, lo:lo + n, :], ref[i + 1, lo:lo + n, :]], axis=1)

def attend(s, blocks, mask_ref):
    d = s.qs.shape[1]
    hd = d // HEADS
    ones = jnp.ones((16, 2 * BLK), BF)
    def scores(i):
        win = pl.ds(i * BLK, 2 * BLK)
        return [dot(s.kp[win, tile], split_heads(s.qst[i, tile, :], a, hd)) for _, tile, a, _ in pairs_of(d)]
    def soft(i, all_scores):
        mask = mask_ref[i]
        mask = jnp.concatenate([mask, mask], axis=1)
        out = []
        for sc in all_scores:
            sc = sc + mask
            out.append(jnp.exp2(sc - jnp.max(sc, axis=0, keepdims=True)).astype(BF))
        return out
    def values(i, es):
        return [dot(jnp.concatenate([window(s.vt, i, lo, 2 * hd), ones], axis=0), es[p]) for p, _, _, lo in pairs_of(d)]
    es = []
    ready = scores(blocks[0])
    for n, i in enumerate(blocks):
        ahead = scores(blocks[n + 1]) if n + 1 < len(blocks) else None
        es.append(soft(i, ready))
        ready = ahead
    os = [values(i, e) for i, e in zip(blocks, es)]
    for i, e, o in zip(blocks, es, os):
        for p, _, _, lo in pairs_of(d):
            s.e[i, p] = e[p]
            inv = 1.0 / o[p][2 * hd:2 * hd + 1, :]
            s.linv[i, 2 * p:2 * p + 1, :] = inv[:, :BLK]
            s.linv[i, 2 * p + 1:2 * p + 2, :] = inv[:, BLK:]
            s.ht[i, lo:lo + hd, :] = (o[p][0:hd, :BLK] * inv[:, :BLK]).astype(BF)
            s.ht[i, lo + hd:lo + 2 * hd, :] = (o[p][hd:2 * hd, BLK:] * inv[:, BLK:]).astype(BF)

def heads_chunk(s, j):
    return jnp.concatenate([s.ht[j * (CHUNK // BLK) + b] for b in range(CHUNK // BLK)], axis=1)

def mlp(s, j, ent, wout, wup, wdown):
    mid = ent + dot_tn(heads_chunk(s, j), wout[...])
    n, r = ln_fwd(mid)
    nb16 = n.astype(BF)
    at = rows(j * CHUNK, CHUNK)
    s.n2[at, :] = nb16
    s.r2[at, :] = jnp.broadcast_to(r, (CHUNK, 128))
    acc = mid
    for f in range(wup.shape[1] // 256):
        c = slice(f * 256, (f + 1) * 256)
        h = dot(nb16, wup[:, c]).astype(BF)
        h2 = h * h
        sg = 0.5 * jnp.tanh(h * (GELU_B * h2 + GELU_A)) + 0.5
        act = h * sg
        s.act[at, c] = act
        s.gp[at, c] = sg + act * (2.0 - 2.0 * sg) * (3 * GELU_B * h2 + GELU_A)
    return mid + dot(s.act[at, :], wdown[...])

def mlp_back(s, j, g, wdown_t, wup_t):
    at = rows(j * CHUNK, CHUNK)
    gb = g.astype(BF)
    s.g2[at, :] = gb
    acc = None
    for f in range(wdown_t.shape[1] // 256):
        c = slice(f * 256, (f + 1) * 256)
        dh = dot(gb, wdown_t[:, c]).astype(BF) * s.gp[at, c]
        s.gp[at, c] = dh
    acc = dot(s.gp[at, :], wup_t[...])
    g = g + ln_bwd(acc, s.n2[at, :].astype(F32), s.r2[at, 0:1])
    s.gm[at, :] = g.astype(BF)
    return g

def attend_back(s, blocks, wout, dk_ref, dv_ref):
    d = s.qs.shape[1]
    hd = d // HEADS
    minus = jnp.full((2 * BLK, 128), -1.0, BF)
    def head_grads(i):
        raw = dot_nt(wout[...], s.gm[rows(i * BLK, BLK), :])
        inv = jnp.concatenate([jnp.broadcast_to(s.linv[i, h:h + 1, :], (hd, BLK)) for h in range(HEADS)], axis=0)
        dost = (raw * inv).astype(BF)
        return dost, (dost.astype(F32) * s.ht[i].astype(F32)).astype(BF), dost.T
    def prob_grads(i, dost, doh):
        win = pl.ds(i * BLK, 2 * BLK)
        return [dot(jnp.concatenate([s.vp[win, tile], minus], axis=1),
                    jnp.concatenate([split_heads(dost[tile, :], a, hd), split_heads(doh[tile, :], a, hd)], axis=0))
                for _, tile, a, _ in pairs_of(d)]
    def by_keys(lhs, tokens):
        return [dot(lhs[p], stack_heads(tokens[:, tile], a, hd)) for p, tile, a, _ in pairs_of(d)]
    def by_queries(i, dss):
        out = []
        for p, _, _, lo in pairs_of(d):
            dq = dot(window(s.kt, i, lo, 2 * hd), dss[p])
            out += [dq[0:hd, :BLK], dq[hd:2 * hd, BLK:]]
        return (jnp.concatenate(out, axis=0) * hd ** -0.5).astype(BF)
    heads = [head_grads(i) for i in blocks]
    dps = [prob_grads(i, h[0], h[1]) for i, h in zip(blocks, heads)]
    es = [[s.e[i, p] for p in range(HEADS // 2)] for i in blocks]
    dvs = [by_keys(e, h[2]) for e, h in zip(es, heads)]
    dss = [[(x.astype(F32) * y).astype(BF) for x, y in zip(e, dp)] for e, dp in zip(es, dps)]
    dks = [by_keys(ds, s.qs[rows(i * BLK, BLK), :]) for i, ds in zip(blocks, dss)]
    dqs = [by_queries(i, ds) for i, ds in zip(blocks, dss)]
    per = HEADS // 2 // (d // 128)
    for n, i in enumerate(blocks):
        top, low = pl.ds(i * BLK, BLK), pl.ds(i * BLK + BLK, BLK)
        for ref, parts in ((dk_ref, dks[n]), (dv_ref, dvs[n])):
            for t in range(d // 128):
                tile = slice(t * 128, (t + 1) * 128)
                total = sum(parts[t * per + 1:(t + 1) * per], parts[t * per])
                ref[top, tile] += total[:BLK]
                ref[low, tile] = total[BLK:]
        s.dpk[rows(i * BLK, BLK), 0:d] = dqs[n].T

def finish_packed(s, j, dk_ref, dv_ref):
    d = s.n1.shape[1]
    at = rows(j * CHUNK, CHUNK)
    pat = pl.ds(j * CHUNK + BLK, CHUNK)
    s.dpk[at, d:2 * d] = (dk_ref[pat, :] * LN2).astype(BF)
    s.dpk[at, 2 * d:3 * d] = dv_ref[pat, :].astype(BF)

def project_back(s, j, g, wqkv_t):
    at = rows(j * CHUNK, CHUNK)
    return g + ln_bwd(dot(s.dpk[at, :], wqkv_t[...]), s.n1[at, :].astype(F32), s.r1[at, 0:1])

def weigh(cnt_ref, len_ref, j, cot):
    pos = lax.broadcasted_iota(jnp.int32, (CHUNK, 128), 0) + j * CHUNK
    w = jnp.zeros((CHUNK, 128), F32)
    begin = jnp.int32(0)
    for p in range(len_ref.shape[1]):
        w = jnp.where(pos >= begin, 12.0 / cnt_ref[0, p].astype(F32), w)
        begin = begin + len_ref[0, p]
    return cot * jnp.concatenate([w] * (cot.shape[1] // 128), axis=1)

def saved_shapes(t, d, ff):
    nb = t // BLK
    return dict(n1=((t, d), BF), r1=((t, 128), F32), qs=((t, d), BF), kp=((t + BLK, d), BF), vp=((t + BLK, d), BF),
                qst=((nb, d, BLK), BF), kt=((nb + 1, d, BLK), BF), vt=((nb + 1, d, BLK), BF), e=((nb, HEADS // 2, 2 * BLK, 2 * BLK), BF),
                ht=((nb, d, BLK), BF), linv=((nb, HEADS, BLK), F32))
def more_shapes(t, d, ff):
    return dict(n2=((t, d), BF), r2=((t, 128), F32), act=((t, ff), BF), gp=((t, ff), BF),
                g2=((t, d), BF), gm=((t, d), BF), dpk=((t, 3 * d), BF))

class Memory:
    def __init__(self, ins, outs, sems, hbm, loads):
        self.ins, self.outs, self.sems, self.hbm, self.loads, self.started = ins, outs, sems, hbm, loads, []

    def wait(self, *which):
        for n in which:
            self.loads[n].wait()

    def put(self, n):
        copy = pltpu.make_async_copy(self.outs[n], self.hbm[n], self.sems.at[len(self.started)])
        copy.start()
        self.started.append(copy)

def call(kernel, outs, args, scratch, name, flops, limit=16):
    spec = dict(vmem=pl.BlockSpec(memory_space=pltpu.VMEM), smem=pl.BlockSpec(memory_space=pltpu.SMEM), any=pl.BlockSpec(memory_space=pl.ANY))
    spec["store"] = spec["load"] = spec["any"]
    n_in, n_out, n_scratch = len(args), len(outs), len(scratch)
    stores = [n for n, o in enumerate(outs) if o[0] == "store"]
    loads = [n for n, a in enumerate(args) if a[0] == "load"]
    buffers = [pltpu.VMEM(outs[n][1], outs[n][2]) for n in stores] + [(pltpu.SMEM if args[n][1].dtype == jnp.int32 else pltpu.VMEM)(args[n][1].shape, args[n][1].dtype) for n in loads]
    buffers += [pltpu.SemaphoreType.DMA((max(len(stores), 1),)), pltpu.SemaphoreType.DMA((max(len(loads), 1),))]
    def run(*refs):
        ins, results, rest = list(refs[:n_in]), list(refs[n_in:n_in + n_out]), refs[n_in + n_out:]
        hbm, coming = list(results), {}
        for n, r in zip(stores, rest[n_scratch:]):
            results[n] = r
        for c, (n, r) in enumerate(zip(loads, rest[n_scratch + len(stores):])):
            coming[n] = pltpu.make_async_copy(ins[n], r, rest[-1].at[c])
            coming[n].start()
            ins[n] = r
        memory = Memory(ins, results, rest[-2], hbm, coming)
        kernel(memory, types.SimpleNamespace(**dict(zip(scratch, rest))))
        for copy in memory.started:
            copy.wait()
    shapes = dict(vmem=pltpu.VMEM, store=jax.ShapeDtypeStruct)
    place = dict(vmem=pltpu.VMEM, load=pltpu.HBM)
    return pl.pallas_call(
        run, out_shape=tuple(shapes[o[0]](o[1], o[2]) for o in outs),
        in_specs=[spec[k] for k, _ in args], out_specs=tuple(spec[o[0]] for o in outs),
        scratch_shapes=[pltpu.VMEM(*v) for v in scratch.values()] + buffers,
        compiler_params=pltpu.CompilerParams(vmem_limit_bytes=limit << 20), name=name,
        cost_estimate=pl.CostEstimate(flops=flops, bytes_accessed=1 << 20, transcendentals=0))(
        *[pltpu.with_memory_space_constraint(v, place[k]) if k in place else v for k, v in args])

def place_qkv(me, parts, wqkv):
    r = wqkv.shape[0] // len(parts)
    for x, p in enumerate(parts):
        wqkv[pl.ds(pl.multiple_of((me ^ x) * r, r), r), :] = p[...]

def place_rest(me, parts, wout, wup, wdown):
    r, rd = wout.shape[0] // len(parts), wdown.shape[0] // len(parts)
    for x, p in enumerate(parts):
        at = pl.ds(pl.multiple_of((me ^ x) * r, r), r)
        wout[at, :] = p[0:r, :]
        for c in range(wup.shape[1] // 256):
            wup[at, c * 256:(c + 1) * 256] = p[(c + 1) * r:(c + 2) * r, :]
        lo = r * (1 + wup.shape[1] // 256)
        wdown[pl.ds(pl.multiple_of((me ^ x) * rd, rd), rd), :] = p[lo:lo + rd, :]

def hand_out(me, parts, mats, keep, send):
    for x in range(parts):
        dst = send if x % 2 else keep
        lo = 0
        for m in mats:
            r = m.shape[0] // parts
            at = pl.ds(pl.multiple_of((me ^ x) * r, r), r)
            for c in range(m.shape[1] // 256):
                dst[x // 2, lo:lo + r, :] = m[at, c * 256:(c + 1) * 256]
                lo += r

SAVED = ("e", "n1", "r1", "qs", "vp", "kt", "ht", "linv")

def prepare(lengths, states, inject):
    t, d = states.shape
    nb, nc = t // BLK, t // CHUNK
    def kernel(m, s):
        len_ref, st, inj = m.ins
        n1, r1, mask = m.outs
        m.wait(0)
        make_masks(len_ref, mask, nb)
        m.wait(1, 2)
        for j in range(nc):
            at = slice(j * CHUNK, (j + 1) * CHUNK)
            n, r = ln_fwd(st[at, :] + inj[at, :])
            n1[at, :] = n.astype(BF)
            r1[at, :] = jnp.broadcast_to(r, (CHUNK, 128))
    outs = [("vmem", (t, d), BF), ("vmem", (t, 128), F32), ("vmem", (nb, 2 * BLK, BLK), F32)]
    args = [("load", v) for v in (lengths, states, inject)]
    return call(kernel, outs, args, {}, "prepare", FLOPS_PREPARE)

def first_attention(me, lengths, counts, states, inject, cot, n1, mask, qkv_parts, ff):
    t, d = n1.shape
    nb, nc = t // BLK, t // CHUNK
    shapes = saved_shapes(t, d, ff)
    made = [k for k in SAVED if k not in ("n1", "r1")]
    scratch = {k: v for k, v in shapes.items() if k not in SAVED}
    def kernel(m, s):
        me_ref, len_ref, cnt_ref, st, inj, ct, n1_ref, mask_ref = m.ins[:8]
        vars(s).update(zip(made, m.outs))
        wqkv, ent, inj_out, weighed = m.outs[-4:]
        pad_zero(s)
        place_qkv(me_ref[0], m.ins[8:], wqkv)
        for j in range(nc):
            pack_heads(s, j, n1_ref[j * CHUNK:(j + 1) * CHUNK, :], wqkv)
        for i in range(0, nb, 4):
            attend(s, (i, i + 1, i + 2, i + 3), mask_ref)
        m.wait(1, 2, 3, 4, 5)
        for j in range(nc):
            at = slice(j * CHUNK, (j + 1) * CHUNK)
            ent[at, :] = st[at, :] + inj[at, :]
            inj_out[at, :] = inj[at, :]
            weighed[at, :] = weigh(cnt_ref, len_ref, j, ct[at, :])
    outs = [("vmem",) + shapes[k] for k in made] + [("vmem", (d, 3 * d), BF)] + [("vmem", (t, d), F32)] * 3
    args = [("smem", me)] + [("load", v) for v in (lengths, counts, states, inject, cot)] + [("vmem", v) for v in (n1, mask, *qkv_parts)]
    got = call(kernel, outs, args, scratch, "first_attention", FLOPS_FIRST)
    return dict(zip(made, got)), got[-4], got[-3:]

def middle_part(me, ent, inject, weighed, mask, wqkv, ht, rest_parts, ff):
    t, d = ent.shape
    nb, nc = t // BLK, t // CHUNK
    parts = len(rest_parts)
    sh = {"a_" + k: v for k, v in more_shapes(t, d, ff).items() if k not in ("dpk", "gm")}
    sh.update({"b_" + k: v for k, v in {**saved_shapes(t, d, ff), **more_shapes(t, d, ff)}.items() if k not in ("n1", "dpk", "ht", "gm")})
    sh.update(state=((t, d), F32), dk=((t + BLK, d), F32), dv=((t + BLK, d), F32),
              wqkv_t=((3 * d, d), BF), wup_t=((ff, d), BF), wdown_t=((d, ff), BF), tr=((2, d, t), BF),
              wup=((d, ff), BF), wdown=((ff, d), BF), mup=((d, ff), BF), mdown_t=((d, ff), BF), mdown=((ff, d), BF))
    def kernel(m, x):
        me_ref, ent_ref, inj, weighed_ref, x.mask, wqkv_ref, ht_ref = m.ins[:7]
        final, g, ginj, gm, wout, n1, dpk, ht, gm_two, keep, send = m.outs
        its = [types.SimpleNamespace(**{k[2:]: v for k, v in vars(x).items() if k.startswith(p)}) for p in ("a_", "b_")]
        its[0].ht, its[0].gm = ht_ref, gm
        its[1].n1, its[1].dpk, its[1].ht, its[1].gm = n1, dpk, ht, gm_two
        place_rest(me_ref[0], m.ins[7:], wout, x.wup, x.wdown)
        pad_zero(its[1])
        def rows_of(j):
            return slice(j * CHUNK, (j + 1) * CHUNK)
        def mlp_of(n, j, src, dst):
            at = rows_of(j)
            entered = src[at, :] + inj[at, :] if n else src[at, :]
            dst[at, :] = mlp(its[n], j, entered, wout, x.wup, x.wdown)
        def project_of(j):
            project(its[1], j, x.state[rows_of(j), :] + inj[rows_of(j), :], wqkv_ref)
        def blocks_of(j):
            n = CHUNK // BLK
            return [tuple(range(j * n, j * n + n))]
        def attend_of(j):
            for blocks in blocks_of(j):
                attend(its[1], blocks, x.mask)
        def back_two(j):
            at = rows_of(j)
            g[at, :] = mlp_back(its[1], j, weighed_ref[at, :], x.wdown_t, x.wup_t)
        def attend_back_of(j):
            for blocks in blocks_of(j):
                attend_back(its[1], blocks, wout, x.dk, x.dv)
        def back_one(j):
            at = rows_of(j)
            finish_packed(its[1], j, x.dk, x.dv)
            new = project_back(its[1], j, g[at, :], x.wqkv_t)
            ginj[at, :] = new
            g[at, :] = mlp_back(its[0], j, new, x.wdown_t, x.wup_t)
        x.dk[0:BLK, :] = jnp.zeros((BLK, d), F32)
        x.dv[0:BLK, :] = jnp.zeros((BLK, d), F32)
        for j in range(nc): mlp_of(0, j, ent_ref, x.state)
        for j in range(nc): project_of(j)
        for j in range(nc): attend_of(j)
        for j in range(nc):
            mlp_of(1, j, x.state, final)
            if j == 0:
                x.wup_t[...] = x.wup[...].T
                x.wdown_t[...] = x.wdown[...].T
                x.wqkv_t[...] = wqkv_ref[...].T
        m.put(0)
        for j in range(nc): back_two(j)
        for j in range(nc): attend_back_of(j)
        for j in range(nc): back_one(j)

        def weight_grad(lefts, rights, dst):
            for n, left in enumerate(lefts):
                x.tr[n] = left[...].T
            def tile(c):
                cc = pl.ds(c * 256, 256)
                total = dot(x.tr[0], rights[0][:, cc])
                for n in range(1, len(rights)):
                    total = total + dot(x.tr[n], rights[n][:, cc])
                dst[:, cc] = total.astype(dst.dtype)
            loop(dst.shape[1] // 256, tile)
        weight_grad([s.g2 for s in its], [s.act for s in its], x.mdown_t)
        x.mdown[...] = x.mdown_t[...].T
        weight_grad([s.n2 for s in its], [s.gp for s in its], x.mup)
        hand_out(me_ref[0], parts, (x.mup, x.mdown), keep, send)
    piece = ("vmem", (max(parts // 2, 1), 2 * ff // parts, d), BF)
    outs = [("store", (t, d), F32)] + [("vmem", (t, d), F32)] * 2 + [("vmem", (t, d), BF), ("vmem", (d, d), BF), ("vmem", (t, d), BF), ("vmem", (t, 3 * d), BF)] + [("vmem", (nb, d, BLK), BF), ("vmem", (t, d), BF)] + [piece] * 2
    args = [("smem", me)] + [("vmem", v) for v in (ent, inject, weighed, mask, wqkv, ht, *rest_parts)]
    return call(kernel, outs, args, sh, "middle_part", 25 * 10 ** 9, limit=LIMIT_MIDDLE)

def last_part(me, saved, gm, wout, wqkv, n1, dpk, ht, gm_two, g, ginj, parts, ff, first):
    t, d = gm.shape
    nb, nc = t // BLK, t // CHUNK
    scratch = dict(dk=((t + BLK, d), F32), dv=((t + BLK, d), F32), tr=((2, d, t), BF), mat=((d, 3 * d), BF), mout=((d, d), BF), wt=((3 * d, d), BF), dpk=((t, 3 * d), BF))
    def kernel(m, s):
        me_ref, s.gm, wout_ref, w_ref, n1_ref, dpk_ref, ht_ref, gm_ref, g_ref, gi_ref = m.ins[:10]
        vars(s).update(zip(SAVED, m.ins[10:]))
        keep, send, grad, grad_inject = m.outs
        s.dk[0:BLK, :] = jnp.zeros((BLK, d), F32)
        s.dv[0:BLK, :] = jnp.zeros((BLK, d), F32)
        for i in range(0, nb, 4):
            attend_back(s, (i, i + 1, i + 2, i + 3), wout_ref, s.dk, s.dv)
        s.tr[0] = s.n1[...].T
        s.tr[1] = n1_ref[...].T
        s.wt[...] = w_ref[...].T
        loop(nc, lambda j: finish_packed(s, j, s.dk, s.dv))
        def tile(c):
            cc = slice(c * 256, (c + 1) * 256)
            s.mat[:, cc] = (dot(s.tr[0], s.dpk[:, cc]) + dot(s.tr[1], dpk_ref[:, cc])).astype(BF)
        loop(3, tile)
        total = None
        for left, right in ((s.ht, s.gm), (ht_ref, gm_ref)):
            for b in range(nb):
                part = dot(left[b], right[b * BLK:(b + 1) * BLK, :])
                total = part if total is None else total + part
        s.mout[...] = total.astype(BF)
        hand_out(me_ref[0], parts, (s.mout, s.mat), keep, send)
        def chunk(j):
            at = rows(j * CHUNK, CHUNK)
            new = project_back(s, j, g_ref[at, :], s.wt)
            grad[at, :] = new
            grad_inject[at, :] = new + gi_ref[at, :]
        loop(nc, chunk)
        m.put(2)
        m.put(3)
    outs = [("vmem", (max(parts // 2, 1), 4 * d // parts, d), BF)] * 2 + [("store", (t, d), F32)] * 2
    args = [("smem", me)] + [("vmem", v) for v in (gm, wout, wqkv, n1, dpk, ht, gm_two, g, ginj)]
    args += [("vmem", saved[k]) for k in SAVED] + [("any", v) for v in first]
    return call(kernel, outs, args, scratch, "last_part", FLOPS_LAST, limit=LIMIT_LAST)

def to_column(row):
    n = row.shape[1]
    eye = lax.broadcasted_iota(jnp.int32, (n, n), 0) == lax.broadcasted_iota(jnp.int32, (n, n), 1)
    return jnp.sum(jnp.where(eye, jnp.broadcast_to(row, (n, n)), 0.0), axis=1, keepdims=True)

def to_row(column):
    n = column.shape[0]
    eye = lax.broadcasted_iota(jnp.int32, (n, n), 0) == lax.broadcasted_iota(jnp.int32, (n, n), 1)
    return jnp.sum(jnp.where(eye, jnp.broadcast_to(column, (n, n)), 0.0), axis=0, keepdims=True)

def pack_weights(w_qkv, gain_one, w_out, w_up, w_down, gain_two):
    r, d = w_out.shape
    n = w_up.shape[1] // d
    def kernel(m, s):
        qkv, g_one, out, up, down, g_two = m.ins
        m.wait(0, 1)
        m.outs[0][...] = (qkv[...].astype(F32) * to_column(g_one[...].astype(F32))).astype(BF)
        m.wait(2, 3, 4, 5)
        m.outs[1][0:r, :] = out[...]
        col = to_column(g_two[...].astype(F32))
        for c in range(n):
            m.outs[1][(c + 1) * r:(c + 2) * r, :] = (up[:, c * d:(c + 1) * d].astype(F32) * col).astype(BF)
        m.outs[1][(n + 1) * r:, :] = down[...]
    args = [("load", v) for v in (w_qkv, gain_one.reshape(1, -1), w_out, w_up, w_down, gain_two.reshape(1, -1))]
    return call(kernel, [("vmem", w_qkv.shape, BF), ("vmem", ((n + 1) * r + w_down.shape[0], d), BF)], args, {}, "pack_weights", 10 ** 6)

def sum_parts(parts, lo, size):
    acc = parts[0][lo:lo + size, :].astype(F32)
    for p in parts[1:]:
        acc = acc + p[lo:lo + size, :].astype(F32)
    return acc

def finished(shares, weight, gain, lead, tail, name):
    r, cols = weight.shape
    d = shares[0].shape[1]
    n = cols // d
    others = [(lo, size) for lo, size in ((0, lead), (lead + n * r, tail)) if size]
    def kernel(m, s):
        w, g, parts = m.ins[0], to_column(m.ins[1][...].astype(F32)), m.ins[2:]
        along = jnp.zeros((r, 1), F32)
        for c in range(n):
            v = sum_parts(parts, lead + c * r, r)
            m.outs[0][:, c * d:(c + 1) * d] = v * g
            along = along + jnp.sum(v * w[:, c * d:(c + 1) * d].astype(F32), axis=1, keepdims=True)
        m.put(0)
        m.outs[1][...] = to_row(along)
        m.put(1)
        for at, (lo, size) in enumerate(others):
            m.outs[2 + at][...] = sum_parts(parts, lo, size)
            m.put(2 + at)
    outs = [("store", (r, cols), F32), ("store", (1, r), F32)] + [("store", (size, d), F32) for _, size in others]
    got = call(kernel, outs, [("vmem", v) for v in (weight, gain.reshape(1, -1), *shares)], {}, name, 10 ** 6)
    return [got[0], got[1].reshape(r)] + list(got[2:])

def after(values, *others):
    return lax.optimization_barrier((values, others))[0]

def exchange(x, axis, size, step):
    return lax.ppermute(x, axis, [(i, i ^ step) for i in range(size)])

def far_parts(x, size):
    return [x] + [exchange(x, "fsdp", size, 2 * k) for k in range(1, size // 2)]

def with_near(far, size):
    return [v for x in far for v in (x, exchange(x, "fsdp", size, 1))]

def sum_near(keep, near, then=None):
    total = keep.astype(F32) + near.astype(F32)
    if then is not None:
        total = total + jnp.minimum(jnp.abs(then[:keep.shape[1]].astype(F32)), 0.0)
    return [total[k].astype(BF) for k in range(keep.shape[0])]

def send_far(summed, size):
    return [exchange(summed[k], "fsdp", size, 2 * k) for k in range(size // 2 - 1, 0, -1)]

def along_dp(share, size):
    return [share] + [exchange(share, "dp", size, k) for k in range(1, size)]

def send_near(pieces, size):
    return [exchange(p, "fsdp", size, 1) for p in pieces[1::2]]

def send_far(summed, size):
    return [exchange(summed[k], "fsdp", size, 2 * k) for k in range(size // 2 - 1, 0, -1)]

def reduce_whole(whole, sizes):
    out, lo = [], 0
    for n in sizes:
        share = lax.psum_scatter(whole[lo:lo + n], "fsdp", scatter_dimension=0, tiled=True)
        out.append(lax.psum(share, "dp").astype(F32))
        lo += n
    return jnp.concatenate(out, axis=0)

def on_device(n_dp, n_fsdp, states, inject, ln1_gain, w_qkv, w_out, ln2_gain, w_up, w_down, prompt_lengths, loop_counts, cotangent):
    d = states.shape[1]
    r, ff = w_up.shape
    direct = r % 16 == 0
    if direct:
        me = lax.axis_index("fsdp").astype(jnp.int32).reshape(1)
        own_qkv, own_rest = pack_weights(w_qkv, ln1_gain, w_out, w_up, w_down, ln2_gain)
        qkv_far = far_parts(own_qkv, n_fsdp)
        rest_far = far_parts(own_rest, n_fsdp)
    else:
        me = jnp.zeros((1,), jnp.int32)
        full = lambda v: lax.all_gather(v, "fsdp", axis=0, tiled=True)
        up = full((w_up.astype(F32) * ln2_gain.astype(F32)[:, None]).astype(BF))
        qkv_parts = [full((w_qkv.astype(F32) * ln1_gain.astype(F32)[:, None]).astype(BF))]
        rest_parts = [jnp.concatenate([full(w_out)] + [up[:, c:c + d] for c in range(0, ff, d)] + [full(w_down)], axis=0)]
    n1, r1, mask = prepare(prompt_lengths, states, inject)
    if direct:
        qkv_parts = with_near(qkv_far[:1], n_fsdp) + with_near(after(qkv_far[1:], n1), n_fsdp)
    parts = len(qkv_parts)
    saved, wqkv, entering = first_attention(me, prompt_lengths, loop_counts, states, inject, cotangent, n1, mask, qkv_parts, ff)
    saved.update(n1=n1, r1=r1)
    if direct:
        late = with_near(after(rest_far[:0:-1], wqkv), n_fsdp)
        rest_parts = with_near(rest_far[:1], n_fsdp) + [v for x in range(len(late) - 2, -1, -2) for v in late[x:x + 2]]
    final, g, ginj, gm, wout, n1, dpk, ht, gm_two, keep, send = middle_part(
        me, *entering, mask, wqkv, saved["ht"], rest_parts, ff)
    summed = []
    if direct:
        summed = sum_near(keep, exchange(send, "fsdp", n_fsdp, 1))
        far = send_far(summed, n_fsdp)[::-1]
    else:
        shares = [reduce_whole(keep[0], [d] * (ff // d) + [ff])]
    keep_qkv, send_qkv, grad_states, grad_inject = last_part(
        me, saved, gm, wout, wqkv, n1, dpk, ht, gm_two, g, ginj, parts, ff, summed)
    if direct:
        near = exchange(send_qkv, "fsdp", n_fsdp, 1)
        share = sum_parts([summed[0], *far], 0, summed[0].shape[0]).astype(BF)
        shares = along_dp(share, n_dp)
        summed = sum_near(keep_qkv, near, share)
        shares_qkv = along_dp(sum_parts([summed[0], *send_far(summed, n_fsdp)], 0, 4 * r).astype(BF), n_dp)
    else:
        shares_qkv = [reduce_whole(keep_qkv[0], [d] * 4)]
    d_up, d_gain_two, d_down = finished(shares, w_up, ln2_gain, 0, w_down.shape[0], "finished_mlp")
    d_qkv, d_gain_one, d_out = finished(shares_qkv, w_qkv, ln1_gain, r, 0, "finished_attention")
    return (final, grad_states, grad_inject, d_gain_one, d_qkv, d_out, d_gain_two, d_up, d_down)

def solution(mesh):
    tok, vec, mat = P(("dp", "fsdp"), None), P("fsdp"), P("fsdp", None)
    return jax.shard_map(
        functools.partial(on_device, mesh.shape["dp"], mesh.shape["fsdp"]), mesh=mesh,
        in_specs=(tok, tok, vec, mat, mat, vec, mat, mat, tok, tok, tok),
        out_specs=(tok, tok, tok, vec, mat, mat, vec, mat, mat), check_vma=False)
```
